32 devices in a mesh: dp: 4 (over y, x), seq: 4 (over z), shard: 2 (over core).
Axes of the slice: x: 2, y: 2, z: 4, core: 2. Of those that a mesh axis runs over, the one named last changes fastest.
Arguments:
- tokens: bfloat16 [8, 4096, 1024], P(('dp', 'shard'), 'seq'), may hold values from -6 to 6
- segments: int32 [8, 4096], P(('dp', 'shard')), may hold values from 0 to 2, as said below
- cotangent: bfloat16 [8, 4096, 1024], P(('dp', 'shard'), 'seq'), may hold values from -6 to 6
- norm_one: float32 [1024], P('shard'), may hold values from 0.5 to 1.5
- in_weight: float32 [1024, 3072], P('shard'), may hold values from -0.1875 to 0.1875
- conv_weight: float32 [3, 1024], P(None, 'shard'), may hold values from -3 to 3
- out_weight: float32 [1024, 1024], P('shard'), may hold values from -0.1875 to 0.1875
- norm_two: float32 [1024], P('shard'), may hold values from 0.5 to 1.5
- gate_weight: float32 [1024, 4608], P('shard'), may hold values from -0.1875 to 0.1875
- up_weight: float32 [1024, 4608], P('shard'), may hold values from -0.1875 to 0.1875
- down_weight: float32 [4608, 1024], P('shard'), may hold values from -0.1875 to 0.1875
- moment_norm_one: float32 [1024], P('shard'), may hold values from -1.5 to 1.5
- moment_in: float32 [1024, 3072], P('shard'), may hold values from -1.5 to 1.5
- moment_conv: float32 [3, 1024], P(None, 'shard'), may hold values from -1.5 to 1.5
- moment_out: float32 [1024, 1024], P('shard'), may hold values from -1.5 to 1.5
- moment_norm_two: float32 [1024], P('shard'), may hold values from -1.5 to 1.5
- moment_gate: float32 [1024, 4608], P('shard'), may hold values from -1.5 to 1.5
- moment_up: float32 [1024, 4608], P('shard'), may hold values from -1.5 to 1.5
- moment_down: float32 [4608, 1024], P('shard'), may hold values from -1.5 to 1.5
- learn_rate: float32 [], replicated, may hold values from 0.01 to 0.1
- step_number: int32 [], replicated, may hold values from 0 to 3999
Outputs:
- block_out: bfloat16 [8, 4096, 1024], P(('dp', 'shard'), 'seq')
- input_grad: bfloat16 [8, 4096, 1024], P(('dp', 'shard'), 'seq')
- grad_norm: float32 [], replicated
- next_moment_norm_one: float32 [1024], P('shard')
- next_moment_in: float32 [1024, 3072], P('shard')
- next_moment_conv: float32 [3, 1024], P(None, 'shard')
- next_moment_out: float32 [1024, 1024], P('shard')
- next_moment_norm_two: float32 [1024], P('shard')
- next_moment_gate: float32 [1024, 4608], P('shard')
- next_moment_up: float32 [1024, 4608], P('shard')
- next_moment_down: float32 [4608, 1024], P('shard')
- next_in_weight: bfloat16 [1024, 3072], replicated
- next_out_weight: bfloat16 [1024, 1024], replicated
- next_gate_weight: bfloat16 [1024, 4608], replicated
- next_up_weight: bfloat16 [1024, 4608], replicated
- next_down_weight: bfloat16 [4608, 1024], replicated
The draws below stay inside these ranges and needn't reach their ends.
Inputs may be any that keep to these rules, and one draw needn't show every extreme that they name: `segments`: each sequence is packed from three documents: the numbers start at 0, never fall, and rise by one at exactly two positions. The first two documents each have between 1228 and 1638 tokens; the third fills the rest of the sequence.
All inputs are finite; a program needn't handle non-finite values.
Results may differ from the reference program's by a relative error of at most 0.012.
The reference program's roundings to bfloat16 on the way count: a program that leaves them out, or rounds other values in their place, can miss the bound.
Values may be sent and summed in bfloat16 or wider, within the bound.
A program may use at most 448 MiB of HBM per device.

```python
import math
import jax
import jax.numpy as jnp
from jax import lax

D = 1024
FF = 4608
WARMUP = 2000
LEN = 4096
SEQS = 8


def draw_segments(key, part):
    first_key, second_key = jax.random.split(jax.random.fold_in(key, 17))
    shortest = 3 * LEN // 10
    longest = 4 * LEN // 10
    first_len = jax.random.randint(first_key, (SEQS, 1), shortest, longest + 1)
    second_len = jax.random.randint(second_key, (SEQS, 1), shortest, longest + 1)
    position = lax.broadcasted_iota(jnp.int32, (SEQS, LEN), 1)
    return (position >= first_len).astype(jnp.int32) + (position >= first_len + second_len).astype(jnp.int32)


def levels(stream_key, extent, pieces, least, high):
    def one(axis_at, shards_of):
        steps = jax.random.uniform(jax.random.fold_in(jax.random.fold_in(stream_key, 6), axis_at), (shards_of,), jnp.float32, least / len(pieces), high / len(pieces))
        return jnp.repeat(jnp.exp(steps), extent[axis_at] // shards_of).reshape((-1,) + (1,) * (len(extent) - axis_at - 1))

    loudness = one(*pieces[0])
    for cut in pieces[1:]:
        loudness = loudness * one(*cut)
    return loudness


def noise(own_key, shape, deviation, bound, cuts=(), kind=jnp.bfloat16):
    result = deviation * jax.random.normal(own_key, shape, jnp.float32)
    if cuts:
        result = result * levels(own_key, shape, cuts, -0.22, 0.18)
    return jnp.clip(result, -bound, bound).astype(kind)


def setup_inputs(seed: int = 0) -> dict:
    arg_keys = jax.random.split(jax.random.key(seed), 22)
    tokens = noise(arg_keys[0], (SEQS, LEN, D), 1.0, 6.0, ((0, 8), (1, 4)))
    segments = draw_segments(jax.random.fold_in(arg_keys[21], 71), 0)
    cotangent = noise(arg_keys[2], (SEQS, LEN, D), 1.0, 6.0, ((0, 8), (1, 4)))
    norm_one = jnp.clip(1.0 + 0.1 * jax.random.normal(arg_keys[3], (D,), jnp.float32), 0.5, 1.5)
    in_weight = noise(arg_keys[4], (D, 3 * D), D ** -0.5, 0.1875, ((0, 2),), jnp.float32)
    conv_weight = noise(arg_keys[5], (3, D), 0.6, 3.0, ((1, 2),), jnp.float32)
    out_weight = noise(arg_keys[6], (D, D), D ** -0.5, 0.1875, ((0, 2),), jnp.float32)
    norm_two = jnp.clip(1.0 + 0.1 * jax.random.normal(arg_keys[7], (D,), jnp.float32), 0.5, 1.5)
    gate_weight = noise(arg_keys[8], (D, FF), D ** -0.5, 0.1875, ((0, 2),), jnp.float32)
    up_weight = noise(arg_keys[9], (D, FF), D ** -0.5, 0.1875, ((0, 2),), jnp.float32)
    down_weight = noise(arg_keys[10], (FF, D), (FF // 4) ** -0.5, 0.1875, ((0, 2),), jnp.float32)
    moment_norm_one = noise(arg_keys[11], (D,), 0.25, 1.5, ((0, 2),), jnp.float32)
    moment_in = noise(arg_keys[12], (D, 3 * D), 0.25, 1.5, ((0, 2),), jnp.float32)
    moment_conv = noise(arg_keys[13], (3, D), 0.25, 1.5, ((1, 2),), jnp.float32)
    moment_out = noise(arg_keys[14], (D, D), 0.25, 1.5, ((0, 2),), jnp.float32)
    moment_norm_two = noise(arg_keys[15], (D,), 0.25, 1.5, ((0, 2),), jnp.float32)
    moment_gate = noise(arg_keys[16], (D, FF), 0.25, 1.5, ((0, 2),), jnp.float32)
    moment_up = noise(arg_keys[17], (D, FF), 0.25, 1.5, ((0, 2),), jnp.float32)
    moment_down = noise(arg_keys[18], (FF, D), 0.25, 1.5, ((0, 2),), jnp.float32)
    learn_rate = jnp.clip(jnp.exp(jax.random.uniform(arg_keys[19], (), jnp.float32, math.log(0.01), math.log(0.1))), 0.01, 0.1)
    step_number = jax.random.randint(arg_keys[20], (), 0, 2 * WARMUP).astype(jnp.int32)
    return {"tokens": tokens, "segments": segments, "cotangent": cotangent, "norm_one": norm_one, "in_weight": in_weight, "conv_weight": conv_weight, "out_weight": out_weight, "norm_two": norm_two, "gate_weight": gate_weight, "up_weight": up_weight, "down_weight": down_weight, "moment_norm_one": moment_norm_one, "moment_in": moment_in, "moment_conv": moment_conv, "moment_out": moment_out, "moment_norm_two": moment_norm_two, "moment_gate": moment_gate, "moment_up": moment_up, "moment_down": moment_down, "learn_rate": learn_rate, "step_number": step_number}


EPSILON = 1e-05
MOMENTUM_BETA = 0.9
WEIGHT_DECAY = 0.1
CLIP_RATIO = 0.25

@jax.custom_vjp
def low(v):
    return lax.optimization_barrier(v.astype(jnp.bfloat16)).astype(jnp.float32)

@jax.custom_vjp
def low_back(v):
    return v

def low_keep(v):
    return (low(v), None)

def low_pass(kept, grad):
    return (grad,)

def back_keep(v):
    return (v, None)

def back_low(kept, grad):
    return (low(grad),)
low.defvjp(low_keep, low_pass)
low_back.defvjp(back_keep, back_low)

def product(left, right):
    return jnp.dot(left, right, precision=lax.Precision.HIGHEST)

def rms_scale(values, gain):
    return values * lax.rsqrt(lax.optimization_barrier(jnp.mean(values * values, axis=-1, keepdims=True)) + EPSILON) * gain

def delayed(values, offset):
    return jnp.concatenate([jnp.zeros((offset, values.shape[1]), values.dtype), values[:-offset]], 0)

def conv_block(params, hidden_in, seg_row):
    norm_one, in_weight, conv_weight, out_weight, norm_two, gate_weight, up_weight, down_weight = params
    model_width = hidden_in.shape[1]
    normed = low(rms_scale(hidden_in, norm_one))
    projected = low_back(product(normed, in_weight))
    gate_b = projected[:, :model_width]
    gate_c = projected[:, model_width:2 * model_width]
    values = projected[:, 2 * model_width:]
    mixed_in = gate_b * values
    seg_one = jnp.concatenate([jnp.full((1,), -1, jnp.int32), seg_row[:-1]])
    seg_two = jnp.concatenate([jnp.full((2,), -1, jnp.int32), seg_row[:-2]])
    keep_one = (seg_one == seg_row).astype(jnp.float32)[:, None]
    keep_two = (seg_two == seg_row).astype(jnp.float32)[:, None]
    convolved = conv_weight[2] * mixed_in + conv_weight[1] * keep_one * delayed(mixed_in, 1) + conv_weight[0] * keep_two * delayed(mixed_in, 2)
    mixer_out = low(gate_c * convolved)
    hidden = hidden_in + low_back(product(mixer_out, out_weight))
    normed_two = low(rms_scale(hidden, norm_two))
    gate_pre = low_back(product(normed_two, gate_weight))
    upward = low_back(product(normed_two, up_weight))
    activated = low(gate_pre * jax.nn.sigmoid(gate_pre) * upward)
    return hidden + low_back(product(activated, down_weight))

def reference(tokens, segments, cotangent, norm_one, in_weight, conv_weight, out_weight, norm_two, gate_weight, up_weight, down_weight, moment_norm_one, moment_in, moment_conv, moment_out, moment_norm_two, moment_gate, moment_up, moment_down, learn_rate, step_number):
    masters = (norm_one, in_weight, conv_weight, out_weight, norm_two, gate_weight, up_weight, down_weight)
    moments = (moment_norm_one, moment_in, moment_conv, moment_out, moment_norm_two, moment_gate, moment_up, moment_down)

    def forward(inputs, params):
        lowered = tuple((low(member) for member in params))

        def one_sequence(sequence_pair):
            return conv_block(lowered, sequence_pair[0], sequence_pair[1])
        return lax.map(jax.checkpoint(one_sequence), (inputs, segments))
    outputs, pullback = jax.vjp(forward, tokens.astype(jnp.float32), masters)
    input_grad, gradients = pullback(cotangent.astype(jnp.float32))
    squares_sum = sum((jnp.sum(member * member) for member in gradients))
    grad_norm = jnp.sqrt(squares_sum)
    param_count = sum((member.size for member in masters))
    clip_level = CLIP_RATIO * math.sqrt(param_count)
    clip_factor = clip_level / jnp.maximum(grad_norm, clip_level)
    rate_now = learn_rate * jnp.minimum(1.0, (step_number + 1).astype(jnp.float32) / WARMUP)
    next_moments = tuple((MOMENTUM_BETA * moment + clip_factor * gradient for moment, gradient in zip(moments, gradients)))
    next_weights = tuple(((masters[place] * (1.0 - rate_now * WEIGHT_DECAY) - rate_now * next_moments[place]).astype(jnp.bfloat16) for place in (1, 3, 5, 6, 7)))
    return (outputs.astype(jnp.bfloat16), input_grad.astype(jnp.bfloat16), grad_norm, next_moments[0], next_moments[1], next_moments[2], next_moments[3], next_moments[4], next_moments[5], next_moments[6], next_moments[7], next_weights[0], next_weights[1], next_weights[2], next_weights[3], next_weights[4])
```

```python
import functools
import math

import jax
import jax.numpy as jnp
from jax import lax
from jax.experimental import pallas as pl
from jax.experimental.pallas import tpu as pltpu
from jax.sharding import PartitionSpec as P

WARMUP = 2000


EPSILON = 1e-05
MOMENTUM_BETA = 0.9
WEIGHT_DECAY = 0.1
CLIP_RATIO = 0.25


def from_behind(block, axis, distance):
    devices = range(lax.axis_size(axis))
    route = [(i - distance, i) for i in devices if i - distance in devices]
    return lax.ppermute(block, axis, route)


def rows_dot(left, right):
    return jnp.dot(left, right, preferred_element_type=jnp.float32)


def outer_dot(left, right):
    return lax.dot_general(
        left, right, (((0,), (0,)), ((), ())), preferred_element_type=jnp.float32
    )


def back_dot(left, right):
    return lax.dot_general(
        left, right, (((1,), (1,)), ((), ())), preferred_element_type=jnp.float32
    )


def norm_forward(values, gain):
    scale = lax.rsqrt(jnp.mean(values * values, axis=-1, keepdims=True) + EPSILON)
    return (values * scale * gain, scale)


def norm_backward(values, scale, gain, upstream):
    gain_grad = jnp.sum(upstream * values * scale, axis=0)
    inner = jnp.mean(values * gain * upstream, axis=-1, keepdims=True)
    return (scale * gain * upstream - values * scale * scale * scale * inner, gain_grad)


def segment_window(extended, start, offset, length):
    return lax.dynamic_slice_in_dim(extended, start + 2 + offset, length, 1)


def new_moments(gradients, moments, clip_factor):
    return tuple(
        (
            MOMENTUM_BETA * moment + clip_factor * gradient
            for moment, gradient in zip(moments, gradients)
        )
    )


def new_weights(masters, next_moments, rate_now):
    return tuple(
        (
            (master * (1.0 - rate_now * WEIGHT_DECAY) - rate_now * moment).astype(jnp.bfloat16)
            for master, moment in zip(masters, next_moments)
        )
    )


MESH = pl.DeviceIdType.MESH
ANY = pl.BlockSpec(memory_space=pl.ANY)
INTO_VMEM = pl.BlockSpec(memory_space=pltpu.VMEM)


def finish_kernel(shapes, *refs):
    count = len(shapes)
    pieces = refs[:count]
    small = refs[count]
    wholes = refs[count + 1 : 2 * count + 1]
    small_out, square_out = refs[2 * count + 1 : 2 * count + 3]
    rest = refs[2 * count + 3 :]
    from_end = rest[:count]
    from_mid = rest[count : 2 * count]
    done = rest[2 * count : 3 * count]
    small_in, square_in = rest[3 * count : 3 * count + 2]
    send, recv, small_send, small_recv, square_send, square_recv, own_sem = rest[3 * count + 2 :]

    group = lax.axis_index("dp")
    place = lax.axis_index("seq")
    core = lax.axis_index("shard")
    x_bit = lax.rem(group, 2)
    y_bit = lax.div(group, 2)
    over_x = (group + 1 - 2 * x_bit, place, core)
    over_y = (group + 2 - 4 * y_bit, place, core)
    sibling = (group, place, 1 - core)
    z_near = (group, place + 1 - 2 * lax.rem(place, 2), core)
    z_far = (group, 3 - place, core)
    is_mid = jnp.logical_or(place == 1, place == 2)
    is_end = jnp.logical_not(is_mid)
    first_dev, second_dev = (over_x, over_y), (over_y, over_x)
    first_bit, second_bit = (x_bit, y_bit), (y_bit, x_bit)

    barrier = pltpu.get_barrier_semaphore()
    for device in (over_x, over_y, sibling, z_near, z_far):
        pl.semaphore_signal(barrier, inc=1, device_id=device, device_id_type=MESH)
    pl.semaphore_wait(barrier, 5)

    def remote(source, target, c, k, device):
        return pltpu.make_async_remote_copy(
            src_ref=source,
            dst_ref=target,
            send_sem=send.at[c, k],
            recv_sem=recv.at[c, k],
            device_id=device,
            device_id_type=MESH,
        )

    def rows_of(c, h, first, second, owner):
        unit = shapes[c][0] // 2
        start = owner * (8 * unit) + ((h * 2 + first) * 2 + second) * unit
        return pl.ds(pl.multiple_of(start, 16), unit)

    def mine(c, h):
        unit = shapes[c][0] // 2
        return done[c].at[pl.ds(h * unit, unit)]

    def add_rows(c, one, two, out, square=False):
        def body(i, carry):
            rows = pl.ds(pl.multiple_of(i * 16, 16), 16)
            total = one[rows, :].astype(jnp.float32) + two[rows, :].astype(jnp.float32)
            out[rows, :] = total.astype(jnp.bfloat16)
            return carry

        lax.fori_loop(0, shapes[c][0] // 16, body, 0)

    def add_squares(c):
        width = shapes[c][1]

        def body(i, total):
            rows = pl.ds(pl.multiple_of(i * 16, 16), 16)
            block = done[c][rows, :].astype(jnp.float32)
            block = block * block
            block = block[:8] + block[8:]
            for j in range(width // 128):
                total = total + block[:, j * 128 : (j + 1) * 128]
            return total

        square_out[...] += lax.fori_loop(
            0, shapes[c][0] // 16, body, jnp.zeros((8, 128), jnp.float32)
        )

    def z_in(c):
        return remote(pieces[c], from_end[c], c, 0, z_near)

    def z_mid(c):
        return remote(done[c], from_mid[c], c, 1, z_far)

    def z_out(c):
        return remote(done[c], done[c], c, 2, z_near)

    def to_second(c, h):
        rows = rows_of(c, h, first_bit[h], second_bit[h], core)
        return remote(mine(c, h), wholes[c].at[rows], c, 3 + h, second_dev[h])

    def to_first(c, h):
        rows = rows_of(c, h, first_bit[h], second_bit[h], core)
        return remote(mine(c, h), wholes[c].at[rows], c, 5 + h, first_dev[h])

    def pass_first(c, h):
        rows = rows_of(c, h, first_bit[h], 1 - second_bit[h], core)
        return remote(wholes[c].at[rows], wholes[c].at[rows], c, 7 + h, first_dev[h])

    def to_sibling(c, h, kind):
        first = first_bit[h] if kind < 2 else 1 - first_bit[h]
        second = second_bit[h] if kind % 2 == 0 else 1 - second_bit[h]
        rows = rows_of(c, h, first, second, core)
        source = mine(c, h) if kind == 0 else wholes[c].at[rows]
        return remote(source, wholes[c].at[rows], c, 9 + 2 * kind + h, sibling)

    def keep(c, h):
        rows = rows_of(c, h, first_bit[h], second_bit[h], core)
        return pltpu.make_async_copy(mine(c, h), wholes[c].at[rows], own_sem.at[c, h])

    def enter(c):
        @pl.when(is_end)
        def _():
            z_in(c).start()

    def middle_add(c):
        @pl.when(is_mid)
        def _():
            z_in(c).wait_recv()
            add_rows(c, pieces[c], from_end[c], done[c])
            z_mid(c).start()

    def middle_close(c):
        @pl.when(is_mid)
        def _():
            z_mid(c).wait()
            add_rows(c, done[c], from_mid[c], done[c])
            z_out(c).start()

        @pl.when(is_end)
        def _():
            z_out(c).wait_recv()

    def hand_out(c):
        for h in range(2):
            to_second(c, h).start()
            to_first(c, h).start()
            to_sibling(c, h, 0).start()
            keep(c, h).start()
        add_squares(c)

    def forward(c):
        for h in range(2):
            to_second(c, h).wait_recv()
            pass_first(c, h).start()
            to_sibling(c, h, 1).start()

    def last_hop(c):
        for h in range(2):
            to_first(c, h).wait_recv()
            to_sibling(c, h, 2).start()
            pass_first(c, h).wait_recv()
            to_sibling(c, h, 3).start()

    def drain(c):
        @pl.when(is_end)
        def _():
            z_in(c).wait_send()

        @pl.when(is_mid)
        def _():
            z_out(c).wait_send()

        for h in range(2):
            to_second(c, h).wait_send()
            to_first(c, h).wait_send()
            pass_first(c, h).wait_send()
            keep(c, h).wait()
            for kind in range(4):
                to_sibling(c, h, kind).wait()

    small_route = (sibling, over_x, over_y, z_near, z_far)

    def small_copy(k):
        return pltpu.make_async_remote_copy(
            src_ref=small_out,
            dst_ref=small_in.at[k],
            send_sem=small_send.at[k],
            recv_sem=small_recv.at[k],
            device_id=small_route[k],
            device_id_type=MESH,
        )

    def square_copy(k):
        return pltpu.make_async_remote_copy(
            src_ref=square_out,
            dst_ref=square_in.at[k],
            send_sem=square_send.at[k],
            recv_sem=square_recv.at[k],
            device_id=small_route[k],
            device_id_type=MESH,
        )

    small_out[...] = small[...]
    square_out[...] = jnp.zeros_like(square_out)
    enter(0)
    small_copy(0).start()
    for t in range(count + 3):
        if t + 1 < count:
            enter(t + 1)
        if t < 5:
            small_copy(t).wait()
            small_out[...] += small_in[t]
            if t < 4:
                small_copy(t + 1).start()
        if t < count:
            middle_add(t)
        if 0 <= t - 1 < count:
            middle_close(t - 1)
            hand_out(t - 1)
        if 0 <= t - 2 < count:
            forward(t - 2)
        if t >= count:
            k = t - count
            if k >= 1:
                square_copy(k - 1).wait()
                square_out[...] += square_in[k - 1]
            square_copy(k).start()
        if 0 <= t - 3 < count:
            last_hop(t - 3)
    square_copy(2).wait()
    square_out[...] += square_in[2]
    for c in range(count):
        drain(c)


def finish(pieces, small):
    shapes = tuple(piece.shape for piece in pieces)
    count = len(pieces)
    semaphore = pltpu.SemaphoreType.DMA
    outs = pl.pallas_call(
        functools.partial(finish_kernel, shapes),
        out_shape=[jax.ShapeDtypeStruct((8 * r, c), jnp.bfloat16) for r, c in shapes]
        + [
            jax.ShapeDtypeStruct((8, small.shape[1]), jnp.float32),
            jax.ShapeDtypeStruct((8, 128), jnp.float32),
        ],
        in_specs=[INTO_VMEM] * (count + 1),
        out_specs=[ANY] * count + [INTO_VMEM] * 2,
        scratch_shapes=[pltpu.VMEM(shape, jnp.bfloat16) for shape in shapes] * 3
        + [
            pltpu.VMEM((5, 8, small.shape[1]), jnp.float32),
            pltpu.VMEM((3, 8, 128), jnp.float32),
            semaphore((count, 17)),
            semaphore((count, 17)),
            semaphore((5,)),
            semaphore((5,)),
            semaphore((3,)),
            semaphore((3,)),
            semaphore((count, 2)),
        ],
        compiler_params=pltpu.CompilerParams(
            collective_id=0, has_side_effects=True, vmem_limit_bytes=48 * 1024 * 1024
        ),
    )(*pieces, small)
    return outs[:count], outs[count], outs[count + 1]


def swap_first(block, axis_bit):
    route = ((0, 1), (1, 0), (2, 3), (3, 2)) if axis_bit == 0 else ((0, 2), (2, 0), (1, 3), (3, 1))
    return lax.ppermute(block, "dp", route)


def halve(block, bit, axis_bit):
    rows = block.shape[0] // 2
    give = lax.dynamic_slice_in_dim(block, (1 - bit) * rows, rows, 0)
    keep = lax.dynamic_slice_in_dim(block, bit * rows, rows, 0)
    got = swap_first(give, axis_bit)
    return (keep.astype(jnp.float32) + got.astype(jnp.float32)).astype(jnp.bfloat16)


def scatter_piece(gradient):
    core = lax.axis_index("shard")
    group = lax.axis_index("dp")
    x_bit, y_bit = lax.rem(group, 2), lax.div(group, 2)
    rows = gradient.shape[0] // 2
    give = lax.dynamic_slice_in_dim(gradient, (1 - core) * rows, rows, 0)
    keep = lax.dynamic_slice_in_dim(gradient, core * rows, rows, 0)
    got = lax.ppermute(give, "shard", ((0, 1), (1, 0)))
    half = (keep.astype(jnp.float32) + got.astype(jnp.float32)).astype(jnp.bfloat16)
    part = half[: rows // 2]
    other = half[rows // 2 :]
    part = halve(halve(part, x_bit, 0), y_bit, 1)
    other = halve(halve(other, y_bit, 1), x_bit, 0)
    return jnp.concatenate([part, other], 0)


def local_fast(
    tokens,
    segments,
    cotangent,
    norm_one,
    in_weight,
    conv_weight,
    out_weight,
    norm_two,
    gate_weight,
    up_weight,
    down_weight,
    moment_norm_one,
    moment_in,
    moment_conv,
    moment_out,
    moment_norm_two,
    moment_gate,
    moment_up,
    moment_down,
    learn_rate,
    step_number,
):
    masters = (
        norm_one,
        in_weight,
        conv_weight,
        out_weight,
        norm_two,
        gate_weight,
        up_weight,
        down_weight,
    )
    moments = (
        moment_norm_one,
        moment_in,
        moment_conv,
        moment_out,
        moment_norm_two,
        moment_gate,
        moment_up,
        moment_down,
    )
    whole = (
        lax.all_gather(norm_one.astype(jnp.bfloat16), "shard", axis=0, tiled=True),
        lax.all_gather(in_weight.astype(jnp.bfloat16), "shard", axis=0, tiled=True),
        lax.all_gather(conv_weight.astype(jnp.bfloat16), "shard", axis=1, tiled=True),
        lax.all_gather(out_weight.astype(jnp.bfloat16), "shard", axis=0, tiled=True),
        lax.all_gather(norm_two.astype(jnp.bfloat16), "shard", axis=0, tiled=True),
        lax.all_gather(gate_weight.astype(jnp.bfloat16), "shard", axis=0, tiled=True),
        lax.all_gather(up_weight.astype(jnp.bfloat16), "shard", axis=0, tiled=True),
        lax.all_gather(down_weight.astype(jnp.bfloat16), "shard", axis=0, tiled=True),
    )
    gain_one = whole[0].astype(jnp.float32)
    in_matrix = whole[1]
    conv_taps = whole[2].astype(jnp.float32)
    out_matrix = whole[3]
    gain_two = whole[4].astype(jnp.float32)
    gate_matrix = whole[5]
    up_matrix = whole[6]
    down_matrix = whole[7]
    seq_count, span, model_width = tokens.shape
    row_count = seq_count * span
    hidden_in = tokens.reshape(row_count, model_width).astype(jnp.float32)
    start = lax.axis_index("seq") * span
    padding = jnp.full((seq_count, 2), -1, jnp.int32)
    extended = jnp.concatenate([padding, segments, padding], 1)
    current = segment_window(extended, start, 0, span)
    keep_one = (
        (segment_window(extended, start, -1, span) == current)
        .astype(jnp.float32)
        .reshape(row_count, 1)
    )
    keep_two = (
        (segment_window(extended, start, -2, span) == current)
        .astype(jnp.float32)
        .reshape(row_count, 1)
    )
    next_one = (
        (segment_window(extended, start, 1, span) == current)
        .astype(jnp.float32)
        .reshape(row_count, 1)
    )
    next_two = (
        (segment_window(extended, start, 2, span) == current)
        .astype(jnp.float32)
        .reshape(row_count, 1)
    )
    normed_f, scale_one = norm_forward(hidden_in, gain_one)
    normed_one = normed_f.astype(jnp.bfloat16)
    projected = rows_dot(normed_one, in_matrix)
    gate_b = projected[:, :model_width]
    gate_c = projected[:, model_width : 2 * model_width]
    values = projected[:, 2 * model_width :]
    mixed_in = gate_b * values
    mixed_grid = mixed_in.reshape(seq_count, span, model_width)
    before_edge = from_behind(mixed_grid[:, span - 2 :, :], "seq", 1)
    before = jnp.concatenate([before_edge, mixed_grid], 1)
    before_one = before[:, 1:-1, :].reshape(row_count, model_width)
    before_two = before[:, :-2, :].reshape(row_count, model_width)
    convolved = (
        conv_taps[2] * mixed_in
        + conv_taps[1] * keep_one * before_one
        + conv_taps[0] * keep_two * before_two
    )
    mixer_out = (gate_c * convolved).astype(jnp.bfloat16)
    hidden = hidden_in + rows_dot(mixer_out, out_matrix)
    normed_g, scale_two = norm_forward(hidden, gain_two)
    normed_two = normed_g.astype(jnp.bfloat16)
    gate_pre = rows_dot(normed_two, gate_matrix)
    upward = rows_dot(normed_two, up_matrix)
    sigmoid_gate = jax.nn.sigmoid(gate_pre)
    activated = (gate_pre * sigmoid_gate * upward).astype(jnp.bfloat16)
    block_out = (
        (hidden + rows_dot(activated, down_matrix)).astype(jnp.bfloat16).reshape(tokens.shape)
    )
    cotangent_rows = cotangent.reshape(row_count, model_width)
    down_grad = outer_dot(activated, cotangent_rows).astype(jnp.bfloat16)
    act_grad = back_dot(cotangent_rows, down_matrix)
    gate_back = (act_grad * upward * sigmoid_gate * (1.0 + gate_pre * (1.0 - sigmoid_gate))).astype(
        jnp.bfloat16
    )
    up_back = (act_grad * gate_pre * sigmoid_gate).astype(jnp.bfloat16)
    gate_grad = outer_dot(normed_two, gate_back).astype(jnp.bfloat16)
    up_grad = outer_dot(normed_two, up_back).astype(jnp.bfloat16)
    normed_two_grad = back_dot(gate_back, gate_matrix) + back_dot(up_back, up_matrix)
    hidden_part, gain_two_grad = norm_backward(hidden, scale_two, gain_two, normed_two_grad)
    hidden_grad = cotangent_rows.astype(jnp.float32) + hidden_part
    hidden_low = hidden_grad.astype(jnp.bfloat16)
    out_grad = outer_dot(mixer_out, hidden_low).astype(jnp.bfloat16)
    mixer_grad = back_dot(hidden_low, out_matrix)
    gate_c_grad = mixer_grad * convolved
    conv_out_grad = mixer_grad * gate_c
    conv_grid = conv_out_grad.reshape(seq_count, span, model_width)
    after_edge = from_behind(conv_grid[:, :2, :], "seq", -1)
    after = jnp.concatenate([conv_grid, after_edge], 1)
    follow_one = after[:, 1:-1, :].reshape(row_count, model_width)
    follow_two = after[:, 2:, :].reshape(row_count, model_width)
    mixed_grad = (
        conv_taps[2] * conv_out_grad
        + conv_taps[1] * next_one * follow_one
        + conv_taps[0] * next_two * follow_two
    )
    conv_grad = jnp.stack(
        [
            jnp.sum(conv_out_grad * keep_two * before_two, axis=0),
            jnp.sum(conv_out_grad * keep_one * before_one, axis=0),
            jnp.sum(conv_out_grad * mixed_in, axis=0),
        ],
        0,
    )
    proj_back = jnp.concatenate([mixed_grad * values, gate_c_grad, mixed_grad * gate_b], 1).astype(
        jnp.bfloat16
    )
    in_grad = outer_dot(normed_one, proj_back).astype(jnp.bfloat16)
    normed_one_grad = back_dot(proj_back, in_matrix)
    input_part, gain_one_grad = norm_backward(hidden_in, scale_one, gain_one, normed_one_grad)
    input_grad = (hidden_grad + input_part).astype(jnp.bfloat16).reshape(tokens.shape)
    core = lax.axis_index("shard")
    pieces = [scatter_piece(g) for g in (out_grad, in_grad, gate_grad, up_grad, down_grad)]
    small = jnp.concatenate(
        [gain_one_grad[None], conv_grad, gain_two_grad[None], jnp.zeros((3, model_width))], 0
    )
    wholes, small_sum, squares = finish(pieces, small)
    param_count = sum((member.size for member in whole))
    clip_level = CLIP_RATIO * math.sqrt(param_count)
    rate_now = learn_rate * jnp.minimum(1.0, (step_number + 1).astype(jnp.float32) / WARMUP)
    grad_norm = jnp.sqrt(jnp.sum(squares) + jnp.sum(small_sum * small_sum))
    clip_factor = clip_level / jnp.maximum(grad_norm, clip_level)
    large = (3, 1, 5, 6, 7)
    new_moment = {}
    new_weight = {}
    for place, gradient in zip(large, wholes):
        master, moment = masters[place], moments[place]
        rows = master.shape[0]
        base = master * (1.0 - rate_now * WEIGHT_DECAY) - (rate_now * MOMENTUM_BETA) * moment
        base = lax.all_gather(base.astype(jnp.bfloat16), "shard", axis=0, tiled=True)
        new_weight[place] = (
            base.astype(jnp.float32) - (rate_now * clip_factor) * gradient.astype(jnp.float32)
        ).astype(jnp.bfloat16)
        own = lax.dynamic_slice_in_dim(gradient, core * rows, rows, 0).astype(jnp.float32)
        new_moment[place] = MOMENTUM_BETA * moment + clip_factor * own
    width = model_width // 2
    small_own = lax.dynamic_slice_in_dim(small_sum, core * width, width, 1)
    for place, gradient in ((0, small_own[0]), (2, small_own[1:4]), (4, small_own[4])):
        new_moment[place] = MOMENTUM_BETA * moments[place] + clip_factor * gradient
    return (
        (block_out, input_grad, grad_norm)
        + tuple(new_moment[place] for place in range(8))
        + tuple(new_weight[place] for place in (1, 3, 5, 6, 7))
    )


def local(
    tokens,
    segments,
    cotangent,
    norm_one,
    in_weight,
    conv_weight,
    out_weight,
    norm_two,
    gate_weight,
    up_weight,
    down_weight,
    moment_norm_one,
    moment_in,
    moment_conv,
    moment_out,
    moment_norm_two,
    moment_gate,
    moment_up,
    moment_down,
    learn_rate,
    step_number,
):
    masters = (
        norm_one,
        in_weight,
        conv_weight,
        out_weight,
        norm_two,
        gate_weight,
        up_weight,
        down_weight,
    )
    moments = (
        moment_norm_one,
        moment_in,
        moment_conv,
        moment_out,
        moment_norm_two,
        moment_gate,
        moment_up,
        moment_down,
    )
    whole = (
        lax.all_gather(norm_one.astype(jnp.bfloat16), "shard", axis=0, tiled=True),
        lax.all_gather(in_weight.astype(jnp.bfloat16), "shard", axis=0, tiled=True),
        lax.all_gather(conv_weight.astype(jnp.bfloat16), "shard", axis=1, tiled=True),
        lax.all_gather(out_weight.astype(jnp.bfloat16), "shard", axis=0, tiled=True),
        lax.all_gather(norm_two.astype(jnp.bfloat16), "shard", axis=0, tiled=True),
        lax.all_gather(gate_weight.astype(jnp.bfloat16), "shard", axis=0, tiled=True),
        lax.all_gather(up_weight.astype(jnp.bfloat16), "shard", axis=0, tiled=True),
        lax.all_gather(down_weight.astype(jnp.bfloat16), "shard", axis=0, tiled=True),
    )
    gain_one = whole[0].astype(jnp.float32)
    in_matrix = whole[1]
    conv_taps = whole[2].astype(jnp.float32)
    out_matrix = whole[3]
    gain_two = whole[4].astype(jnp.float32)
    gate_matrix = whole[5]
    up_matrix = whole[6]
    down_matrix = whole[7]
    seq_count, span, model_width = tokens.shape
    row_count = seq_count * span
    hidden_in = tokens.reshape(row_count, model_width).astype(jnp.float32)
    start = lax.axis_index("seq") * span
    padding = jnp.full((seq_count, 2), -1, jnp.int32)
    extended = jnp.concatenate([padding, segments, padding], 1)
    current = segment_window(extended, start, 0, span)
    keep_one = (
        (segment_window(extended, start, -1, span) == current)
        .astype(jnp.float32)
        .reshape(row_count, 1)
    )
    keep_two = (
        (segment_window(extended, start, -2, span) == current)
        .astype(jnp.float32)
        .reshape(row_count, 1)
    )
    next_one = (
        (segment_window(extended, start, 1, span) == current)
        .astype(jnp.float32)
        .reshape(row_count, 1)
    )
    next_two = (
        (segment_window(extended, start, 2, span) == current)
        .astype(jnp.float32)
        .reshape(row_count, 1)
    )
    normed_f, scale_one = norm_forward(hidden_in, gain_one)
    normed_one = normed_f.astype(jnp.bfloat16)
    projected = rows_dot(normed_one, in_matrix)
    gate_b = projected[:, :model_width]
    gate_c = projected[:, model_width : 2 * model_width]
    values = projected[:, 2 * model_width :]
    mixed_in = gate_b * values
    mixed_grid = mixed_in.reshape(seq_count, span, model_width)
    before_edge = from_behind(mixed_grid[:, span - 2 :, :], "seq", 1)
    before = jnp.concatenate([before_edge, mixed_grid], 1)
    before_one = before[:, 1:-1, :].reshape(row_count, model_width)
    before_two = before[:, :-2, :].reshape(row_count, model_width)
    convolved = (
        conv_taps[2] * mixed_in
        + conv_taps[1] * keep_one * before_one
        + conv_taps[0] * keep_two * before_two
    )
    mixer_out = (gate_c * convolved).astype(jnp.bfloat16)
    hidden = hidden_in + rows_dot(mixer_out, out_matrix)
    normed_g, scale_two = norm_forward(hidden, gain_two)
    normed_two = normed_g.astype(jnp.bfloat16)
    gate_pre = rows_dot(normed_two, gate_matrix)
    upward = rows_dot(normed_two, up_matrix)
    sigmoid_gate = jax.nn.sigmoid(gate_pre)
    activated = (gate_pre * sigmoid_gate * upward).astype(jnp.bfloat16)
    block_out = (
        (hidden + rows_dot(activated, down_matrix)).astype(jnp.bfloat16).reshape(tokens.shape)
    )
    cotangent_rows = cotangent.reshape(row_count, model_width)
    down_grad = outer_dot(activated, cotangent_rows)
    act_grad = back_dot(cotangent_rows, down_matrix)
    gate_back = (act_grad * upward * sigmoid_gate * (1.0 + gate_pre * (1.0 - sigmoid_gate))).astype(
        jnp.bfloat16
    )
    up_back = (act_grad * gate_pre * sigmoid_gate).astype(jnp.bfloat16)
    gate_grad = outer_dot(normed_two, gate_back)
    up_grad = outer_dot(normed_two, up_back)
    normed_two_grad = back_dot(gate_back, gate_matrix) + back_dot(up_back, up_matrix)
    hidden_part, gain_two_grad = norm_backward(hidden, scale_two, gain_two, normed_two_grad)
    hidden_grad = cotangent_rows.astype(jnp.float32) + hidden_part
    hidden_low = hidden_grad.astype(jnp.bfloat16)
    out_grad = outer_dot(mixer_out, hidden_low)
    mixer_grad = back_dot(hidden_low, out_matrix)
    gate_c_grad = mixer_grad * convolved
    conv_out_grad = mixer_grad * gate_c
    conv_grid = conv_out_grad.reshape(seq_count, span, model_width)
    after_edge = from_behind(conv_grid[:, :2, :], "seq", -1)
    after = jnp.concatenate([conv_grid, after_edge], 1)
    follow_one = after[:, 1:-1, :].reshape(row_count, model_width)
    follow_two = after[:, 2:, :].reshape(row_count, model_width)
    mixed_grad = (
        conv_taps[2] * conv_out_grad
        + conv_taps[1] * next_one * follow_one
        + conv_taps[0] * next_two * follow_two
    )
    conv_grad = jnp.stack(
        [
            jnp.sum(conv_out_grad * keep_two * before_two, axis=0),
            jnp.sum(conv_out_grad * keep_one * before_one, axis=0),
            jnp.sum(conv_out_grad * mixed_in, axis=0),
        ],
        0,
    )
    proj_back = jnp.concatenate([mixed_grad * values, gate_c_grad, mixed_grad * gate_b], 1).astype(
        jnp.bfloat16
    )
    in_grad = outer_dot(normed_one, proj_back)
    normed_one_grad = back_dot(proj_back, in_matrix)
    input_part, gain_one_grad = norm_backward(hidden_in, scale_one, gain_one, normed_one_grad)
    input_grad = (hidden_grad + input_part).astype(jnp.bfloat16).reshape(tokens.shape)
    shares = (
        lax.psum_scatter(gain_one_grad, "shard", scatter_dimension=0, tiled=True),
        lax.psum_scatter(in_grad, "shard", scatter_dimension=0, tiled=True),
        lax.psum_scatter(conv_grad, "shard", scatter_dimension=1, tiled=True),
        lax.psum_scatter(out_grad, "shard", scatter_dimension=0, tiled=True),
        lax.psum_scatter(gain_two_grad, "shard", scatter_dimension=0, tiled=True),
        lax.psum_scatter(gate_grad, "shard", scatter_dimension=0, tiled=True),
        lax.psum_scatter(up_grad, "shard", scatter_dimension=0, tiled=True),
        lax.psum_scatter(down_grad, "shard", scatter_dimension=0, tiled=True),
    )
    param_count = sum((member.size for member in whole))
    clip_level = CLIP_RATIO * math.sqrt(param_count)
    rate_now = learn_rate * jnp.minimum(1.0, (step_number + 1).astype(jnp.float32) / WARMUP)
    large_places = (1, 3, 5, 6, 7)
    summed = lax.psum(
        (shares[0], shares[1], shares[2], shares[3], shares[4], shares[5], shares[6], shares[7]),
        ("dp", "seq"),
    )
    squares_local = sum((jnp.sum(member * member) for member in summed))
    squares_sum = lax.psum(squares_local, "shard")
    grad_norm = jnp.sqrt(squares_sum)
    clip_factor = clip_level / jnp.maximum(grad_norm, clip_level)
    next_moments = new_moments(summed, moments, clip_factor)
    large_low = new_weights(
        tuple((masters[place] for place in large_places)),
        tuple((next_moments[place] for place in large_places)),
        rate_now,
    )
    weights = (
        lax.all_gather(large_low[0], "shard", axis=0, tiled=True),
        lax.all_gather(large_low[1], "shard", axis=0, tiled=True),
        lax.all_gather(large_low[2], "shard", axis=0, tiled=True),
        lax.all_gather(large_low[3], "shard", axis=0, tiled=True),
        lax.all_gather(large_low[4], "shard", axis=0, tiled=True),
    )
    return (
        block_out,
        input_grad,
        grad_norm,
        next_moments[0],
        next_moments[1],
        next_moments[2],
        next_moments[3],
        next_moments[4],
        next_moments[5],
        next_moments[6],
        next_moments[7],
        weights[0],
        weights[1],
        weights[2],
        weights[3],
        weights[4],
    )


def solution(mesh):
    placed = (
        P(("dp", "shard"), "seq", None),
        P(("dp", "shard"), None),
        P(("dp", "shard"), "seq", None),
        P("shard"),
        P("shard", None),
        P(None, "shard"),
        P("shard", None),
        P("shard"),
        P("shard", None),
        P("shard", None),
        P("shard", None),
        P("shard"),
        P("shard", None),
        P(None, "shard"),
        P("shard", None),
        P("shard"),
        P("shard", None),
        P("shard", None),
        P("shard", None),
        P(),
        P(),
    )
    sizes = (mesh.shape["dp"], mesh.shape["seq"], mesh.shape["shard"])
    return jax.shard_map(
        local_fast if sizes == (4, 4, 2) else local,
        mesh=mesh,
        in_specs=placed,
        out_specs=(
            P(("dp", "shard"), "seq", None),
            P(("dp", "shard"), "seq", None),
            P(),
            P("shard"),
            P("shard", None),
            P(None, "shard"),
            P("shard", None),
            P("shard"),
            P("shard", None),
            P("shard", None),
            P("shard", None),
            P(),
            P(),
            P(),
            P(),
            P(),
        ),
        check_vma=False,
    )
```

```python
import functools
import math

import jax
import jax.numpy as jnp
from jax import lax
from jax.experimental import pallas as pl
from jax.experimental.pallas import tpu as pltpu
from jax.sharding import PartitionSpec as P

WARMUP = 2000


EPSILON = 1e-05
MOMENTUM_BETA = 0.9
WEIGHT_DECAY = 0.1
CLIP_RATIO = 0.25

FEED_PARTS = 3


def from_behind(block, axis, distance):
    devices = range(lax.axis_size(axis))
    route = [(i - distance, i) for i in devices if i - distance in devices]
    return lax.ppermute(block, axis, route)


def rows_dot(left, right):
    return jnp.dot(left, right, preferred_element_type=jnp.float32)


def outer_dot(left, right):
    return lax.dot_general(
        left, right, (((0,), (0,)), ((), ())), preferred_element_type=jnp.float32
    )


def back_dot(left, right):
    return lax.dot_general(
        left, right, (((1,), (1,)), ((), ())), preferred_element_type=jnp.float32
    )


def norm_forward(values, gain):
    scale = lax.rsqrt(jnp.mean(values * values, axis=-1, keepdims=True) + EPSILON)
    return (values * scale * gain, scale)


def norm_backward(values, scale, gain, upstream):
    gain_grad = jnp.sum(upstream * values * scale, axis=0)
    inner = jnp.mean(values * gain * upstream, axis=-1, keepdims=True)
    return (scale * gain * upstream - values * scale * scale * scale * inner, gain_grad)


def segment_window(extended, start, offset, length):
    return lax.dynamic_slice_in_dim(extended, start + 2 + offset, length, 1)


def new_moments(gradients, moments, clip_factor):
    return tuple(
        (
            MOMENTUM_BETA * moment + clip_factor * gradient
            for moment, gradient in zip(moments, gradients)
        )
    )


def new_weights(masters, next_moments, rate_now):
    return tuple(
        (
            (master * (1.0 - rate_now * WEIGHT_DECAY) - rate_now * moment).astype(jnp.bfloat16)
            for master, moment in zip(masters, next_moments)
        )
    )


MESH = pl.DeviceIdType.MESH
ANY = pl.BlockSpec(memory_space=pl.ANY)
INTO_VMEM = pl.BlockSpec(memory_space=pltpu.VMEM)
ROWS_DOT = (((1,), (0,)), ((), ()))
BACK_DOT = (((1,), (1,)), ((), ()))
KEEP_SLOTS, GOT_SLOTS, GIVE_SLOTS = 5, 3, 2


def kernel_dot(left, right, dims=ROWS_DOT):
    return lax.dot_general(left, right, dims, preferred_element_type=jnp.float32)


def finish_kernel(chunks, parts, wholes_count, unused, *refs):
    count = len(chunks)
    out_keep, out_give, in_keep, in_give = refs[:4]
    n2t, et, gate_back, up_back, act, small = refs[4:10]
    refs = refs[10 + unused :]
    whole_refs = refs[:wholes_count]
    small_out, square_out = refs[wholes_count : wholes_count + 2]
    rest = refs[wholes_count + 2 :]
    plain = sum(1 for chunk in chunks if chunk[0] != "feed")
    plain_keep, plain_got = rest[:plain], rest[plain : 2 * plain]
    rest = rest[2 * plain :]
    keep_ring, got_ring, give_ring, tiles = rest[:4]
    rest = rest[4:]
    first_in = rest[:count]
    pieces = rest[count : 2 * count]
    done = rest[2 * count : 3 * count]
    from_mid = rest[3 * count : 4 * count]
    small_in, square_in = rest[4 * count : 4 * count + 2]
    (
        send,
        recv,
        small_send,
        small_recv,
        square_send,
        square_recv,
        own_sem,
        load_sem,
        tile_sem,
        credit,
    ) = rest[4 * count + 2 :]

    group = lax.axis_index("dp")
    place = lax.axis_index("seq")
    core = lax.axis_index("shard")
    x_bit = lax.rem(group, 2)
    y_bit = lax.div(group, 2)
    over_x = (group + 1 - 2 * x_bit, place, core)
    over_y = (group + 2 - 4 * y_bit, place, core)
    sibling = (group, place, 1 - core)
    z_near = (group, place + 1 - 2 * lax.rem(place, 2), core)
    z_far = (group, 3 - place, core)
    is_mid = jnp.logical_or(place == 1, place == 2)
    is_end = jnp.logical_not(is_mid)
    first_dev, second_dev = (over_x, over_y), (over_y, over_x)
    first_bit, second_bit = (x_bit, y_bit), (y_bit, x_bit)

    barrier = pltpu.get_barrier_semaphore()
    for device in (over_x, over_y, sibling, z_near, z_far):
        pl.semaphore_signal(barrier, inc=1, device_id=device, device_id_type=MESH)
    pl.semaphore_wait(barrier, 5)

    def unit_of(c):
        return chunks[c][2] // 8

    def feed_index(c):
        return c - plain

    def is_feed(c):
        return chunks[c][0] == "feed"

    def keep_of(c):
        return keep_ring.at[feed_index(c) % KEEP_SLOTS] if is_feed(c) else plain_keep[c]

    def got_of(c):
        return got_ring.at[feed_index(c) % GOT_SLOTS] if is_feed(c) else plain_got[c]

    def remote(source, target, c, k, device):
        return pltpu.make_async_remote_copy(
            src_ref=source,
            dst_ref=target,
            send_sem=send.at[c, k],
            recv_sem=recv.at[c, k],
            device_id=device,
            device_id_type=MESH,
        )

    def aligned(start, size):
        return pl.ds(pl.multiple_of(start, 16), size)

    def rows_of(c, h, first, second, owner):
        unit = unit_of(c)
        _, _, _, _, base, stride = chunks[c][:6]
        return aligned(base + owner * stride + ((h * 2 + first) * 2 + second) * unit, unit)

    def local_rows(c, h, first, second=None):
        unit = unit_of(c)
        if second is None:
            return aligned((h * 2 + first) * 2 * unit, 2 * unit)
        return aligned(((h * 2 + first) * 2 + second) * unit, unit)

    def whole_of(c):
        return whole_refs[chunks[c][3 + 0]]

    def mine(c, h):
        unit = unit_of(c)
        return done[c].at[pl.ds(h * unit, unit)]

    def add_into(target, target_row, one, one_row, two, two_row, rows):
        def body(i, carry):
            at = lambda start: aligned(start + i * 16, 16)
            total = one[at(one_row), :].astype(jnp.float32) + two[at(two_row), :].astype(
                jnp.float32
            )
            target[at(target_row), :] = total.astype(jnp.bfloat16)
            return carry

        lax.fori_loop(0, rows // 16, body, 0)

    def add_squares(c):
        width = chunks[c][7]

        def body(i, total):
            block = done[c][aligned(i * 16, 16), :].astype(jnp.float32)
            block = block * block
            block = block[:8] + block[8:]
            for j in range(width // 128):
                total = total + block[:, j * 128 : (j + 1) * 128]
            return total

        square_out[...] += lax.fori_loop(
            0, 2 * unit_of(c) // 16, body, jnp.zeros((8, 128), jnp.float32)
        )

    def over_core(c):
        if is_feed(c):
            return remote(give_ring.at[feed_index(c) % GIVE_SLOTS], got_of(c), c, 0, sibling)
        name, start, rows = chunks[c][0], chunks[c][6], chunks[c][2]
        source = out_give if name == "out" else in_give
        return remote(source.at[pl.ds(start, rows)], got_of(c), c, 0, sibling)

    def load_keep(c):
        name, start, rows = chunks[c][0], chunks[c][6], chunks[c][2]
        source = out_keep if name == "out" else in_keep
        return pltpu.make_async_copy(source.at[pl.ds(start, rows)], plain_keep[c], load_sem.at[c])

    def over_first(c, h):
        unit = unit_of(c)
        source = keep_of(c).at[local_rows(c, h, 1 - first_bit[h])]
        return remote(source, first_in[c].at[pl.ds(h * 2 * unit, 2 * unit)], c, 1 + h, first_dev[h])

    def over_second(c, h):
        unit = unit_of(c)
        source = keep_of(c).at[local_rows(c, h, first_bit[h], 1 - second_bit[h])]
        return remote(source, pieces[c].at[pl.ds(h * unit, unit)], c, 3 + h, second_dev[h])

    def z_in(c):
        return remote(pieces[c], done[c], c, 5, z_near)

    def z_mid(c):
        return remote(done[c], from_mid[c], c, 6, z_far)

    def z_out(c):
        return remote(done[c], done[c], c, 7, z_near)

    def to_second(c, h):
        rows = rows_of(c, h, first_bit[h], second_bit[h], core)
        return remote(mine(c, h), whole_of(c).at[rows], c, 8 + h, second_dev[h])

    def to_first(c, h):
        rows = rows_of(c, h, first_bit[h], second_bit[h], core)
        return remote(mine(c, h), whole_of(c).at[rows], c, 10 + h, first_dev[h])

    def pass_first(c, h):
        rows = rows_of(c, h, first_bit[h], 1 - second_bit[h], core)
        return remote(whole_of(c).at[rows], whole_of(c).at[rows], c, 12 + h, first_dev[h])

    def to_sibling(c, h, kind):
        first = first_bit[h] if kind < 2 else 1 - first_bit[h]
        second = second_bit[h] if kind % 2 == 0 else 1 - second_bit[h]
        rows = rows_of(c, h, first, second, core)
        source = mine(c, h) if kind == 0 else whole_of(c).at[rows]
        return remote(source, whole_of(c).at[rows], c, 14 + 2 * kind + h, sibling)

    def own_copy(c, h):
        rows = rows_of(c, h, first_bit[h], second_bit[h], core)
        return pltpu.make_async_copy(mine(c, h), whole_of(c).at[rows], own_sem.at[c, h])

    def load_tile(c, half):
        part, kind = chunks[c][1]
        cols = tiles.shape[2]
        source = (gate_back, up_back, act)[kind]
        return pltpu.make_async_copy(
            source.at[:, pl.ds((half * parts + part) * cols, cols)], tiles.at[half], tile_sem.at[half]
        )

    def produce(c):
        if not is_feed(c):
            over_core(c).start()
            load_keep(c).start()
            return
        index = feed_index(c)
        kind = chunks[c][1][1]
        keep, give = keep_of(c), give_ring.at[index % GIVE_SLOTS]
        rows = n2t.shape[0] // 2
        for half in range(2):
            load_tile(c, half).wait()

        @pl.loop(0, 2)
        def _(r):
            target = aligned(r * rows, rows)
            for ref, side in ((keep, core), (give, 1 - core)):
                if kind < 2:
                    block = kernel_dot(n2t[aligned(side * rows, rows), :], tiles[r])
                else:
                    block = kernel_dot(et[target, :], tiles[side])
                ref[target, :] = block.astype(jnp.bfloat16)

        if c + 1 < count:
            for half in range(2):
                load_tile(c + 1, half).start()
        if index >= GOT_SLOTS:
            pl.semaphore_wait(credit, 1)
        over_core(c).start()

    def sum_core(c):
        if not is_feed(c):
            load_keep(c).wait()
        over_core(c).wait()
        add_into(keep_of(c), 0, keep_of(c), 0, got_of(c), 0, chunks[c][2])
        if is_feed(c) and c + GOT_SLOTS < count:
            pl.semaphore_signal(credit, inc=1, device_id=sibling, device_id_type=MESH)
        for h in range(2):
            over_first(c, h).start()

    def sum_first(c):
        unit = unit_of(c)
        for h in range(2):
            over_first(c, h).wait()
            row = (h * 2 + first_bit[h]) * 2 * unit
            add_into(keep_of(c), row, keep_of(c), row, first_in[c], h * 2 * unit, 2 * unit)
            over_second(c, h).start()

    def sum_second(c):
        unit = unit_of(c)
        for h in range(2):
            over_second(c, h).wait()
            row = ((h * 2 + first_bit[h]) * 2 + second_bit[h]) * unit
            add_into(pieces[c], h * unit, pieces[c], h * unit, keep_of(c), row, unit)

        @pl.when(is_end)
        def _():
            z_in(c).start()

    def sum_end(c):
        @pl.when(is_mid)
        def _():
            z_in(c).wait_recv()
            add_into(done[c], 0, pieces[c], 0, done[c], 0, 2 * unit_of(c))
            z_mid(c).start()

    def sum_middle(c):
        @pl.when(is_mid)
        def _():
            z_mid(c).wait()
            add_into(done[c], 0, done[c], 0, from_mid[c], 0, 2 * unit_of(c))
            z_out(c).start()

        @pl.when(is_end)
        def _():
            z_in(c).wait_send()
            z_out(c).wait_recv()

        for h in range(2):
            to_second(c, h).start()
            to_first(c, h).start()
            to_sibling(c, h, 0).start()
            own_copy(c, h).start()
        add_squares(c)

    def forward(c):
        for h in range(2):
            to_second(c, h).wait_recv()
            pass_first(c, h).start()
            to_sibling(c, h, 1).start()

    def last_hop(c):
        for h in range(2):
            to_first(c, h).wait_recv()
            to_sibling(c, h, 2).start()
            pass_first(c, h).wait_recv()
            to_sibling(c, h, 3).start()

    def drain(c):
        @pl.when(is_mid)
        def _():
            z_out(c).wait_send()

        for h in range(2):
            to_second(c, h).wait_send()
            to_first(c, h).wait_send()
            pass_first(c, h).wait_send()
            own_copy(c, h).wait()
            for kind in range(4):
                to_sibling(c, h, kind).wait()

    small_route = (sibling, over_x, over_y, z_near, z_far)

    def small_copy(k):
        return pltpu.make_async_remote_copy(
            src_ref=small_out,
            dst_ref=small_in.at[k],
            send_sem=small_send.at[k],
            recv_sem=small_recv.at[k],
            device_id=small_route[k],
            device_id_type=MESH,
        )

    def square_copy(k):
        return pltpu.make_async_remote_copy(
            src_ref=square_out,
            dst_ref=square_in.at[k],
            send_sem=square_send.at[k],
            recv_sem=square_recv.at[k],
            device_id=small_route[k],
            device_id_type=MESH,
        )

    small_out[...] = small[...]
    square_out[...] = jnp.zeros_like(square_out)
    for half in range(2):
        load_tile(plain, half).start()
    small_copy(0).start()

    def at(step, action):
        if 0 <= step < count:
            action(step)

    squares_from = count + 3
    for t in range(count + 7):
        at(t, produce)
        if t < 5:
            small_copy(t).wait()
            small_out[...] += small_in[t]
            if t < 4:
                small_copy(t + 1).start()
        at(t - 1, sum_first)
        at(t - 2, sum_second)
        at(t - 3, sum_middle)
        if squares_from <= t < squares_from + 4:
            k = t - squares_from
            if k >= 1:
                square_copy(k - 1).wait()
                square_out[...] += square_in[k - 1]
            if k < 3:
                square_copy(k).start()
        at(t - 5, last_hop)
        at(t, sum_core)
        at(t - 2, sum_end)
        at(t - 4, forward)
    for c in range(count):
        drain(c)


def finish(out_sides, in_sides, n2t, et, gate_back, up_back, act, parts, small, order):
    width = n2t.shape[0]
    half = width // 2
    cols = gate_back.shape[1] // (2 * parts)
    in_cols = in_sides[0].shape[1]
    chunks = [("out", None, half, 0, 0, half, 0, width)]
    chunks += [("in", None, half // 2, 1, t * half // 2, half, t * half // 2, in_cols) for t in range(2)]
    for part in range(parts):
        for kind in range(3):
            first = (part * 3 + kind) * 2 * width
            chunks.append(("feed", (part, kind), width, 2, first, width, 0, cols))
    count, plain = len(chunks), 3
    low = jnp.bfloat16
    semaphore = pltpu.SemaphoreType.DMA
    wholes = [(width, width), (width, in_cols), (parts * 3 * 2 * width, cols)]
    eighths = [(chunk[2] // 8, chunk[7]) for chunk in chunks]
    plain_shapes = [(chunk[2], chunk[7]) for chunk in chunks[:plain]]
    pair = [pltpu.VMEM((2 * rows, c), low) for rows, c in eighths]
    outs = pl.pallas_call(
        functools.partial(finish_kernel, tuple(chunks), parts, len(wholes), len(order)),
        out_shape=[jax.ShapeDtypeStruct(shape, low) for shape in wholes]
        + [
            jax.ShapeDtypeStruct((8, small.shape[1]), jnp.float32),
            jax.ShapeDtypeStruct((8, 128), jnp.float32),
        ],
        in_specs=[ANY] * 4 + [INTO_VMEM] * 2 + [ANY] * 3 + [INTO_VMEM] + [ANY] * len(order),
        out_specs=[ANY] * len(wholes) + [INTO_VMEM] * 2,
        scratch_shapes=[pltpu.VMEM(shape, low) for shape in plain_shapes] * 2
        + [
            pltpu.VMEM((KEEP_SLOTS, width, cols), low),
            pltpu.VMEM((GOT_SLOTS, width, cols), low),
            pltpu.VMEM((GIVE_SLOTS, width, cols), low),
            pltpu.VMEM((2, act.shape[0], cols), low),
        ]
        + [pltpu.VMEM((4 * rows, c), low) for rows, c in eighths]
        + pair * 3
        + [
            pltpu.VMEM((5, 8, small.shape[1]), jnp.float32),
            pltpu.VMEM((3, 8, 128), jnp.float32),
            semaphore((count, 22)),
            semaphore((count, 22)),
            semaphore((5,)),
            semaphore((5,)),
            semaphore((3,)),
            semaphore((3,)),
            semaphore((count, 2)),
            semaphore((plain,)),
            semaphore((2,)),
            pltpu.SemaphoreType.REGULAR,
        ],
        compiler_params=pltpu.CompilerParams(
            collective_id=0, has_side_effects=True, vmem_limit_bytes=62 * 1024 * 1024
        ),
    )(*out_sides, *in_sides, n2t, et, gate_back, up_back, act, small, *order)
    return outs[: len(wholes)], outs[-2], outs[-1]


def feed_kernel(step, n2, e, wg, wu, wd, out, back, act, gate_back, up_back):
    @pl.when(pl.program_id(0) == 0)
    def _():
        out[...] = jnp.zeros_like(out)
        back[...] = jnp.zeros_like(back)

    @pl.loop(0, n2.shape[0] // step)
    def _(t):
        rows = pl.ds(pl.multiple_of(t * step, step), step)
        gate = kernel_dot(n2[rows, :], wg[...])
        up = kernel_dot(n2[rows, :], wu[...])
        grad = kernel_dot(e[rows, :], wd[...], BACK_DOT)
        sigmoid = 0.5 * jnp.tanh(0.5 * gate) + 0.5
        silu = gate * sigmoid
        low_act = (silu * up).astype(jnp.bfloat16)
        low_up = (grad * silu).astype(jnp.bfloat16)
        low_gate = (grad * up * (sigmoid + silu * (1.0 - sigmoid))).astype(jnp.bfloat16)
        act[rows, :] = low_act
        gate_back[rows, :] = low_gate
        up_back[rows, :] = low_up
        out[rows, :] += kernel_dot(low_act, wd[...])
        back[rows, :] += kernel_dot(low_gate, wg[...], BACK_DOT) + kernel_dot(
            low_up, wu[...], BACK_DOT
        )


def feed(n2, e, gate_matrix, up_matrix, down_matrix, tiles):
    rows, width = n2.shape
    cols = gate_matrix.shape[1] // tiles
    whole = pl.BlockSpec((rows, width), lambda i: (0, 0), pipeline_mode=pl.Buffered(1))
    tile = pl.BlockSpec((rows, cols), lambda i: (0, i))
    return pl.pallas_call(
        functools.partial(feed_kernel, rows // 2),
        grid=(tiles,),
        in_specs=[whole, whole]
        + [pl.BlockSpec((width, cols), lambda i: (0, i))] * 2
        + [pl.BlockSpec((cols, width), lambda i: (i, 0))],
        out_specs=[whole, whole, tile, tile, tile],
        out_shape=[jax.ShapeDtypeStruct((rows, width), jnp.float32)] * 2
        + [jax.ShapeDtypeStruct((rows, tiles * cols), jnp.bfloat16)] * 3,
        cost_estimate=pl.CostEstimate(
            flops=12 * rows * width * cols * tiles,
            bytes_accessed=70 * 1024 * 1024,
            transcendentals=rows * cols * tiles,
        ),
        compiler_params=pltpu.CompilerParams(vmem_limit_bytes=56 * 1024 * 1024),
    )(n2, e, gate_matrix, up_matrix, down_matrix)


CORE_ROUTE = ((0, 1), (1, 0))


def over_core(give):
    return lax.ppermute(give, "shard", CORE_ROUTE)


def scale_of(values):
    return lax.rsqrt(jnp.mean(values * values, axis=-1, keepdims=True) + EPSILON)


def shifted(values, edge, distance):
    rows = values.shape[0]
    moved = pltpu.roll(values, (-distance) % rows, 0)
    index = lax.broadcasted_iota(jnp.int32, values.shape, 0)
    if distance < 0:
        for row in range(-distance):
            moved = jnp.where(index == row, edge[8 + distance + row : 9 + distance + row, :], moved)
    else:
        for row in range(distance):
            moved = jnp.where(index == rows - distance + row, edge[row : row + 1, :], moved)
    return moved


def mixer_kernel(
    x_ref, edge_ref, masks, gain_one, gain_two, taps, w_in, w_out, proj, conv, hid, n1t, zt, n2, n2t, carry
):
    width = x_ref.shape[1]
    low = jnp.bfloat16

    def project(values, first, count):
        return kernel_dot(values, w_in[:, first * width : (first + count) * width])

    def normed(values):
        return (values * scale_of(values) * gain_one[...]).astype(low)

    @pl.when(pl.program_id(0) == 0)
    def _():
        edge = normed(edge_ref[...].astype(jnp.float32))
        mixed = project(edge, 0, 1) * project(edge, 2, 1)
        carry[...] = mixed[8:, :]

    x = x_ref[...].astype(jnp.float32)
    first = normed(x)
    n1t[...] = first.T
    gate_b, gate_c, values = project(first, 0, 1), project(first, 1, 1), project(first, 2, 1)
    proj[:, :width] = gate_b
    proj[:, width : 2 * width] = gate_c
    proj[:, 2 * width :] = values
    mixed = gate_b * values
    edge = carry[...]
    convolved = (
        taps[2:3, :] * mixed
        + taps[1:2, :] * masks[:, 0:1] * shifted(mixed, edge, -1)
        + taps[0:1, :] * masks[:, 1:2] * shifted(mixed, edge, -2)
    )
    carry[...] = mixed[mixed.shape[0] - 8 :, :]
    conv[...] = convolved
    mixer_out = (gate_c * convolved).astype(low)
    zt[...] = mixer_out.T
    hidden = x + kernel_dot(mixer_out, w_out[...])
    hid[...] = hidden
    second = (hidden * scale_of(hidden) * gain_two[...]).astype(low)
    n2[...] = second
    n2t[...] = second.T


def resident(shape):
    return pl.BlockSpec(shape, lambda i: (0,) * len(shape), pipeline_mode=pl.Buffered(1))


def mixer(x, edge, masks, gain_one, gain_two, taps, w_in, w_out):
    rows, width = x.shape
    step = rows // 4
    tile = lambda cols: pl.BlockSpec((step, cols), lambda i: (i, 0))
    turned = pl.BlockSpec((width, step), lambda i: (0, i))
    low, full = jnp.bfloat16, jnp.float32
    shape = jax.ShapeDtypeStruct
    return pl.pallas_call(
        mixer_kernel,
        grid=(4,),
        in_specs=[
            tile(width),
            resident(edge.shape),
            tile(masks.shape[1]),
            resident(gain_one.shape),
            resident(gain_two.shape),
            resident(taps.shape),
            resident(w_in.shape),
            resident(w_out.shape),
        ],
        out_specs=[tile(3 * width), tile(width), tile(width), turned, turned, tile(width), turned],
        out_shape=[
            shape((rows, 3 * width), full),
            shape((rows, width), full),
            shape((rows, width), full),
            shape((width, rows), low),
            shape((width, rows), low),
            shape((rows, width), low),
            shape((width, rows), low),
        ],
        scratch_shapes=[pltpu.VMEM((8, width), full)],
        compiler_params=pltpu.CompilerParams(vmem_limit_bytes=56 * 1024 * 1024),
        cost_estimate=pl.CostEstimate(
            flops=8 * rows * width * width, bytes_accessed=48 * rows * width, transcendentals=0
        ),
    )(x, edge, masks, gain_one, gain_two, taps, w_in, w_out)


def out_back_kernel(parts, *refs):
    h_ref, c_ref, gc_ref, e_ref, gain_two, w_out, zt = refs[:7]
    outs, backs = refs[7 : 7 + parts], refs[7 + parts : 7 + 2 * parts]
    block_out, hidden_grad, gc_grad, conv_grad, gain_grad, keep, give, total = refs[-8:]
    step = pl.program_id(0)
    core = lax.axis_index("shard")
    hidden = h_ref[...]
    gain = gain_two[...]
    summed = hidden
    for ref in outs:
        summed = summed + ref[...]
    block_out[...] = summed.astype(jnp.bfloat16)
    upstream = backs[0][...]
    for ref in backs[1:]:
        upstream = upstream + ref[...]
    scale = scale_of(hidden)
    inner = jnp.mean(hidden * gain * upstream, axis=-1, keepdims=True)
    grad = (
        e_ref[...].astype(jnp.float32)
        + scale * gain * upstream
        - hidden * (scale * scale * scale * inner)
    )
    hidden_grad[...] = grad
    low = grad.astype(jnp.bfloat16)
    share = jnp.sum(upstream * hidden * scale, axis=0, keepdims=True)
    mixer_grad = kernel_dot(low, w_out[...], BACK_DOT)
    gc_grad[...] = (mixer_grad * c_ref[...]).astype(jnp.bfloat16)
    conv_grad[...] = mixer_grad * gc_ref[...]

    @pl.when(step == 0)
    def _():
        total[...] = jnp.zeros_like(total)
        gain_grad[...] = jnp.zeros_like(gain_grad)

    gain_grad[0:1, :] += share
    total[...] += kernel_dot(zt[...], low)

    @pl.when(step == pl.num_programs(0) - 1)
    def _():
        rows = total.shape[0] // 2
        for target, side in ((keep, core), (give, 1 - core)):
            target[...] = total[pl.ds(pl.multiple_of(side * rows, rows), rows), :].astype(
                jnp.bfloat16
            )


def skip_last(kernel, inputs, extra):
    def wrapped(*refs):
        return kernel(*refs[:inputs], *refs[inputs + extra :])

    return wrapped


def out_back(hidden, convolved, proj, e, gain_two, w_out, zt, outs, backs, order):
    rows, width = hidden.shape
    step = rows // 4
    tile = pl.BlockSpec((step, width), lambda i: (i, 0))
    low, full = jnp.bfloat16, jnp.float32
    shape = jax.ShapeDtypeStruct
    inputs = 7 + len(outs) + len(backs)
    return pl.pallas_call(
        skip_last(functools.partial(out_back_kernel, len(outs)), inputs, len(order)),
        grid=(4,),
        in_specs=[
            tile,
            tile,
            pl.BlockSpec((step, width), lambda i: (i, 1)),
            tile,
            resident(gain_two.shape),
            resident(w_out.shape),
            pl.BlockSpec((width, step), lambda i: (0, i)),
        ]
        + [tile] * (len(outs) + len(backs))
        + [ANY] * len(order),
        out_specs=[tile] * 4 + [resident((8, width))] + [resident((width // 2, width))] * 2,
        out_shape=[
            shape((rows, width), low),
            shape((rows, width), full),
            shape((rows, width), low),
            shape((rows, width), full),
            shape((8, width), full),
            shape((width // 2, width), low),
            shape((width // 2, width), low),
        ],
        scratch_shapes=[pltpu.VMEM((width, width), full)],
        compiler_params=pltpu.CompilerParams(vmem_limit_bytes=56 * 1024 * 1024),
        cost_estimate=pl.CostEstimate(
            flops=4 * rows * width * width, bytes_accessed=48 * rows * width, transcendentals=0
        ),
    )(hidden, convolved, proj, e, gain_two, w_out, zt, *outs, *backs, *order)


def conv_back_kernel(
    dc_ref, dgc, gb_ref, v_ref, masks, edge_ref, taps, n1t, dp_ref, taps_grad, keep, give, carry, all_dp
):
    step = pl.program_id(0)
    last = pl.num_programs(0) - 1
    core = lax.axis_index("shard")
    rows, width = dc_ref.shape
    low = jnp.bfloat16

    @pl.when(step == 0)
    def _():
        carry[...] = edge_ref[...]
        taps_grad[...] = jnp.zeros_like(taps_grad)

    grad = dc_ref[...]
    edge = carry[...]
    next_one = masks[:, 2:3] * shifted(grad, edge, 1)
    next_two = masks[:, 3:4] * shifted(grad, edge, 2)
    carry[...] = grad[:8, :]
    gate_b, values = gb_ref[...], v_ref[...]
    mixed = gate_b * values
    for row, term in ((0, next_two), (1, next_one), (2, grad)):
        taps_grad[row : row + 1, :] += jnp.sum(term * mixed, axis=0, keepdims=True)
    mixed_grad = taps[2:3, :] * grad + taps[1:2, :] * next_one + taps[0:1, :] * next_two
    place = pl.ds(pl.multiple_of((last - step) * rows, rows), rows)
    for k, block in enumerate(
        ((mixed_grad * values).astype(low), dgc[...], (mixed_grad * gate_b).astype(low))
    ):
        dp_ref[:, k * width : (k + 1) * width] = block
        all_dp[place, k * width : (k + 1) * width] = block

    @pl.when(step == last)
    def _():
        half = width // 2
        for target, side in ((keep, core), (give, 1 - core)):
            left = n1t[pl.ds(pl.multiple_of(side * half, half), half), :]
            for k in range(3):
                cols = slice(k * width, (k + 1) * width)
                target[:, cols] = kernel_dot(left, all_dp[:, cols]).astype(low)


def conv_back(conv_grad, gc_grad, proj, masks, edge, taps, n1t, order):
    rows, width = conv_grad.shape
    step = rows // 4
    tile = lambda cols, k=0: pl.BlockSpec((step, cols), lambda i: (3 - i, k))
    low, full = jnp.bfloat16, jnp.float32
    shape = jax.ShapeDtypeStruct
    return pl.pallas_call(
        skip_last(conv_back_kernel, 8, len(order)),
        grid=(4,),
        in_specs=[
            tile(width),
            tile(width),
            tile(width, 0),
            tile(width, 2),
            tile(masks.shape[1]),
            resident(edge.shape),
            resident(taps.shape),
            resident(n1t.shape),
        ]
        + [ANY] * len(order),
        out_specs=[tile(3 * width), resident((8, width))] + [resident((width // 2, 3 * width))] * 2,
        out_shape=[
            shape((rows, 3 * width), low),
            shape((8, width), full),
            shape((width // 2, 3 * width), low),
            shape((width // 2, 3 * width), low),
        ],
        scratch_shapes=[pltpu.VMEM((8, width), full), pltpu.VMEM((rows, 3 * width), low)],
        compiler_params=pltpu.CompilerParams(vmem_limit_bytes=56 * 1024 * 1024),
        cost_estimate=pl.CostEstimate(
            flops=6 * rows * width * width, bytes_accessed=32 * rows * width, transcendentals=0
        ),
    )(conv_grad, gc_grad, proj, proj, masks, edge, taps, n1t, *order)


def in_back_kernel(dp_ref, w_in, x_ref, grad_ref, gain_one, input_grad, gain_grad):
    upstream = kernel_dot(dp_ref[...], w_in[...], BACK_DOT)
    x = x_ref[...].astype(jnp.float32)
    gain = gain_one[...]
    scale = scale_of(x)
    inner = jnp.mean(x * gain * upstream, axis=-1, keepdims=True)
    input_grad[...] = (
        grad_ref[...] + scale * gain * upstream - x * (scale * scale * scale * inner)
    ).astype(jnp.bfloat16)

    @pl.when(pl.program_id(0) == 0)
    def _():
        gain_grad[...] = jnp.zeros_like(gain_grad)

    gain_grad[0:1, :] += jnp.sum(upstream * x * scale, axis=0, keepdims=True)


def in_back(dp, w_in, x, hidden_grad, gain_one, order):
    rows, width = x.shape
    step = rows // 4
    tile = lambda cols: pl.BlockSpec((step, cols), lambda i: (i, 0))
    return pl.pallas_call(
        skip_last(in_back_kernel, 5, len(order)),
        grid=(4,),
        in_specs=[
            tile(3 * width),
            resident(w_in.shape),
            tile(width),
            tile(width),
            resident(gain_one.shape),
        ]
        + [ANY] * len(order),
        out_specs=[tile(width), resident((8, width))],
        out_shape=[
            jax.ShapeDtypeStruct((rows, width), jnp.bfloat16),
            jax.ShapeDtypeStruct((8, width), jnp.float32),
        ],
        compiler_params=pltpu.CompilerParams(vmem_limit_bytes=56 * 1024 * 1024),
        cost_estimate=pl.CostEstimate(
            flops=6 * rows * width * width, bytes_accessed=20 * rows * width, transcendentals=0
        ),
    )(dp, w_in, x, hidden_grad, gain_one, *order)


def base_kernel(rate, master, moment, base):
    base[...] = (
        master[...] * (1.0 - rate[0] * WEIGHT_DECAY) - (rate[0] * MOMENTUM_BETA) * moment[...]
    ).astype(jnp.bfloat16)


def base_of(rate, master, moment, order):
    rows, cols = master.shape
    step = rows // 4
    tile = pl.BlockSpec((step, cols), lambda i: (i, 0))
    return pl.pallas_call(
        skip_last(base_kernel, 3, len(order)),
        grid=(4,),
        in_specs=[pl.BlockSpec(memory_space=pltpu.SMEM), tile, tile] + [ANY] * len(order),
        out_specs=tile,
        out_shape=jax.ShapeDtypeStruct((rows, cols), jnp.bfloat16),
        compiler_params=pltpu.CompilerParams(vmem_limit_bytes=40 * 1024 * 1024),
        cost_estimate=pl.CostEstimate(
            flops=3 * rows * cols, bytes_accessed=10 * rows * cols, transcendentals=0
        ),
    )(rate, master, moment, *order)


def update_kernel(bits, scalars, *refs):
    core = bits[2]
    clip, scale = scalars[0], scalars[1]
    count = len(refs) // 7
    for n in range(count):
        own, other, base_own, base_other, moment = refs[5 * n : 5 * n + 5]
        weight, new_moment = refs[5 * count + 2 * n : 5 * count + 2 * n + 2]
        rows = own.shape[0]
        gradient = own[...].astype(jnp.float32)
        new_moment[...] = MOMENTUM_BETA * moment[...] + clip * gradient
        mine = pl.ds(pl.multiple_of(core * rows, rows), rows)
        theirs = pl.ds(pl.multiple_of((1 - core) * rows, rows), rows)
        weight[mine, :] = (base_own[...].astype(jnp.float32) - scale * gradient).astype(jnp.bfloat16)
        weight[theirs, :] = (
            base_other[...].astype(jnp.float32) - scale * other[...].astype(jnp.float32)
        ).astype(jnp.bfloat16)


def update_rows(bits, scalars, grid, block, matrices):
    width = block[1]
    in_specs, out_specs, out_shape, operands = [], [], [], []
    total = 0
    for gradient, source, column, base, base_other, moment in matrices:
        in_specs += [
            pl.BlockSpec(block, lambda *a, source=source: source(a[-1][2], *a[:-1])),
            pl.BlockSpec(block, lambda *a, source=source: source(1 - a[-1][2], *a[:-1])),
        ]
        in_specs += [pl.BlockSpec(block, lambda *a, column=column: (0, column(*a[:-1])))] * 3
        out_specs += [
            pl.BlockSpec((2 * block[0], width), lambda *a, column=column: (0, column(*a[:-1]))),
            pl.BlockSpec(block, lambda *a, column=column: (0, column(*a[:-1]))),
        ]
        rows, cols = moment.shape
        total += rows * cols
        out_shape += [
            jax.ShapeDtypeStruct((2 * rows, cols), jnp.bfloat16),
            jax.ShapeDtypeStruct((rows, cols), jnp.float32),
        ]
        operands += [gradient, gradient, base, base_other, moment]
    in_specs = [pl.BlockSpec(memory_space=pltpu.SMEM)] + in_specs
    return pl.pallas_call(
        update_kernel,
        grid_spec=pltpu.PrefetchScalarGridSpec(
            num_scalar_prefetch=1, grid=grid, in_specs=in_specs, out_specs=out_specs
        ),
        out_shape=out_shape,
        compiler_params=pltpu.CompilerParams(vmem_limit_bytes=48 * 1024 * 1024),
        cost_estimate=pl.CostEstimate(flops=8 * total, bytes_accessed=20 * total, transcendentals=0),
    )(bits, scalars, *operands)


def update_down_kernel(bits, scalars, own, other, base_own, base_other, moment, weight, new_moment):
    core = bits[2]
    clip, scale = scalars[0], scalars[1]
    gradient = own[...].astype(jnp.float32).T
    new_moment[...] = MOMENTUM_BETA * moment[...] + clip * gradient
    weight[core] = (base_own[...].astype(jnp.float32) - scale * gradient).astype(jnp.bfloat16)
    gradient = other[...].astype(jnp.float32).T
    weight[1 - core] = (base_other[...].astype(jnp.float32) - scale * gradient).astype(jnp.bfloat16)


def update_down(bits, scalars, gradient, parts, base, base_other, moment):
    rows, width = moment.shape
    cols = gradient.shape[1]
    subs = 2
    step = cols // subs
    row = pl.BlockSpec((step, width), lambda k, t, b: (k * subs + t, 0))
    weight, new_moment = pl.pallas_call(
        update_down_kernel,
        grid_spec=pltpu.PrefetchScalarGridSpec(
            num_scalar_prefetch=1,
            grid=(parts, subs),
            in_specs=[
                pl.BlockSpec(memory_space=pltpu.SMEM),
                pl.BlockSpec((width, step), lambda k, t, b: ((k * 3 + 2) * 2 + b[2], t)),
                pl.BlockSpec((width, step), lambda k, t, b: ((k * 3 + 2) * 2 + 1 - b[2], t)),
                row,
                row,
                row,
            ],
            out_specs=[pl.BlockSpec((2, step, width), lambda k, t, b: (0, k * subs + t, 0)), row],
        ),
        out_shape=[
            jax.ShapeDtypeStruct((2, rows, width), jnp.bfloat16),
            jax.ShapeDtypeStruct((rows, width), jnp.float32),
        ],
        compiler_params=pltpu.CompilerParams(vmem_limit_bytes=48 * 1024 * 1024),
        cost_estimate=pl.CostEstimate(
            flops=8 * rows * width, bytes_accessed=20 * rows * width, transcendentals=0
        ),
    )(bits, scalars, gradient, gradient, base, base_other, moment)
    return weight.reshape(2 * rows, width), new_moment


def local_fast(
    tokens,
    segments,
    cotangent,
    norm_one,
    in_weight,
    conv_weight,
    out_weight,
    norm_two,
    gate_weight,
    up_weight,
    down_weight,
    moment_norm_one,
    moment_in,
    moment_conv,
    moment_out,
    moment_norm_two,
    moment_gate,
    moment_up,
    moment_down,
    learn_rate,
    step_number,
):
    masters = (
        norm_one,
        in_weight,
        conv_weight,
        out_weight,
        norm_two,
        gate_weight,
        up_weight,
        down_weight,
    )
    moments = (
        moment_norm_one,
        moment_in,
        moment_conv,
        moment_out,
        moment_norm_two,
        moment_gate,
        moment_up,
        moment_down,
    )
    whole = (
        lax.all_gather(norm_one.astype(jnp.bfloat16), "shard", axis=0, tiled=True),
        lax.all_gather(in_weight.astype(jnp.bfloat16), "shard", axis=0, tiled=True),
        lax.all_gather(conv_weight.astype(jnp.bfloat16), "shard", axis=1, tiled=True),
        lax.all_gather(out_weight.astype(jnp.bfloat16), "shard", axis=0, tiled=True),
        lax.all_gather(norm_two.astype(jnp.bfloat16), "shard", axis=0, tiled=True),
        lax.all_gather(gate_weight.astype(jnp.bfloat16), "shard", axis=0, tiled=True),
        lax.all_gather(up_weight.astype(jnp.bfloat16), "shard", axis=0, tiled=True),
        lax.all_gather(down_weight.astype(jnp.bfloat16), "shard", axis=0, tiled=True),
    )
    gain_one = whole[0].astype(jnp.float32)
    in_matrix = whole[1]
    conv_taps = whole[2].astype(jnp.float32)
    out_matrix = whole[3]
    gain_two = whole[4].astype(jnp.float32)
    gate_matrix = whole[5]
    up_matrix = whole[6]
    down_matrix = whole[7]
    seq_count, span, model_width = tokens.shape
    row_count = seq_count * span
    x = tokens.reshape(row_count, model_width)
    e = cotangent.reshape(row_count, model_width)
    core = lax.axis_index("shard")
    group = lax.axis_index("dp")
    bits = jnp.stack([lax.rem(group, 2), lax.div(group, 2), core]).astype(jnp.int32)
    start = lax.axis_index("seq") * span
    padding = jnp.full((seq_count, 2), -1, jnp.int32)
    extended = jnp.concatenate([padding, segments, padding], 1)
    current = segment_window(extended, start, 0, span)
    masks = jnp.stack(
        [
            (segment_window(extended, start, offset, span) == current).reshape(row_count)
            for offset in (-1, -2, 1, 2)
        ],
        1,
    ).astype(jnp.float32)
    edge = from_behind(x[row_count - 16 :, :], "seq", 1)
    gain_one_row, gain_two_row = gain_one[None], gain_two[None]
    proj, convolved, hidden, n1t, zt, n2, n2t = mixer(
        x, edge, masks, gain_one_row, gain_two_row, conv_taps, in_matrix, out_matrix
    )
    et = e.T
    feed_out, feed_back, act, gate_back, up_back = feed(
        n2, e, gate_matrix, up_matrix, down_matrix, 2 * FEED_PARTS
    )
    block_out, hidden_grad, gc_grad, conv_out_grad, gain_two_grad, out_keep, out_give = out_back(
        hidden,
        convolved,
        proj,
        e,
        gain_two_row,
        out_matrix,
        zt,
        [feed_out],
        [feed_back],
        [],
    )
    after_edge = from_behind(conv_out_grad[:8, :], "seq", -1)
    proj_back, taps_grad, in_keep, in_give = conv_back(
        conv_out_grad, gc_grad, proj, masks, after_edge, conv_taps, n1t, []
    )
    input_grad, gain_one_grad = in_back(
        proj_back, in_matrix, x, hidden_grad, gain_one_row, []
    )
    rate_now = learn_rate * jnp.minimum(1.0, (step_number + 1).astype(jnp.float32) / WARMUP)
    rate = rate_now.reshape(1)
    base, base_other = {}, {}
    for place in (5, 6, 7, 1, 3):
        base[place] = base_of(rate, masters[place], moments[place], [proj_back])
        base_other[place] = over_core(base[place])
    input_grad = input_grad.reshape(tokens.shape)
    block_out = block_out.reshape(tokens.shape)
    small = jnp.concatenate(
        [gain_one_grad[:1], taps_grad[:3], gain_two_grad[:1], jnp.zeros((3, model_width))], 0
    )
    hidden_units = gate_matrix.shape[1]
    cols = hidden_units // (2 * FEED_PARTS)
    wholes, small_sum, squares = finish(
        (out_keep, out_give),
        (in_keep, in_give),
        n2t,
        et,
        gate_back,
        up_back,
        act,
        FEED_PARTS,
        small,
        [base[place] for place in (5, 6, 7, 1, 3)],
    )
    param_count = sum((member.size for member in whole))
    clip_level = CLIP_RATIO * math.sqrt(param_count)
    grad_norm = jnp.sqrt(jnp.sum(squares) + jnp.sum(small_sum * small_sum))
    clip_factor = clip_level / jnp.maximum(grad_norm, clip_level)
    scalars = jnp.stack([clip_factor, rate_now * clip_factor])
    half = model_width // 2
    narrow = cols // 2

    def feed_matrix(place, kind):
        return (
            wholes[2],
            lambda side, k, i, t: ((k * 3 + kind) * 4 + side * 2 + i, t),
            lambda k, i, t: (i * FEED_PARTS + k) * 2 + t,
            base[place],
            base_other[place],
            moments[place],
        )

    def plain_matrix(place, gradient):
        return (
            gradient,
            lambda side, t: (side, t),
            lambda t: t,
            base[place],
            base_other[place],
            moments[place],
        )

    new_weight, new_moment = {}, {}
    new_weight[3], new_moment[3] = update_rows(
        bits, scalars, (2,), (half, half), [plain_matrix(3, wholes[0])]
    )
    new_weight[5], new_moment[5], new_weight[6], new_moment[6] = update_rows(
        bits,
        scalars,
        (FEED_PARTS, 2, 2),
        (half, narrow),
        [feed_matrix(5, 0), feed_matrix(6, 1)],
    )
    new_weight[7], new_moment[7] = update_down(
        bits, scalars, wholes[2], FEED_PARTS, base[7], base_other[7], moments[7]
    )
    new_weight[1], new_moment[1] = update_rows(
        bits, scalars, (6,), (half, half), [plain_matrix(1, wholes[1])]
    )
    small_own = lax.dynamic_slice_in_dim(small_sum, core * half, half, 1)
    for place, gradient in ((0, small_own[0]), (2, small_own[1:4]), (4, small_own[4])):
        new_moment[place] = MOMENTUM_BETA * moments[place] + clip_factor * gradient
    return (
        (block_out, input_grad, grad_norm)
        + tuple(new_moment[place] for place in range(8))
        + tuple(new_weight[place] for place in (1, 3, 5, 6, 7))
    )


def local(
    tokens,
    segments,
    cotangent,
    norm_one,
    in_weight,
    conv_weight,
    out_weight,
    norm_two,
    gate_weight,
    up_weight,
    down_weight,
    moment_norm_one,
    moment_in,
    moment_conv,
    moment_out,
    moment_norm_two,
    moment_gate,
    moment_up,
    moment_down,
    learn_rate,
    step_number,
):
    masters = (
        norm_one,
        in_weight,
        conv_weight,
        out_weight,
        norm_two,
        gate_weight,
        up_weight,
        down_weight,
    )
    moments = (
        moment_norm_one,
        moment_in,
        moment_conv,
        moment_out,
        moment_norm_two,
        moment_gate,
        moment_up,
        moment_down,
    )
    whole = (
        lax.all_gather(norm_one.astype(jnp.bfloat16), "shard", axis=0, tiled=True),
        lax.all_gather(in_weight.astype(jnp.bfloat16), "shard", axis=0, tiled=True),
        lax.all_gather(conv_weight.astype(jnp.bfloat16), "shard", axis=1, tiled=True),
        lax.all_gather(out_weight.astype(jnp.bfloat16), "shard", axis=0, tiled=True),
        lax.all_gather(norm_two.astype(jnp.bfloat16), "shard", axis=0, tiled=True),
        lax.all_gather(gate_weight.astype(jnp.bfloat16), "shard", axis=0, tiled=True),
        lax.all_gather(up_weight.astype(jnp.bfloat16), "shard", axis=0, tiled=True),
        lax.all_gather(down_weight.astype(jnp.bfloat16), "shard", axis=0, tiled=True),
    )
    gain_one = whole[0].astype(jnp.float32)
    in_matrix = whole[1]
    conv_taps = whole[2].astype(jnp.float32)
    out_matrix = whole[3]
    gain_two = whole[4].astype(jnp.float32)
    gate_matrix = whole[5]
    up_matrix = whole[6]
    down_matrix = whole[7]
    seq_count, span, model_width = tokens.shape
    row_count = seq_count * span
    hidden_in = tokens.reshape(row_count, model_width).astype(jnp.float32)
    start = lax.axis_index("seq") * span
    padding = jnp.full((seq_count, 2), -1, jnp.int32)
    extended = jnp.concatenate([padding, segments, padding], 1)
    current = segment_window(extended, start, 0, span)
    keep_one = (
        (segment_window(extended, start, -1, span) == current)
        .astype(jnp.float32)
        .reshape(row_count, 1)
    )
    keep_two = (
        (segment_window(extended, start, -2, span) == current)
        .astype(jnp.float32)
        .reshape(row_count, 1)
    )
    next_one = (
        (segment_window(extended, start, 1, span) == current)
        .astype(jnp.float32)
        .reshape(row_count, 1)
    )
    next_two = (
        (segment_window(extended, start, 2, span) == current)
        .astype(jnp.float32)
        .reshape(row_count, 1)
    )
    normed_f, scale_one = norm_forward(hidden_in, gain_one)
    normed_one = normed_f.astype(jnp.bfloat16)
    projected = rows_dot(normed_one, in_matrix)
    gate_b = projected[:, :model_width]
    gate_c = projected[:, model_width : 2 * model_width]
    values = projected[:, 2 * model_width :]
    mixed_in = gate_b * values
    mixed_grid = mixed_in.reshape(seq_count, span, model_width)
    before_edge = from_behind(mixed_grid[:, span - 2 :, :], "seq", 1)
    before = jnp.concatenate([before_edge, mixed_grid], 1)
    before_one = before[:, 1:-1, :].reshape(row_count, model_width)
    before_two = before[:, :-2, :].reshape(row_count, model_width)
    convolved = (
        conv_taps[2] * mixed_in
        + conv_taps[1] * keep_one * before_one
        + conv_taps[0] * keep_two * before_two
    )
    mixer_out = (gate_c * convolved).astype(jnp.bfloat16)
    hidden = hidden_in + rows_dot(mixer_out, out_matrix)
    normed_g, scale_two = norm_forward(hidden, gain_two)
    normed_two = normed_g.astype(jnp.bfloat16)
    gate_pre = rows_dot(normed_two, gate_matrix)
    upward = rows_dot(normed_two, up_matrix)
    sigmoid_gate = jax.nn.sigmoid(gate_pre)
    activated = (gate_pre * sigmoid_gate * upward).astype(jnp.bfloat16)
    block_out = (
        (hidden + rows_dot(activated, down_matrix)).astype(jnp.bfloat16).reshape(tokens.shape)
    )
    cotangent_rows = cotangent.reshape(row_count, model_width)
    down_grad = outer_dot(activated, cotangent_rows)
    act_grad = back_dot(cotangent_rows, down_matrix)
    gate_back = (act_grad * upward * sigmoid_gate * (1.0 + gate_pre * (1.0 - sigmoid_gate))).astype(
        jnp.bfloat16
    )
    up_back = (act_grad * gate_pre * sigmoid_gate).astype(jnp.bfloat16)
    gate_grad = outer_dot(normed_two, gate_back)
    up_grad = outer_dot(normed_two, up_back)
    normed_two_grad = back_dot(gate_back, gate_matrix) + back_dot(up_back, up_matrix)
    hidden_part, gain_two_grad = norm_backward(hidden, scale_two, gain_two, normed_two_grad)
    hidden_grad = cotangent_rows.astype(jnp.float32) + hidden_part
    hidden_low = hidden_grad.astype(jnp.bfloat16)
    out_grad = outer_dot(mixer_out, hidden_low)
    mixer_grad = back_dot(hidden_low, out_matrix)
    gate_c_grad = mixer_grad * convolved
    conv_out_grad = mixer_grad * gate_c
    conv_grid = conv_out_grad.reshape(seq_count, span, model_width)
    after_edge = from_behind(conv_grid[:, :2, :], "seq", -1)
    after = jnp.concatenate([conv_grid, after_edge], 1)
    follow_one = after[:, 1:-1, :].reshape(row_count, model_width)
    follow_two = after[:, 2:, :].reshape(row_count, model_width)
    mixed_grad = (
        conv_taps[2] * conv_out_grad
        + conv_taps[1] * next_one * follow_one
        + conv_taps[0] * next_two * follow_two
    )
    conv_grad = jnp.stack(
        [
            jnp.sum(conv_out_grad * keep_two * before_two, axis=0),
            jnp.sum(conv_out_grad * keep_one * before_one, axis=0),
            jnp.sum(conv_out_grad * mixed_in, axis=0),
        ],
        0,
    )
    proj_back = jnp.concatenate([mixed_grad * values, gate_c_grad, mixed_grad * gate_b], 1).astype(
        jnp.bfloat16
    )
    in_grad = outer_dot(normed_one, proj_back)
    normed_one_grad = back_dot(proj_back, in_matrix)
    input_part, gain_one_grad = norm_backward(hidden_in, scale_one, gain_one, normed_one_grad)
    input_grad = (hidden_grad + input_part).astype(jnp.bfloat16).reshape(tokens.shape)
    shares = (
        lax.psum_scatter(gain_one_grad, "shard", scatter_dimension=0, tiled=True),
        lax.psum_scatter(in_grad, "shard", scatter_dimension=0, tiled=True),
        lax.psum_scatter(conv_grad, "shard", scatter_dimension=1, tiled=True),
        lax.psum_scatter(out_grad, "shard", scatter_dimension=0, tiled=True),
        lax.psum_scatter(gain_two_grad, "shard", scatter_dimension=0, tiled=True),
        lax.psum_scatter(gate_grad, "shard", scatter_dimension=0, tiled=True),
        lax.psum_scatter(up_grad, "shard", scatter_dimension=0, tiled=True),
        lax.psum_scatter(down_grad, "shard", scatter_dimension=0, tiled=True),
    )
    param_count = sum((member.size for member in whole))
    clip_level = CLIP_RATIO * math.sqrt(param_count)
    rate_now = learn_rate * jnp.minimum(1.0, (step_number + 1).astype(jnp.float32) / WARMUP)
    large_places = (1, 3, 5, 6, 7)
    summed = lax.psum(
        (shares[0], shares[1], shares[2], shares[3], shares[4], shares[5], shares[6], shares[7]),
        ("dp", "seq"),
    )
    squares_local = sum((jnp.sum(member * member) for member in summed))
    squares_sum = lax.psum(squares_local, "shard")
    grad_norm = jnp.sqrt(squares_sum)
    clip_factor = clip_level / jnp.maximum(grad_norm, clip_level)
    next_moments = new_moments(summed, moments, clip_factor)
    large_low = new_weights(
        tuple((masters[place] for place in large_places)),
        tuple((next_moments[place] for place in large_places)),
        rate_now,
    )
    weights = (
        lax.all_gather(large_low[0], "shard", axis=0, tiled=True),
        lax.all_gather(large_low[1], "shard", axis=0, tiled=True),
        lax.all_gather(large_low[2], "shard", axis=0, tiled=True),
        lax.all_gather(large_low[3], "shard", axis=0, tiled=True),
        lax.all_gather(large_low[4], "shard", axis=0, tiled=True),
    )
    return (
        block_out,
        input_grad,
        grad_norm,
        next_moments[0],
        next_moments[1],
        next_moments[2],
        next_moments[3],
        next_moments[4],
        next_moments[5],
        next_moments[6],
        next_moments[7],
        weights[0],
        weights[1],
        weights[2],
        weights[3],
        weights[4],
    )


def solution(mesh):
    placed = (
        P(("dp", "shard"), "seq", None),
        P(("dp", "shard"), None),
        P(("dp", "shard"), "seq", None),
        P("shard"),
        P("shard", None),
        P(None, "shard"),
        P("shard", None),
        P("shard"),
        P("shard", None),
        P("shard", None),
        P("shard", None),
        P("shard"),
        P("shard", None),
        P(None, "shard"),
        P("shard", None),
        P("shard"),
        P("shard", None),
        P("shard", None),
        P("shard", None),
        P(),
        P(),
    )
    sizes = (mesh.shape["dp"], mesh.shape["seq"], mesh.shape["shard"])
    return jax.shard_map(
        local_fast if sizes == (4, 4, 2) else local,
        mesh=mesh,
        in_specs=placed,
        out_specs=(
            P(("dp", "shard"), "seq", None),
            P(("dp", "shard"), "seq", None),
            P(),
            P("shard"),
            P("shard", None),
            P(None, "shard"),
            P("shard", None),
            P("shard"),
            P("shard", None),
            P("shard", None),
            P("shard", None),
            P(),
            P(),
            P(),
            P(),
            P(),
        ),
        check_vma=False,
    )
```

```python
import functools
import math

import jax
import jax.numpy as jnp
from jax import lax
from jax.experimental import pallas as pl
from jax.experimental.pallas import tpu as pltpu
from jax.sharding import PartitionSpec as P

WARMUP = 2000


EPSILON = 1e-05
MOMENTUM_BETA = 0.9
WEIGHT_DECAY = 0.1
CLIP_RATIO = 0.25

FEED_PARTS = 3


def from_behind(block, axis, distance):
    devices = range(lax.axis_size(axis))
    route = [(i - distance, i) for i in devices if i - distance in devices]
    return lax.ppermute(block, axis, route)


def rows_dot(left, right):
    return jnp.dot(left, right, preferred_element_type=jnp.float32)


def outer_dot(left, right):
    return lax.dot_general(
        left, right, (((0,), (0,)), ((), ())), preferred_element_type=jnp.float32
    )


def back_dot(left, right):
    return lax.dot_general(
        left, right, (((1,), (1,)), ((), ())), preferred_element_type=jnp.float32
    )


def norm_forward(values, gain):
    scale = lax.rsqrt(jnp.mean(values * values, axis=-1, keepdims=True) + EPSILON)
    return (values * scale * gain, scale)


def norm_backward(values, scale, gain, upstream):
    gain_grad = jnp.sum(upstream * values * scale, axis=0)
    inner = jnp.mean(values * gain * upstream, axis=-1, keepdims=True)
    return (scale * gain * upstream - values * scale * scale * scale * inner, gain_grad)


def segment_window(extended, start, offset, length):
    return lax.dynamic_slice_in_dim(extended, start + 2 + offset, length, 1)


def new_moments(gradients, moments, clip_factor):
    return tuple(
        (
            MOMENTUM_BETA * moment + clip_factor * gradient
            for moment, gradient in zip(moments, gradients)
        )
    )


def new_weights(masters, next_moments, rate_now):
    return tuple(
        (
            (master * (1.0 - rate_now * WEIGHT_DECAY) - rate_now * moment).astype(jnp.bfloat16)
            for master, moment in zip(masters, next_moments)
        )
    )


MESH = pl.DeviceIdType.MESH
ANY = pl.BlockSpec(memory_space=pl.ANY)
INTO_VMEM = pl.BlockSpec(memory_space=pltpu.VMEM)
ROWS_DOT = (((1,), (0,)), ((), ()))
BACK_DOT = (((1,), (1,)), ((), ()))
KEEP_SLOTS, GOT_SLOTS, GIVE_SLOTS = 5, 3, 2


def kernel_dot(left, right, dims=ROWS_DOT):
    return lax.dot_general(left, right, dims, preferred_element_type=jnp.float32)


def finish_kernel(chunks, parts, wholes_count, unused, *refs):
    count = len(chunks)
    out_keep, out_give, in_keep, in_give = refs[:4]
    n2t, et, gate_back, up_back, act, small = refs[4:10]
    refs = refs[10 + unused :]
    whole_refs = refs[:wholes_count]
    small_out, square_out = refs[wholes_count : wholes_count + 2]
    rest = refs[wholes_count + 2 :]
    plain = sum(1 for chunk in chunks if chunk[0] != "feed")
    plain_keep, plain_got = rest[:plain], rest[plain : 2 * plain]
    rest = rest[2 * plain :]
    keep_ring, got_ring, give_ring, tiles = rest[:4]
    rest = rest[4:]
    first_in = rest[:count]
    pieces = rest[count : 2 * count]
    done = rest[2 * count : 3 * count]
    from_mid = rest[3 * count : 4 * count]
    small_in, square_in = rest[4 * count : 4 * count + 2]
    (
        send,
        recv,
        small_send,
        small_recv,
        square_send,
        square_recv,
        own_sem,
        load_sem,
        tile_sem,
        credit,
    ) = rest[4 * count + 2 :]

    group = lax.axis_index("dp")
    place = lax.axis_index("seq")
    core = lax.axis_index("shard")
    x_bit = lax.rem(group, 2)
    y_bit = lax.div(group, 2)
    over_x = (group + 1 - 2 * x_bit, place, core)
    over_y = (group + 2 - 4 * y_bit, place, core)
    sibling = (group, place, 1 - core)
    z_near = (group, place + 1 - 2 * lax.rem(place, 2), core)
    z_far = (group, 3 - place, core)
    is_mid = jnp.logical_or(place == 1, place == 2)
    is_end = jnp.logical_not(is_mid)
    first_dev, second_dev = (over_x, over_y), (over_y, over_x)
    first_bit, second_bit = (x_bit, y_bit), (y_bit, x_bit)

    barrier = pltpu.get_barrier_semaphore()
    for device in (over_x, over_y, sibling, z_near, z_far):
        pl.semaphore_signal(barrier, inc=1, device_id=device, device_id_type=MESH)
    pl.semaphore_wait(barrier, 5)

    def unit_of(c):
        return chunks[c][2] // 8

    def feed_index(c):
        return c - plain

    def is_feed(c):
        return chunks[c][0] == "feed"

    def keep_of(c):
        return keep_ring.at[feed_index(c) % KEEP_SLOTS] if is_feed(c) else plain_keep[c]

    def got_of(c):
        return got_ring.at[feed_index(c) % GOT_SLOTS] if is_feed(c) else plain_got[c]

    def remote(source, target, c, k, device):
        return pltpu.make_async_remote_copy(
            src_ref=source,
            dst_ref=target,
            send_sem=send.at[c, k],
            recv_sem=recv.at[c, k],
            device_id=device,
            device_id_type=MESH,
        )

    def aligned(start, size):
        return pl.ds(pl.multiple_of(start, 16), size)

    def rows_of(c, h, first, second, owner):
        unit = unit_of(c)
        _, _, _, _, base, stride = chunks[c][:6]
        return aligned(base + owner * stride + ((h * 2 + first) * 2 + second) * unit, unit)

    def local_rows(c, h, first, second=None):
        unit = unit_of(c)
        if second is None:
            return aligned((h * 2 + first) * 2 * unit, 2 * unit)
        return aligned(((h * 2 + first) * 2 + second) * unit, unit)

    def whole_of(c):
        return whole_refs[chunks[c][3 + 0]]

    def mine(c, h):
        unit = unit_of(c)
        return done[c].at[pl.ds(h * unit, unit)]

    def add_into(target, target_row, one, one_row, two, two_row, rows):
        def body(i, carry):
            at = lambda start: aligned(start + i * 16, 16)
            total = one[at(one_row), :].astype(jnp.float32) + two[at(two_row), :].astype(
                jnp.float32
            )
            target[at(target_row), :] = total.astype(jnp.bfloat16)
            return carry

        lax.fori_loop(0, rows // 16, body, 0)

    def add_squares(c):
        width = chunks[c][7]

        def body(i, total):
            block = done[c][aligned(i * 16, 16), :].astype(jnp.float32)
            block = block * block
            block = block[:8] + block[8:]
            for j in range(width // 128):
                total = total + block[:, j * 128 : (j + 1) * 128]
            return total

        square_out[...] += lax.fori_loop(
            0, 2 * unit_of(c) // 16, body, jnp.zeros((8, 128), jnp.float32)
        )

    def over_core(c):
        if is_feed(c):
            return remote(give_ring.at[feed_index(c) % GIVE_SLOTS], got_of(c), c, 0, sibling)
        name, start, rows = chunks[c][0], chunks[c][6], chunks[c][2]
        source = out_give if name == "out" else in_give
        return remote(source.at[pl.ds(start, rows)], got_of(c), c, 0, sibling)

    def load_keep(c):
        name, start, rows = chunks[c][0], chunks[c][6], chunks[c][2]
        source = out_keep if name == "out" else in_keep
        return pltpu.make_async_copy(source.at[pl.ds(start, rows)], plain_keep[c], load_sem.at[c])

    def over_first(c, h):
        unit = unit_of(c)
        source = keep_of(c).at[local_rows(c, h, 1 - first_bit[h])]
        return remote(source, first_in[c].at[pl.ds(h * 2 * unit, 2 * unit)], c, 1 + h, first_dev[h])

    def over_second(c, h):
        unit = unit_of(c)
        source = keep_of(c).at[local_rows(c, h, first_bit[h], 1 - second_bit[h])]
        return remote(source, pieces[c].at[pl.ds(h * unit, unit)], c, 3 + h, second_dev[h])

    def z_in(c):
        return remote(pieces[c], done[c], c, 5, z_near)

    def z_mid(c):
        return remote(done[c], from_mid[c], c, 6, z_far)

    def z_out(c):
        return remote(done[c], done[c], c, 7, z_near)

    def to_second(c, h):
        rows = rows_of(c, h, first_bit[h], second_bit[h], core)
        return remote(mine(c, h), whole_of(c).at[rows], c, 8 + h, second_dev[h])

    def to_first(c, h):
        rows = rows_of(c, h, first_bit[h], second_bit[h], core)
        return remote(mine(c, h), whole_of(c).at[rows], c, 10 + h, first_dev[h])

    def pass_first(c, h):
        rows = rows_of(c, h, first_bit[h], 1 - second_bit[h], core)
        return remote(whole_of(c).at[rows], whole_of(c).at[rows], c, 12 + h, first_dev[h])

    def to_sibling(c, h, kind):
        first = first_bit[h] if kind < 2 else 1 - first_bit[h]
        second = second_bit[h] if kind % 2 == 0 else 1 - second_bit[h]
        rows = rows_of(c, h, first, second, core)
        source = mine(c, h) if kind == 0 else whole_of(c).at[rows]
        return remote(source, whole_of(c).at[rows], c, 14 + 2 * kind + h, sibling)

    def own_copy(c, h):
        rows = rows_of(c, h, first_bit[h], second_bit[h], core)
        return pltpu.make_async_copy(mine(c, h), whole_of(c).at[rows], own_sem.at[c, h])

    def load_tile(c, half):
        part, kind = chunks[c][1]
        cols = tiles.shape[2]
        source = (gate_back, up_back, act)[kind]
        return pltpu.make_async_copy(
            source.at[:, pl.ds((half * parts + part) * cols, cols)], tiles.at[half], tile_sem.at[half]
        )

    def produce(c):
        if not is_feed(c):
            over_core(c).start()
            load_keep(c).start()
            return
        index = feed_index(c)
        kind = chunks[c][1][1]
        keep, give = keep_of(c), give_ring.at[index % GIVE_SLOTS]
        rows = n2t.shape[0] // 2
        for half in range(2):
            load_tile(c, half).wait()

        @pl.loop(0, 2)
        def _(r):
            target = aligned(r * rows, rows)
            for ref, side in ((keep, core), (give, 1 - core)):
                if kind < 2:
                    block = kernel_dot(n2t[aligned(side * rows, rows), :], tiles[r])
                else:
                    block = kernel_dot(et[target, :], tiles[side])
                ref[target, :] = block.astype(jnp.bfloat16)

        if c + 1 < count:
            for half in range(2):
                load_tile(c + 1, half).start()
        if index >= GOT_SLOTS:
            pl.semaphore_wait(credit, 1)
        over_core(c).start()

    def sum_core(c):
        if not is_feed(c):
            load_keep(c).wait()
        over_core(c).wait()
        add_into(keep_of(c), 0, keep_of(c), 0, got_of(c), 0, chunks[c][2])
        if is_feed(c) and c + GOT_SLOTS < count:
            pl.semaphore_signal(credit, inc=1, device_id=sibling, device_id_type=MESH)
        for h in range(2):
            over_first(c, h).start()

    def sum_first(c):
        unit = unit_of(c)
        for h in range(2):
            over_first(c, h).wait()
            row = (h * 2 + first_bit[h]) * 2 * unit
            add_into(keep_of(c), row, keep_of(c), row, first_in[c], h * 2 * unit, 2 * unit)
            over_second(c, h).start()

    def sum_second(c):
        unit = unit_of(c)
        for h in range(2):
            over_second(c, h).wait()
            row = ((h * 2 + first_bit[h]) * 2 + second_bit[h]) * unit
            add_into(pieces[c], h * unit, pieces[c], h * unit, keep_of(c), row, unit)

        @pl.when(is_end)
        def _():
            z_in(c).start()

    def sum_end(c):
        @pl.when(is_mid)
        def _():
            z_in(c).wait_recv()
            add_into(done[c], 0, pieces[c], 0, done[c], 0, 2 * unit_of(c))
            z_mid(c).start()

    def sum_middle(c):
        @pl.when(is_mid)
        def _():
            z_mid(c).wait()
            add_into(done[c], 0, done[c], 0, from_mid[c], 0, 2 * unit_of(c))
            z_out(c).start()

        @pl.when(is_end)
        def _():
            z_in(c).wait_send()
            z_out(c).wait_recv()

        for h in range(2):
            to_second(c, h).start()
            to_first(c, h).start()
            to_sibling(c, h, 0).start()
            own_copy(c, h).start()
        add_squares(c)

    def forward(c):
        for h in range(2):
            to_second(c, h).wait_recv()
            pass_first(c, h).start()
            to_sibling(c, h, 1).start()

    def last_hop(c):
        for h in range(2):
            to_first(c, h).wait_recv()
            to_sibling(c, h, 2).start()
            pass_first(c, h).wait_recv()
            to_sibling(c, h, 3).start()

    def drain(c):
        @pl.when(is_mid)
        def _():
            z_out(c).wait_send()

        for h in range(2):
            to_second(c, h).wait_send()
            to_first(c, h).wait_send()
            pass_first(c, h).wait_send()
            own_copy(c, h).wait()
            for kind in range(4):
                to_sibling(c, h, kind).wait()

    small_route = (sibling, over_x, over_y, z_near, z_far)

    def small_copy(k):
        return pltpu.make_async_remote_copy(
            src_ref=small_out,
            dst_ref=small_in.at[k],
            send_sem=small_send.at[k],
            recv_sem=small_recv.at[k],
            device_id=small_route[k],
            device_id_type=MESH,
        )

    def square_copy(k):
        return pltpu.make_async_remote_copy(
            src_ref=square_out,
            dst_ref=square_in.at[k],
            send_sem=square_send.at[k],
            recv_sem=square_recv.at[k],
            device_id=small_route[k],
            device_id_type=MESH,
        )

    small_out[...] = small[...]
    square_out[...] = jnp.zeros_like(square_out)
    for half in range(2):
        load_tile(plain, half).start()
    small_copy(0).start()

    def at(step, action):
        if 0 <= step < count:
            action(step)

    squares_from = count + 3
    for t in range(count + 7):
        at(t, produce)
        if t < 5:
            small_copy(t).wait()
            small_out[...] += small_in[t]
            if t < 4:
                small_copy(t + 1).start()
        at(t - 1, sum_first)
        at(t - 2, sum_second)
        at(t - 3, sum_middle)
        if squares_from <= t < squares_from + 4:
            k = t - squares_from
            if k >= 1:
                square_copy(k - 1).wait()
                square_out[...] += square_in[k - 1]
            if k < 3:
                square_copy(k).start()
        at(t - 5, last_hop)
        at(t, sum_core)
        at(t - 2, sum_end)
        at(t - 4, forward)
    for c in range(count):
        drain(c)


def finish(out_sides, in_sides, n2t, et, gate_back, up_back, act, parts, small, order):
    width = n2t.shape[0]
    half = width // 2
    cols = gate_back.shape[1] // (2 * parts)
    in_cols = in_sides[0].shape[1]
    chunks = [("out", None, half, 0, 0, half, 0, width)]
    chunks += [("in", None, half // 2, 1, t * half // 2, half, t * half // 2, in_cols) for t in range(2)]
    for part in range(parts):
        for kind in range(3):
            first = (part * 3 + kind) * 2 * width
            chunks.append(("feed", (part, kind), width, 2, first, width, 0, cols))
    count, plain = len(chunks), 3
    low = jnp.bfloat16
    semaphore = pltpu.SemaphoreType.DMA
    wholes = [(width, width), (width, in_cols), (parts * 3 * 2 * width, cols)]
    eighths = [(chunk[2] // 8, chunk[7]) for chunk in chunks]
    plain_shapes = [(chunk[2], chunk[7]) for chunk in chunks[:plain]]
    pair = [pltpu.VMEM((2 * rows, c), low) for rows, c in eighths]
    outs = pl.pallas_call(
        functools.partial(finish_kernel, tuple(chunks), parts, len(wholes), len(order)),
        out_shape=[jax.ShapeDtypeStruct(shape, low) for shape in wholes]
        + [
            jax.ShapeDtypeStruct((8, small.shape[1]), jnp.float32),
            jax.ShapeDtypeStruct((8, 128), jnp.float32),
        ],
        in_specs=[ANY] * 4 + [INTO_VMEM] * 2 + [ANY] * 3 + [INTO_VMEM] + [ANY] * len(order),
        out_specs=[ANY] * len(wholes) + [INTO_VMEM] * 2,
        scratch_shapes=[pltpu.VMEM(shape, low) for shape in plain_shapes] * 2
        + [
            pltpu.VMEM((KEEP_SLOTS, width, cols), low),
            pltpu.VMEM((GOT_SLOTS, width, cols), low),
            pltpu.VMEM((GIVE_SLOTS, width, cols), low),
            pltpu.VMEM((2, act.shape[0], cols), low),
        ]
        + [pltpu.VMEM((4 * rows, c), low) for rows, c in eighths]
        + pair * 3
        + [
            pltpu.VMEM((5, 8, small.shape[1]), jnp.float32),
            pltpu.VMEM((3, 8, 128), jnp.float32),
            semaphore((count, 22)),
            semaphore((count, 22)),
            semaphore((5,)),
            semaphore((5,)),
            semaphore((3,)),
            semaphore((3,)),
            semaphore((count, 2)),
            semaphore((plain,)),
            semaphore((2,)),
            pltpu.SemaphoreType.REGULAR,
        ],
        compiler_params=pltpu.CompilerParams(
            collective_id=0, has_side_effects=True, vmem_limit_bytes=62 * 1024 * 1024
        ),
    )(*out_sides, *in_sides, n2t, et, gate_back, up_back, act, small, *order)
    return outs[: len(wholes)], outs[-2], outs[-1]


def feed_kernel(step, n2, e, wg, wu, wd, out, back, act, gate_back, up_back, et):
    @pl.when(pl.program_id(0) == 0)
    def _():
        et[...] = e[...].T
        out[...] = jnp.zeros_like(out)
        back[...] = jnp.zeros_like(back)

    @pl.loop(0, n2.shape[0] // step)
    def _(t):
        rows = pl.ds(pl.multiple_of(t * step, step), step)
        gate = kernel_dot(n2[rows, :], wg[...])
        up = kernel_dot(n2[rows, :], wu[...])
        grad = kernel_dot(e[rows, :], wd[...], BACK_DOT)
        sigmoid = 0.5 * jnp.tanh(0.5 * gate) + 0.5
        silu = gate * sigmoid
        low_act = (silu * up).astype(jnp.bfloat16)
        low_up = (grad * silu).astype(jnp.bfloat16)
        low_gate = (grad * up * (sigmoid + silu * (1.0 - sigmoid))).astype(jnp.bfloat16)
        act[rows, :] = low_act
        gate_back[rows, :] = low_gate
        up_back[rows, :] = low_up
        out[rows, :] += kernel_dot(low_act, wd[...])
        back[rows, :] += kernel_dot(low_gate, wg[...], BACK_DOT) + kernel_dot(
            low_up, wu[...], BACK_DOT
        )


def feed(n2, e, gate_matrix, up_matrix, down_matrix, tiles):
    rows, width = n2.shape
    assert rows == width
    cols = gate_matrix.shape[1] // tiles
    whole = pl.BlockSpec((rows, width), lambda i: (0, 0), pipeline_mode=pl.Buffered(1))
    tile = pl.BlockSpec((rows, cols), lambda i: (0, i))
    return pl.pallas_call(
        functools.partial(feed_kernel, rows // 2),
        grid=(tiles,),
        in_specs=[whole, whole]
        + [pl.BlockSpec((width, cols), lambda i: (0, i))] * 2
        + [pl.BlockSpec((cols, width), lambda i: (i, 0))],
        out_specs=[whole, whole, tile, tile, tile, whole],
        out_shape=[jax.ShapeDtypeStruct((rows, width), jnp.float32)] * 2
        + [jax.ShapeDtypeStruct((rows, tiles * cols), jnp.bfloat16)] * 3
        + [jax.ShapeDtypeStruct((width, rows), jnp.bfloat16)],
        cost_estimate=pl.CostEstimate(
            flops=12 * rows * width * cols * tiles,
            bytes_accessed=70 * 1024 * 1024,
            transcendentals=rows * cols * tiles,
        ),
        compiler_params=pltpu.CompilerParams(vmem_limit_bytes=56 * 1024 * 1024),
    )(n2, e, gate_matrix, up_matrix, down_matrix)


CORE_ROUTE = ((0, 1), (1, 0))


def over_core(give):
    return lax.ppermute(give, "shard", CORE_ROUTE)


def scale_of(values):
    return lax.rsqrt(jnp.mean(values * values, axis=-1, keepdims=True) + EPSILON)


def shifted(values, edge, distance):
    rows = values.shape[0]
    moved = pltpu.roll(values, (-distance) % rows, 0)
    index = lax.broadcasted_iota(jnp.int32, values.shape, 0)
    if distance < 0:
        for row in range(-distance):
            moved = jnp.where(index == row, edge[8 + distance + row : 9 + distance + row, :], moved)
    else:
        for row in range(distance):
            moved = jnp.where(index == rows - distance + row, edge[row : row + 1, :], moved)
    return moved


STEPS = 4


def mixer_kernel(
    x_ref,
    x_all,
    masks,
    pack,
    in_master,
    out_master,
    gate_master,
    up_master,
    down_master,
    proj,
    conv,
    hid,
    n1t,
    zt,
    n2,
    n2t,
    gains,
    in_whole,
    out_whole,
    gate_whole,
    up_whole,
    down_whole,
    carry,
    edge,
    pack_in,
    w_in,
    w_out,
    in_stage,
    out_stage,
    gate_stage,
    up_stage,
    down_stage,
    gate_low,
    up_low,
    down_low,
    load_sem,
    send,
    recv,
    keep_sem,
    part_load,
    part_send,
    part_recv,
    part_keep,
):
    width = x_ref.shape[1]
    half = width // 2
    low = jnp.bfloat16
    step = pl.program_id(0)
    group = lax.axis_index("dp")
    place = lax.axis_index("seq")
    core = lax.axis_index("shard")
    places = lax.axis_size("seq")
    sibling = (group, place, 1 - core)
    after = (group, lax.rem(place + 1, places), core)
    before = (group, lax.rem(place + places - 1, places), core)

    def remote(source, target, k, device):
        return pltpu.make_async_remote_copy(
            src_ref=source,
            dst_ref=target,
            send_sem=send.at[k],
            recv_sem=recv.at[k],
            device_id=device,
            device_id_type=MESH,
        )

    def own_rows(rows, start=0, count=None):
        return pl.ds(pl.multiple_of(core * rows + start, 16), rows if count is None else count)

    def cast(target, target_row, source, source_row, rows):
        block = 16

        def body(i, carry_):
            put = pl.ds(pl.multiple_of(target_row + i * block, block), block)
            get = pl.ds(pl.multiple_of(source_row + i * block, block), block)
            target[put, :] = source[get, :].astype(low)
            return carry_

        lax.fori_loop(0, rows // block, body, 0)

    stages = (gate_stage, up_stage, down_stage)
    masters = (gate_master, up_master, down_master)
    wholes = (gate_whole, up_whole, down_whole)
    lows = (gate_low, up_low, down_low)

    def part_in(m, i):
        rows = stages[m].shape[0]
        return pltpu.make_async_copy(
            masters[m].at[pl.ds(pl.multiple_of(i * rows, 16), rows)], stages[m], part_load.at[m]
        )

    def part_rows(m, i):
        rows = stages[m].shape[0]
        return pl.ds(pl.multiple_of(core * (STEPS * rows) + i * rows, 16), rows)

    def part_out(m, i):
        slot = lax.rem(i, 2)
        return pltpu.make_async_remote_copy(
            src_ref=lows[m].at[slot],
            dst_ref=wholes[m].at[part_rows(m, i)],
            send_sem=part_send.at[i, m],
            recv_sem=part_recv.at[i, m],
            device_id=sibling,
            device_id_type=MESH,
        )

    def part_own(m, i):
        slot = lax.rem(i, 2)
        return pltpu.make_async_copy(
            lows[m].at[slot], wholes[m].at[part_rows(m, i)], part_keep.at[i, m]
        )

    quarter = half // 2
    copies = []
    for k in range(2):
        rows = own_rows(half, k * quarter, quarter)
        copies.append(remote(w_in.at[rows], w_in.at[rows], k, sibling))
    rows = own_rows(half)
    copies.append(remote(w_out.at[rows], w_out.at[rows], 2, sibling))
    copies.append(remote(pack, pack_in, 3, sibling))
    to_after = remote(x_all.at[pl.ds(x_all.shape[0] - 16, 16)], edge, 4, after)
    in_loads = [
        pltpu.make_async_copy(
            in_master.at[pl.ds(k * quarter, quarter)],
            in_stage.at[pl.ds(k * quarter, quarter)],
            load_sem.at[k],
        )
        for k in range(2)
    ]
    out_load = pltpu.make_async_copy(out_master, out_stage, load_sem.at[2])
    keeps = [
        pltpu.make_async_copy(w_in, in_whole, keep_sem.at[0]),
        pltpu.make_async_copy(w_out, out_whole, keep_sem.at[1]),
    ]

    def project(values, first, count=1):
        return kernel_dot(values, w_in[:, first * width : (first + count) * width])

    def normed(values):
        return (values * scale_of(values) * gains[0:1, :]).astype(low)

    @pl.when(step == 0)
    def _():
        for load in (*in_loads, out_load):
            load.start()
        for m in range(3):
            part_in(m, 0).start()
        barrier = pltpu.get_barrier_semaphore()
        for device in (sibling, after, before):
            pl.semaphore_signal(barrier, inc=1, device_id=device, device_id_type=MESH)
        pl.semaphore_wait(barrier, 3)
        copies[3].start()

        @pl.when(place < places - 1)
        def _():
            to_after.start()

        for k in range(2):
            in_loads[k].wait()
            cast(w_in, core * half + k * quarter, in_stage, k * quarter, quarter)
            copies[k].start()
        out_load.wait()
        cast(w_out, core * half, out_stage, 0, half)
        copies[2].start()

        @pl.when(place == 0)
        def _():
            edge[...] = jnp.zeros_like(edge)

        @pl.when(place > 0)
        def _():
            to_after.wait_recv()

        @pl.when(place < places - 1)
        def _():
            to_after.wait_send()

        for copy in copies:
            copy.wait()
        gains[:, pl.ds(pl.multiple_of(core * half, half), half)] = pack[...]
        gains[:, pl.ds(pl.multiple_of((1 - core) * half, half), half)] = pack_in[...]
        for copy in keeps:
            copy.start()
        rows = normed(edge[...].astype(jnp.float32))
        mixed = project(rows, 0) * project(rows, 2)
        carry[...] = mixed[8:, :]

    @pl.when(step > 0)
    def _():
        i = step - 1

        @pl.when(i >= 2)
        def _():
            for m in range(3):
                part_out(m, i - 2).wait_send()
                part_own(m, i - 2).wait()

        for m in range(3):
            part_in(m, i).wait()
            cast(lows[m].at[lax.rem(i, 2)], 0, stages[m], 0, stages[m].shape[0])
            part_out(m, i).start()
            part_own(m, i).start()

        @pl.when(i + 1 < STEPS)
        def _():
            for m in range(3):
                part_in(m, i + 1).start()

        x = x_ref[...].astype(jnp.float32)
        first = normed(x)
        n1t[...] = first.T
        gate_b, gate_c, values = project(first, 0), project(first, 1), project(first, 2)
        proj[:, :width] = gate_b
        proj[:, width : 2 * width] = gate_c
        proj[:, 2 * width :] = values
        mixed = gate_b * values
        beside = carry[...]
        convolved = (
            gains[4:5, :] * mixed
            + gains[3:4, :] * masks[:, 0:1] * shifted(mixed, beside, -1)
            + gains[2:3, :] * masks[:, 1:2] * shifted(mixed, beside, -2)
        )
        carry[...] = mixed[mixed.shape[0] - 8 :, :]
        conv[...] = convolved
        mixer_out = (gate_c * convolved).astype(low)
        zt[...] = mixer_out.T
        hidden = x + kernel_dot(mixer_out, w_out[...])
        hid[...] = hidden
        second = (hidden * scale_of(hidden) * gains[1:2, :]).astype(low)
        n2[...] = second
        n2t[...] = second.T

    @pl.when(step == STEPS)
    def _():
        for copy in keeps:
            copy.wait()
        for i in range(STEPS):
            for m in range(3):
                if i >= STEPS - 2:
                    part_out(m, i).wait_send()
                    part_own(m, i).wait()
                part_out(m, i).wait_recv()


def resident(shape):
    return pl.BlockSpec(shape, lambda i: (0,) * len(shape), pipeline_mode=pl.Buffered(1))


def mixer(x, masks, pack, masters):
    rows, width = x.shape
    step = rows // STEPS
    at = lambda i: jnp.maximum(i - 1, 0)
    tile = lambda cols: pl.BlockSpec((step, cols), lambda i: (at(i), 0))
    turned = pl.BlockSpec((width, step), lambda i: (0, at(i)))
    low, full = jnp.bfloat16, jnp.float32
    shape = jax.ShapeDtypeStruct
    in_master, out_master = masters[:2]
    large = masters[2:]
    whole = [shape((2 * m.shape[0], m.shape[1]), low) for m in masters]
    parts = [(m.shape[0] // STEPS, m.shape[1]) for m in large]
    semaphore = pltpu.SemaphoreType.DMA
    return pl.pallas_call(
        mixer_kernel,
        grid=(STEPS + 1,),
        in_specs=[tile(width), ANY, tile(masks.shape[1]), resident(pack.shape)] + [ANY] * 5,
        out_specs=[tile(3 * width), tile(width), tile(width), turned, turned, tile(width), turned]
        + [resident((8, width))]
        + [ANY] * 5,
        out_shape=[
            shape((rows, 3 * width), full),
            shape((rows, width), full),
            shape((rows, width), full),
            shape((width, rows), low),
            shape((width, rows), low),
            shape((rows, width), low),
            shape((width, rows), low),
            shape((8, width), full),
        ]
        + whole,
        scratch_shapes=[
            pltpu.VMEM((8, width), full),
            pltpu.VMEM((16, width), low),
            pltpu.VMEM(pack.shape, full),
            pltpu.VMEM(whole[0].shape, low),
            pltpu.VMEM(whole[1].shape, low),
            pltpu.VMEM(in_master.shape, full),
            pltpu.VMEM(out_master.shape, full),
        ]
        + [pltpu.VMEM(part, full) for part in parts]
        + [pltpu.VMEM((2, *part), low) for part in parts]
        + [
            semaphore((3,)),
            semaphore((5,)),
            semaphore((5,)),
            semaphore((2,)),
            semaphore((3,)),
            semaphore((STEPS, 3)),
            semaphore((STEPS, 3)),
            semaphore((STEPS, 3)),
        ],
        compiler_params=pltpu.CompilerParams(
            collective_id=1, has_side_effects=True, vmem_limit_bytes=60 * 1024 * 1024
        ),
    )(x, x, masks, pack, *masters)


def out_back_kernel(parts, *refs):
    h_ref, c_ref, gc_ref, e_ref, gain_two, w_out, zt = refs[:7]
    outs, backs = refs[7 : 7 + parts], refs[7 + parts : 7 + 2 * parts]
    block_out, hidden_grad, gc_grad, conv_grad, gain_grad, keep, give, total = refs[-8:]
    step = pl.program_id(0)
    core = lax.axis_index("shard")
    hidden = h_ref[...]
    gain = gain_two[...]
    summed = hidden
    for ref in outs:
        summed = summed + ref[...]
    block_out[...] = summed.astype(jnp.bfloat16)
    upstream = backs[0][...]
    for ref in backs[1:]:
        upstream = upstream + ref[...]
    scale = scale_of(hidden)
    inner = jnp.mean(hidden * gain * upstream, axis=-1, keepdims=True)
    grad = (
        e_ref[...].astype(jnp.float32)
        + scale * gain * upstream
        - hidden * (scale * scale * scale * inner)
    )
    hidden_grad[...] = grad
    low = grad.astype(jnp.bfloat16)
    share = jnp.sum(upstream * hidden * scale, axis=0, keepdims=True)
    mixer_grad = kernel_dot(low, w_out[...], BACK_DOT)
    gc_grad[...] = (mixer_grad * c_ref[...]).astype(jnp.bfloat16)
    conv_grad[...] = mixer_grad * gc_ref[...]

    @pl.when(step == 0)
    def _():
        total[...] = jnp.zeros_like(total)
        gain_grad[...] = jnp.zeros_like(gain_grad)

    gain_grad[0:1, :] += share
    total[...] += kernel_dot(zt[...], low)

    @pl.when(step == pl.num_programs(0) - 1)
    def _():
        rows = total.shape[0] // 2
        for target, side in ((keep, core), (give, 1 - core)):
            target[...] = total[pl.ds(pl.multiple_of(side * rows, rows), rows), :].astype(
                jnp.bfloat16
            )


def skip_last(kernel, inputs, extra):
    def wrapped(*refs):
        return kernel(*refs[:inputs], *refs[inputs + extra :])

    return wrapped


def out_back(hidden, convolved, proj, e, gain_two, w_out, zt, outs, backs, order):
    rows, width = hidden.shape
    step = rows // 4
    tile = pl.BlockSpec((step, width), lambda i: (i, 0))
    low, full = jnp.bfloat16, jnp.float32
    shape = jax.ShapeDtypeStruct
    inputs = 7 + len(outs) + len(backs)
    return pl.pallas_call(
        skip_last(functools.partial(out_back_kernel, len(outs)), inputs, len(order)),
        grid=(4,),
        in_specs=[
            tile,
            tile,
            pl.BlockSpec((step, width), lambda i: (i, 1)),
            tile,
            resident(gain_two.shape),
            resident(w_out.shape),
            pl.BlockSpec((width, step), lambda i: (0, i)),
        ]
        + [tile] * (len(outs) + len(backs))
        + [ANY] * len(order),
        out_specs=[tile] * 4 + [resident((8, width))] + [resident((width // 2, width))] * 2,
        out_shape=[
            shape((rows, width), low),
            shape((rows, width), full),
            shape((rows, width), low),
            shape((rows, width), full),
            shape((8, width), full),
            shape((width // 2, width), low),
            shape((width // 2, width), low),
        ],
        scratch_shapes=[pltpu.VMEM((width, width), full)],
        compiler_params=pltpu.CompilerParams(vmem_limit_bytes=56 * 1024 * 1024),
        cost_estimate=pl.CostEstimate(
            flops=4 * rows * width * width, bytes_accessed=48 * rows * width, transcendentals=0
        ),
    )(hidden, convolved, proj, e, gain_two, w_out, zt, *outs, *backs, *order)


def conv_back_kernel(
    dc_ref, dgc, gb_ref, v_ref, masks, edge_ref, taps, n1t, dp_ref, taps_grad, keep, give, carry, all_dp
):
    step = pl.program_id(0)
    last = pl.num_programs(0) - 1
    core = lax.axis_index("shard")
    rows, width = dc_ref.shape
    low = jnp.bfloat16

    @pl.when(step == 0)
    def _():
        carry[...] = edge_ref[...]
        taps_grad[...] = jnp.zeros_like(taps_grad)

    grad = dc_ref[...]
    edge = carry[...]
    next_one = masks[:, 2:3] * shifted(grad, edge, 1)
    next_two = masks[:, 3:4] * shifted(grad, edge, 2)
    carry[...] = grad[:8, :]
    gate_b, values = gb_ref[...], v_ref[...]
    mixed = gate_b * values
    for row, term in ((0, next_two), (1, next_one), (2, grad)):
        taps_grad[row : row + 1, :] += jnp.sum(term * mixed, axis=0, keepdims=True)
    mixed_grad = taps[2:3, :] * grad + taps[1:2, :] * next_one + taps[0:1, :] * next_two
    place = pl.ds(pl.multiple_of((last - step) * rows, rows), rows)
    for k, block in enumerate(
        ((mixed_grad * values).astype(low), dgc[...], (mixed_grad * gate_b).astype(low))
    ):
        dp_ref[:, k * width : (k + 1) * width] = block
        all_dp[place, k * width : (k + 1) * width] = block

    @pl.when(step == last)
    def _():
        half = width // 2
        for target, side in ((keep, core), (give, 1 - core)):
            left = n1t[pl.ds(pl.multiple_of(side * half, half), half), :]
            for k in range(3):
                cols = slice(k * width, (k + 1) * width)
                target[:, cols] = kernel_dot(left, all_dp[:, cols]).astype(low)


def conv_back(conv_grad, gc_grad, proj, masks, edge, taps, n1t, order):
    rows, width = conv_grad.shape
    step = rows // 4
    tile = lambda cols, k=0: pl.BlockSpec((step, cols), lambda i: (3 - i, k))
    low, full = jnp.bfloat16, jnp.float32
    shape = jax.ShapeDtypeStruct
    return pl.pallas_call(
        skip_last(conv_back_kernel, 8, len(order)),
        grid=(4,),
        in_specs=[
            tile(width),
            tile(width),
            tile(width, 0),
            tile(width, 2),
            tile(masks.shape[1]),
            resident(edge.shape),
            resident(taps.shape),
            resident(n1t.shape),
        ]
        + [ANY] * len(order),
        out_specs=[tile(3 * width), resident((8, width))] + [resident((width // 2, 3 * width))] * 2,
        out_shape=[
            shape((rows, 3 * width), low),
            shape((8, width), full),
            shape((width // 2, 3 * width), low),
            shape((width // 2, 3 * width), low),
        ],
        scratch_shapes=[pltpu.VMEM((8, width), full), pltpu.VMEM((rows, 3 * width), low)],
        compiler_params=pltpu.CompilerParams(vmem_limit_bytes=56 * 1024 * 1024),
        cost_estimate=pl.CostEstimate(
            flops=6 * rows * width * width, bytes_accessed=32 * rows * width, transcendentals=0
        ),
    )(conv_grad, gc_grad, proj, proj, masks, edge, taps, n1t, *order)


def in_back_kernel(dp_ref, w_in, x_ref, grad_ref, gain_one, input_grad, gain_grad):
    upstream = kernel_dot(dp_ref[...], w_in[...], BACK_DOT)
    x = x_ref[...].astype(jnp.float32)
    gain = gain_one[...]
    scale = scale_of(x)
    inner = jnp.mean(x * gain * upstream, axis=-1, keepdims=True)
    input_grad[...] = (
        grad_ref[...] + scale * gain * upstream - x * (scale * scale * scale * inner)
    ).astype(jnp.bfloat16)

    @pl.when(pl.program_id(0) == 0)
    def _():
        gain_grad[...] = jnp.zeros_like(gain_grad)

    gain_grad[0:1, :] += jnp.sum(upstream * x * scale, axis=0, keepdims=True)


def in_back(dp, w_in, x, hidden_grad, gain_one, order):
    rows, width = x.shape
    step = rows // 4
    tile = lambda cols: pl.BlockSpec((step, cols), lambda i: (i, 0))
    return pl.pallas_call(
        skip_last(in_back_kernel, 5, len(order)),
        grid=(4,),
        in_specs=[
            tile(3 * width),
            resident(w_in.shape),
            tile(width),
            tile(width),
            resident(gain_one.shape),
        ]
        + [ANY] * len(order),
        out_specs=[tile(width), resident((8, width))],
        out_shape=[
            jax.ShapeDtypeStruct((rows, width), jnp.bfloat16),
            jax.ShapeDtypeStruct((8, width), jnp.float32),
        ],
        compiler_params=pltpu.CompilerParams(vmem_limit_bytes=56 * 1024 * 1024),
        cost_estimate=pl.CostEstimate(
            flops=6 * rows * width * width, bytes_accessed=20 * rows * width, transcendentals=0
        ),
    )(dp, w_in, x, hidden_grad, gain_one, *order)


def base_kernel(rate, master, moment, base):
    base[...] = (
        master[...] * (1.0 - rate[0] * WEIGHT_DECAY) - (rate[0] * MOMENTUM_BETA) * moment[...]
    ).astype(jnp.bfloat16)


def base_of(rate, master, moment, order):
    rows, cols = master.shape
    step = rows // 4
    tile = pl.BlockSpec((step, cols), lambda i: (i, 0))
    return pl.pallas_call(
        skip_last(base_kernel, 3, len(order)),
        grid=(4,),
        in_specs=[pl.BlockSpec(memory_space=pltpu.SMEM), tile, tile] + [ANY] * len(order),
        out_specs=tile,
        out_shape=jax.ShapeDtypeStruct((rows, cols), jnp.bfloat16),
        compiler_params=pltpu.CompilerParams(vmem_limit_bytes=40 * 1024 * 1024),
        cost_estimate=pl.CostEstimate(
            flops=3 * rows * cols, bytes_accessed=10 * rows * cols, transcendentals=0
        ),
    )(rate, master, moment, *order)


def update_kernel(bits, scalars, *refs):
    core = bits[2]
    clip, scale = scalars[0], scalars[1]
    count = len(refs) // 7
    for n in range(count):
        own, other, base_own, base_other, moment = refs[5 * n : 5 * n + 5]
        weight, new_moment = refs[5 * count + 2 * n : 5 * count + 2 * n + 2]
        rows = own.shape[0]
        gradient = own[...].astype(jnp.float32)
        new_moment[...] = MOMENTUM_BETA * moment[...] + clip * gradient
        mine = pl.ds(pl.multiple_of(core * rows, rows), rows)
        theirs = pl.ds(pl.multiple_of((1 - core) * rows, rows), rows)
        weight[mine, :] = (base_own[...].astype(jnp.float32) - scale * gradient).astype(jnp.bfloat16)
        weight[theirs, :] = (
            base_other[...].astype(jnp.float32) - scale * other[...].astype(jnp.float32)
        ).astype(jnp.bfloat16)


def update_rows(bits, scalars, grid, block, matrices):
    width = block[1]
    in_specs, out_specs, out_shape, operands = [], [], [], []
    total = 0
    for gradient, source, column, base, base_other, moment in matrices:
        in_specs += [
            pl.BlockSpec(block, lambda *a, source=source: source(a[-1][2], *a[:-1])),
            pl.BlockSpec(block, lambda *a, source=source: source(1 - a[-1][2], *a[:-1])),
        ]
        in_specs += [pl.BlockSpec(block, lambda *a, column=column: (0, column(*a[:-1])))] * 3
        out_specs += [
            pl.BlockSpec((2 * block[0], width), lambda *a, column=column: (0, column(*a[:-1]))),
            pl.BlockSpec(block, lambda *a, column=column: (0, column(*a[:-1]))),
        ]
        rows, cols = moment.shape
        total += rows * cols
        out_shape += [
            jax.ShapeDtypeStruct((2 * rows, cols), jnp.bfloat16),
            jax.ShapeDtypeStruct((rows, cols), jnp.float32),
        ]
        operands += [gradient, gradient, base, base_other, moment]
    in_specs = [pl.BlockSpec(memory_space=pltpu.SMEM)] + in_specs
    return pl.pallas_call(
        update_kernel,
        grid_spec=pltpu.PrefetchScalarGridSpec(
            num_scalar_prefetch=1, grid=grid, in_specs=in_specs, out_specs=out_specs
        ),
        out_shape=out_shape,
        compiler_params=pltpu.CompilerParams(vmem_limit_bytes=48 * 1024 * 1024),
        cost_estimate=pl.CostEstimate(flops=8 * total, bytes_accessed=20 * total, transcendentals=0),
    )(bits, scalars, *operands)


def update_down_kernel(bits, scalars, own, other, base_own, base_other, moment, weight, new_moment):
    core = bits[2]
    clip, scale = scalars[0], scalars[1]
    gradient = own[...].astype(jnp.float32).T
    new_moment[...] = MOMENTUM_BETA * moment[...] + clip * gradient
    weight[core] = (base_own[...].astype(jnp.float32) - scale * gradient).astype(jnp.bfloat16)
    gradient = other[...].astype(jnp.float32).T
    weight[1 - core] = (base_other[...].astype(jnp.float32) - scale * gradient).astype(jnp.bfloat16)


def update_down(bits, scalars, gradient, parts, base, base_other, moment):
    rows, width = moment.shape
    cols = gradient.shape[1]
    subs = 2
    step = cols // subs
    row = pl.BlockSpec((step, width), lambda k, t, b: (k * subs + t, 0))
    weight, new_moment = pl.pallas_call(
        update_down_kernel,
        grid_spec=pltpu.PrefetchScalarGridSpec(
            num_scalar_prefetch=1,
            grid=(parts, subs),
            in_specs=[
                pl.BlockSpec(memory_space=pltpu.SMEM),
                pl.BlockSpec((width, step), lambda k, t, b: ((k * 3 + 2) * 2 + b[2], t)),
                pl.BlockSpec((width, step), lambda k, t, b: ((k * 3 + 2) * 2 + 1 - b[2], t)),
                row,
                row,
                row,
            ],
            out_specs=[pl.BlockSpec((2, step, width), lambda k, t, b: (0, k * subs + t, 0)), row],
        ),
        out_shape=[
            jax.ShapeDtypeStruct((2, rows, width), jnp.bfloat16),
            jax.ShapeDtypeStruct((rows, width), jnp.float32),
        ],
        compiler_params=pltpu.CompilerParams(vmem_limit_bytes=48 * 1024 * 1024),
        cost_estimate=pl.CostEstimate(
            flops=8 * rows * width, bytes_accessed=20 * rows * width, transcendentals=0
        ),
    )(bits, scalars, gradient, gradient, base, base_other, moment)
    return weight.reshape(2 * rows, width), new_moment


def local_fast(
    tokens,
    segments,
    cotangent,
    norm_one,
    in_weight,
    conv_weight,
    out_weight,
    norm_two,
    gate_weight,
    up_weight,
    down_weight,
    moment_norm_one,
    moment_in,
    moment_conv,
    moment_out,
    moment_norm_two,
    moment_gate,
    moment_up,
    moment_down,
    learn_rate,
    step_number,
):
    masters = (
        norm_one,
        in_weight,
        conv_weight,
        out_weight,
        norm_two,
        gate_weight,
        up_weight,
        down_weight,
    )
    moments = (
        moment_norm_one,
        moment_in,
        moment_conv,
        moment_out,
        moment_norm_two,
        moment_gate,
        moment_up,
        moment_down,
    )
    seq_count, span, model_width = tokens.shape
    row_count = seq_count * span
    x = tokens.reshape(row_count, model_width)
    e = cotangent.reshape(row_count, model_width)
    core = lax.axis_index("shard")
    group = lax.axis_index("dp")
    bits = jnp.stack([lax.rem(group, 2), lax.div(group, 2), core]).astype(jnp.int32)
    start = lax.axis_index("seq") * span
    padding = jnp.full((seq_count, 2), -1, jnp.int32)
    extended = jnp.concatenate([padding, segments, padding], 1)
    current = segment_window(extended, start, 0, span)
    masks = jnp.stack(
        [
            (segment_window(extended, start, offset, span) == current).reshape(row_count)
            for offset in (-1, -2, 1, 2)
        ],
        1,
    ).astype(jnp.float32)
    pack = jnp.concatenate(
        [norm_one[None], norm_two[None], conv_weight, jnp.zeros((3, norm_one.size))], 0
    )
    pack = pack.astype(jnp.bfloat16).astype(jnp.float32)
    (
        proj,
        convolved,
        hidden,
        n1t,
        zt,
        n2,
        n2t,
        gains,
        in_matrix,
        out_matrix,
        gate_matrix,
        up_matrix,
        down_matrix,
    ) = mixer(x, masks, pack, (in_weight, out_weight, gate_weight, up_weight, down_weight))
    gain_one_row, gain_two_row, conv_taps = gains[0:1], gains[1:2], gains[2:5]
    feed_out, feed_back, act, gate_back, up_back, et = feed(
        n2, e, gate_matrix, up_matrix, down_matrix, 2 * FEED_PARTS
    )
    block_out, hidden_grad, gc_grad, conv_out_grad, gain_two_grad, out_keep, out_give = out_back(
        hidden,
        convolved,
        proj,
        e,
        gain_two_row,
        out_matrix,
        zt,
        [feed_out],
        [feed_back],
        [],
    )
    after_edge = from_behind(conv_out_grad[:8, :], "seq", -1)
    proj_back, taps_grad, in_keep, in_give = conv_back(
        conv_out_grad, gc_grad, proj, masks, after_edge, conv_taps, n1t, []
    )
    input_grad, gain_one_grad = in_back(
        proj_back, in_matrix, x, hidden_grad, gain_one_row, []
    )
    rate_now = learn_rate * jnp.minimum(1.0, (step_number + 1).astype(jnp.float32) / WARMUP)
    rate = rate_now.reshape(1)
    base, base_other = {}, {}
    for place in (5, 6, 7, 1, 3):
        base[place] = base_of(rate, masters[place], moments[place], [proj_back])
        base_other[place] = over_core(base[place])
    input_grad = input_grad.reshape(tokens.shape)
    block_out = block_out.reshape(tokens.shape)
    small = jnp.concatenate(
        [gain_one_grad[:1], taps_grad[:3], gain_two_grad[:1], jnp.zeros((3, model_width))], 0
    )
    hidden_units = gate_matrix.shape[1]
    cols = hidden_units // (2 * FEED_PARTS)
    wholes, small_sum, squares = finish(
        (out_keep, out_give),
        (in_keep, in_give),
        n2t,
        et,
        gate_back,
        up_back,
        act,
        FEED_PARTS,
        small,
        [base[place] for place in (5, 6, 7, 1, 3)],
    )
    param_count = 2 * sum((member.size for member in masters))
    clip_level = CLIP_RATIO * math.sqrt(param_count)
    grad_norm = jnp.sqrt(jnp.sum(squares) + jnp.sum(small_sum * small_sum))
    clip_factor = clip_level / jnp.maximum(grad_norm, clip_level)
    scalars = jnp.stack([clip_factor, rate_now * clip_factor])
    half = model_width // 2
    narrow = cols // 2

    def feed_matrix(place, kind):
        return (
            wholes[2],
            lambda side, k, i, t: ((k * 3 + kind) * 4 + side * 2 + i, t),
            lambda k, i, t: (i * FEED_PARTS + k) * 2 + t,
            base[place],
            base_other[place],
            moments[place],
        )

    def plain_matrix(place, gradient):
        return (
            gradient,
            lambda side, t: (side, t),
            lambda t: t,
            base[place],
            base_other[place],
            moments[place],
        )

    new_weight, new_moment = {}, {}
    new_weight[3], new_moment[3] = update_rows(
        bits, scalars, (2,), (half, half), [plain_matrix(3, wholes[0])]
    )
    new_weight[5], new_moment[5], new_weight[6], new_moment[6] = update_rows(
        bits,
        scalars,
        (FEED_PARTS, 2, 2),
        (half, narrow),
        [feed_matrix(5, 0), feed_matrix(6, 1)],
    )
    new_weight[7], new_moment[7] = update_down(
        bits, scalars, wholes[2], FEED_PARTS, base[7], base_other[7], moments[7]
    )
    new_weight[1], new_moment[1] = update_rows(
        bits, scalars, (6,), (half, half), [plain_matrix(1, wholes[1])]
    )
    small_own = lax.dynamic_slice_in_dim(small_sum, core * half, half, 1)
    for place, gradient in ((0, small_own[0]), (2, small_own[1:4]), (4, small_own[4])):
        new_moment[place] = MOMENTUM_BETA * moments[place] + clip_factor * gradient
    return (
        (block_out, input_grad, grad_norm)
        + tuple(new_moment[place] for place in range(8))
        + tuple(new_weight[place] for place in (1, 3, 5, 6, 7))
    )


def local(
    tokens,
    segments,
    cotangent,
    norm_one,
    in_weight,
    conv_weight,
    out_weight,
    norm_two,
    gate_weight,
    up_weight,
    down_weight,
    moment_norm_one,
    moment_in,
    moment_conv,
    moment_out,
    moment_norm_two,
    moment_gate,
    moment_up,
    moment_down,
    learn_rate,
    step_number,
):
    masters = (
        norm_one,
        in_weight,
        conv_weight,
        out_weight,
        norm_two,
        gate_weight,
        up_weight,
        down_weight,
    )
    moments = (
        moment_norm_one,
        moment_in,
        moment_conv,
        moment_out,
        moment_norm_two,
        moment_gate,
        moment_up,
        moment_down,
    )
    whole = (
        lax.all_gather(norm_one.astype(jnp.bfloat16), "shard", axis=0, tiled=True),
        lax.all_gather(in_weight.astype(jnp.bfloat16), "shard", axis=0, tiled=True),
        lax.all_gather(conv_weight.astype(jnp.bfloat16), "shard", axis=1, tiled=True),
        lax.all_gather(out_weight.astype(jnp.bfloat16), "shard", axis=0, tiled=True),
        lax.all_gather(norm_two.astype(jnp.bfloat16), "shard", axis=0, tiled=True),
        lax.all_gather(gate_weight.astype(jnp.bfloat16), "shard", axis=0, tiled=True),
        lax.all_gather(up_weight.astype(jnp.bfloat16), "shard", axis=0, tiled=True),
        lax.all_gather(down_weight.astype(jnp.bfloat16), "shard", axis=0, tiled=True),
    )
    gain_one = whole[0].astype(jnp.float32)
    in_matrix = whole[1]
    conv_taps = whole[2].astype(jnp.float32)
    out_matrix = whole[3]
    gain_two = whole[4].astype(jnp.float32)
    gate_matrix = whole[5]
    up_matrix = whole[6]
    down_matrix = whole[7]
    seq_count, span, model_width = tokens.shape
    row_count = seq_count * span
    hidden_in = tokens.reshape(row_count, model_width).astype(jnp.float32)
    start = lax.axis_index("seq") * span
    padding = jnp.full((seq_count, 2), -1, jnp.int32)
    extended = jnp.concatenate([padding, segments, padding], 1)
    current = segment_window(extended, start, 0, span)
    keep_one = (
        (segment_window(extended, start, -1, span) == current)
        .astype(jnp.float32)
        .reshape(row_count, 1)
    )
    keep_two = (
        (segment_window(extended, start, -2, span) == current)
        .astype(jnp.float32)
        .reshape(row_count, 1)
    )
    next_one = (
        (segment_window(extended, start, 1, span) == current)
        .astype(jnp.float32)
        .reshape(row_count, 1)
    )
    next_two = (
        (segment_window(extended, start, 2, span) == current)
        .astype(jnp.float32)
        .reshape(row_count, 1)
    )
    normed_f, scale_one = norm_forward(hidden_in, gain_one)
    normed_one = normed_f.astype(jnp.bfloat16)
    projected = rows_dot(normed_one, in_matrix)
    gate_b = projected[:, :model_width]
    gate_c = projected[:, model_width : 2 * model_width]
    values = projected[:, 2 * model_width :]
    mixed_in = gate_b * values
    mixed_grid = mixed_in.reshape(seq_count, span, model_width)
    before_edge = from_behind(mixed_grid[:, span - 2 :, :], "seq", 1)
    before = jnp.concatenate([before_edge, mixed_grid], 1)
    before_one = before[:, 1:-1, :].reshape(row_count, model_width)
    before_two = before[:, :-2, :].reshape(row_count, model_width)
    convolved = (
        conv_taps[2] * mixed_in
        + conv_taps[1] * keep_one * before_one
        + conv_taps[0] * keep_two * before_two
    )
    mixer_out = (gate_c * convolved).astype(jnp.bfloat16)
    hidden = hidden_in + rows_dot(mixer_out, out_matrix)
    normed_g, scale_two = norm_forward(hidden, gain_two)
    normed_two = normed_g.astype(jnp.bfloat16)
    gate_pre = rows_dot(normed_two, gate_matrix)
    upward = rows_dot(normed_two, up_matrix)
    sigmoid_gate = jax.nn.sigmoid(gate_pre)
    activated = (gate_pre * sigmoid_gate * upward).astype(jnp.bfloat16)
    block_out = (
        (hidden + rows_dot(activated, down_matrix)).astype(jnp.bfloat16).reshape(tokens.shape)
    )
    cotangent_rows = cotangent.reshape(row_count, model_width)
    down_grad = outer_dot(activated, cotangent_rows)
    act_grad = back_dot(cotangent_rows, down_matrix)
    gate_back = (act_grad * upward * sigmoid_gate * (1.0 + gate_pre * (1.0 - sigmoid_gate))).astype(
        jnp.bfloat16
    )
    up_back = (act_grad * gate_pre * sigmoid_gate).astype(jnp.bfloat16)
    gate_grad = outer_dot(normed_two, gate_back)
    up_grad = outer_dot(normed_two, up_back)
    normed_two_grad = back_dot(gate_back, gate_matrix) + back_dot(up_back, up_matrix)
    hidden_part, gain_two_grad = norm_backward(hidden, scale_two, gain_two, normed_two_grad)
    hidden_grad = cotangent_rows.astype(jnp.float32) + hidden_part
    hidden_low = hidden_grad.astype(jnp.bfloat16)
    out_grad = outer_dot(mixer_out, hidden_low)
    mixer_grad = back_dot(hidden_low, out_matrix)
    gate_c_grad = mixer_grad * convolved
    conv_out_grad = mixer_grad * gate_c
    conv_grid = conv_out_grad.reshape(seq_count, span, model_width)
    after_edge = from_behind(conv_grid[:, :2, :], "seq", -1)
    after = jnp.concatenate([conv_grid, after_edge], 1)
    follow_one = after[:, 1:-1, :].reshape(row_count, model_width)
    follow_two = after[:, 2:, :].reshape(row_count, model_width)
    mixed_grad = (
        conv_taps[2] * conv_out_grad
        + conv_taps[1] * next_one * follow_one
        + conv_taps[0] * next_two * follow_two
    )
    conv_grad = jnp.stack(
        [
            jnp.sum(conv_out_grad * keep_two * before_two, axis=0),
            jnp.sum(conv_out_grad * keep_one * before_one, axis=0),
            jnp.sum(conv_out_grad * mixed_in, axis=0),
        ],
        0,
    )
    proj_back = jnp.concatenate([mixed_grad * values, gate_c_grad, mixed_grad * gate_b], 1).astype(
        jnp.bfloat16
    )
    in_grad = outer_dot(normed_one, proj_back)
    normed_one_grad = back_dot(proj_back, in_matrix)
    input_part, gain_one_grad = norm_backward(hidden_in, scale_one, gain_one, normed_one_grad)
    input_grad = (hidden_grad + input_part).astype(jnp.bfloat16).reshape(tokens.shape)
    shares = (
        lax.psum_scatter(gain_one_grad, "shard", scatter_dimension=0, tiled=True),
        lax.psum_scatter(in_grad, "shard", scatter_dimension=0, tiled=True),
        lax.psum_scatter(conv_grad, "shard", scatter_dimension=1, tiled=True),
        lax.psum_scatter(out_grad, "shard", scatter_dimension=0, tiled=True),
        lax.psum_scatter(gain_two_grad, "shard", scatter_dimension=0, tiled=True),
        lax.psum_scatter(gate_grad, "shard", scatter_dimension=0, tiled=True),
        lax.psum_scatter(up_grad, "shard", scatter_dimension=0, tiled=True),
        lax.psum_scatter(down_grad, "shard", scatter_dimension=0, tiled=True),
    )
    param_count = sum((member.size for member in whole))
    clip_level = CLIP_RATIO * math.sqrt(param_count)
    rate_now = learn_rate * jnp.minimum(1.0, (step_number + 1).astype(jnp.float32) / WARMUP)
    large_places = (1, 3, 5, 6, 7)
    summed = lax.psum(
        (shares[0], shares[1], shares[2], shares[3], shares[4], shares[5], shares[6], shares[7]),
        ("dp", "seq"),
    )
    squares_local = sum((jnp.sum(member * member) for member in summed))
    squares_sum = lax.psum(squares_local, "shard")
    grad_norm = jnp.sqrt(squares_sum)
    clip_factor = clip_level / jnp.maximum(grad_norm, clip_level)
    next_moments = new_moments(summed, moments, clip_factor)
    large_low = new_weights(
        tuple((masters[place] for place in large_places)),
        tuple((next_moments[place] for place in large_places)),
        rate_now,
    )
    weights = (
        lax.all_gather(large_low[0], "shard", axis=0, tiled=True),
        lax.all_gather(large_low[1], "shard", axis=0, tiled=True),
        lax.all_gather(large_low[2], "shard", axis=0, tiled=True),
        lax.all_gather(large_low[3], "shard", axis=0, tiled=True),
        lax.all_gather(large_low[4], "shard", axis=0, tiled=True),
    )
    return (
        block_out,
        input_grad,
        grad_norm,
        next_moments[0],
        next_moments[1],
        next_moments[2],
        next_moments[3],
        next_moments[4],
        next_moments[5],
        next_moments[6],
        next_moments[7],
        weights[0],
        weights[1],
        weights[2],
        weights[3],
        weights[4],
    )


def solution(mesh):
    placed = (
        P(("dp", "shard"), "seq", None),
        P(("dp", "shard"), None),
        P(("dp", "shard"), "seq", None),
        P("shard"),
        P("shard", None),
        P(None, "shard"),
        P("shard", None),
        P("shard"),
        P("shard", None),
        P("shard", None),
        P("shard", None),
        P("shard"),
        P("shard", None),
        P(None, "shard"),
        P("shard", None),
        P("shard"),
        P("shard", None),
        P("shard", None),
        P("shard", None),
        P(),
        P(),
    )
    sizes = (mesh.shape["dp"], mesh.shape["seq"], mesh.shape["shard"])
    return jax.shard_map(
        local_fast if sizes == (4, 4, 2) else local,
        mesh=mesh,
        in_specs=placed,
        out_specs=(
            P(("dp", "shard"), "seq", None),
            P(("dp", "shard"), "seq", None),
            P(),
            P("shard"),
            P("shard", None),
            P(None, "shard"),
            P("shard", None),
            P("shard"),
            P("shard", None),
            P("shard", None),
            P("shard", None),
            P(),
            P(),
            P(),
            P(),
            P(),
        ),
        check_vma=False,
    )
```

```python
import functools
import math

import jax
import jax.numpy as jnp
from jax import lax
from jax.experimental import pallas as pl
from jax.experimental.pallas import tpu as pltpu
from jax.sharding import PartitionSpec as P

WARMUP = 2000


EPSILON = 1e-05
MOMENTUM_BETA = 0.9
WEIGHT_DECAY = 0.1
CLIP_RATIO = 0.25

FEED_PARTS = 3


def from_behind(block, axis, distance):
    devices = range(lax.axis_size(axis))
    route = [(i - distance, i) for i in devices if i - distance in devices]
    return lax.ppermute(block, axis, route)


def rows_dot(left, right):
    return jnp.dot(left, right, preferred_element_type=jnp.float32)


def outer_dot(left, right):
    return lax.dot_general(
        left, right, (((0,), (0,)), ((), ())), preferred_element_type=jnp.float32
    )


def back_dot(left, right):
    return lax.dot_general(
        left, right, (((1,), (1,)), ((), ())), preferred_element_type=jnp.float32
    )


def norm_forward(values, gain):
    scale = lax.rsqrt(jnp.mean(values * values, axis=-1, keepdims=True) + EPSILON)
    return (values * scale * gain, scale)


def norm_backward(values, scale, gain, upstream):
    gain_grad = jnp.sum(upstream * values * scale, axis=0)
    inner = jnp.mean(values * gain * upstream, axis=-1, keepdims=True)
    return (scale * gain * upstream - values * scale * scale * scale * inner, gain_grad)


def segment_window(extended, start, offset, length):
    return lax.dynamic_slice_in_dim(extended, start + 2 + offset, length, 1)


def new_moments(gradients, moments, clip_factor):
    return tuple(
        (
            MOMENTUM_BETA * moment + clip_factor * gradient
            for moment, gradient in zip(moments, gradients)
        )
    )


def new_weights(masters, next_moments, rate_now):
    return tuple(
        (
            (master * (1.0 - rate_now * WEIGHT_DECAY) - rate_now * moment).astype(jnp.bfloat16)
            for master, moment in zip(masters, next_moments)
        )
    )


MESH = pl.DeviceIdType.MESH
ANY = pl.BlockSpec(memory_space=pl.ANY)
INTO_VMEM = pl.BlockSpec(memory_space=pltpu.VMEM)
ROWS_DOT = (((1,), (0,)), ((), ()))
BACK_DOT = (((1,), (1,)), ((), ()))
KEEP_SLOTS, GOT_SLOTS, TILE_ROWS = 3, 2, 128


def kernel_dot(left, right, dims=ROWS_DOT):
    return lax.dot_general(left, right, dims, preferred_element_type=jnp.float32)


def finish_kernel(chunks, parts, wholes_count, *refs):
    count = len(chunks)
    (
        n2t,
        et,
        n1t,
        masks,
        gains,
        rate,
        gate_back,
        up_back,
        act,
        hidden,
        convolved,
        proj,
        e,
        back,
        zt,
        x,
        w_in,
        w_out,
    ) = refs[:18]
    masters, moments = refs[18:23], refs[23:28]
    refs = refs[28:]
    whole_refs = refs[:wholes_count]
    small_out, square_out, input_grad, hidden_grad, gc_grad, conv_grad, dp = refs[
        wholes_count : wholes_count + 7
    ]
    refs = refs[wholes_count + 7 :]
    bases, bases_other = refs[:5], refs[5:10]
    rest = refs[10:]
    out_keep, out_give, out_got = rest[:3]
    keep_ring, got_ring, give_buffer, tiles, edge = rest[3:8]
    rest = rest[8:]
    first_in = rest[:count]
    pieces = rest[count : 2 * count]
    done = rest[2 * count : 3 * count]
    from_mid = rest[3 * count : 4 * count]
    small_in, square_in = rest[4 * count : 4 * count + 2]
    (
        send,
        recv,
        small_send,
        small_recv,
        square_send,
        square_recv,
        own_sem,
        load_sem,
        tile_sem,
        base_send,
        base_recv,
        edge_send,
        edge_recv,
        credit,
    ) = rest[4 * count + 2 :]

    group = lax.axis_index("dp")
    place = lax.axis_index("seq")
    core = lax.axis_index("shard")
    x_bit = lax.rem(group, 2)
    y_bit = lax.div(group, 2)
    over_x = (group + 1 - 2 * x_bit, place, core)
    over_y = (group + 2 - 4 * y_bit, place, core)
    sibling = (group, place, 1 - core)
    z_near = (group, place + 1 - 2 * lax.rem(place, 2), core)
    z_far = (group, 3 - place, core)
    is_mid = jnp.logical_or(place == 1, place == 2)
    is_end = jnp.logical_not(is_mid)
    first_dev, second_dev = (over_x, over_y), (over_y, over_x)
    first_bit, second_bit = (x_bit, y_bit), (y_bit, x_bit)

    barrier = pltpu.get_barrier_semaphore()
    for device in (over_x, over_y, sibling, z_near, z_far):
        pl.semaphore_signal(barrier, inc=1, device_id=device, device_id_type=MESH)
    pl.semaphore_wait(barrier, 5)

    def unit_of(c):
        return chunks[c][2] // 8

    ringed = [c for c in range(count) if chunks[c][0] == "feed"]

    def is_feed(c):
        return chunks[c][0] == "feed"

    def keep_of(c):
        return keep_ring.at[ringed.index(c) % KEEP_SLOTS] if is_feed(c) else out_keep

    def got_of(c):
        return got_ring.at[ringed.index(c) % GOT_SLOTS] if is_feed(c) else out_got

    def remote(source, target, c, k, device):
        return pltpu.make_async_remote_copy(
            src_ref=source,
            dst_ref=target,
            send_sem=send.at[c, k],
            recv_sem=recv.at[c, k],
            device_id=device,
            device_id_type=MESH,
        )

    def aligned(start, size):
        return pl.ds(pl.multiple_of(start, 16), size)

    def rows_of(c, h, first, second, owner):
        unit = unit_of(c)
        _, _, _, _, base, stride = chunks[c][:6]
        return aligned(base + owner * stride + ((h * 2 + first) * 2 + second) * unit, unit)

    def local_rows(c, h, first, second=None):
        unit = unit_of(c)
        if second is None:
            return aligned((h * 2 + first) * 2 * unit, 2 * unit)
        return aligned(((h * 2 + first) * 2 + second) * unit, unit)

    def whole_of(c):
        return whole_refs[chunks[c][3 + 0]]

    def mine(c, h):
        unit = unit_of(c)
        return done[c].at[pl.ds(h * unit, unit)]

    def add_into(target, target_row, one, one_row, two, two_row, rows):
        def body(i, carry):
            at = lambda start: aligned(start + i * 16, 16)
            total = one[at(one_row), :].astype(jnp.float32) + two[at(two_row), :].astype(
                jnp.float32
            )
            target[at(target_row), :] = total.astype(jnp.bfloat16)
            return carry

        lax.fori_loop(0, rows // 16, body, 0)

    def add_squares(c):
        width = chunks[c][7]

        def body(i, total):
            block = done[c][aligned(i * 16, 16), :].astype(jnp.float32)
            block = block * block
            block = block[:8] + block[8:]
            for j in range(width // 128):
                total = total + block[:, j * 128 : (j + 1) * 128]
            return total

        square_out[...] += lax.fori_loop(
            0, 2 * unit_of(c) // 16, body, jnp.zeros((8, 128), jnp.float32)
        )

    def over_core(c):
        return remote(give_buffer if is_feed(c) else out_give, got_of(c), c, 0, sibling)

    def over_first(c, h):
        unit = unit_of(c)
        source = keep_of(c).at[local_rows(c, h, 1 - first_bit[h])]
        return remote(source, first_in[c].at[pl.ds(h * 2 * unit, 2 * unit)], c, 1 + h, first_dev[h])

    def over_second(c, h):
        unit = unit_of(c)
        source = keep_of(c).at[local_rows(c, h, first_bit[h], 1 - second_bit[h])]
        return remote(source, pieces[c].at[pl.ds(h * unit, unit)], c, 3 + h, second_dev[h])

    def z_in(c):
        return remote(pieces[c], done[c], c, 5, z_near)

    def z_mid(c):
        return remote(done[c], from_mid[c], c, 6, z_far)

    def z_out(c):
        return remote(done[c], done[c], c, 7, z_near)

    def to_second(c, h):
        rows = rows_of(c, h, first_bit[h], second_bit[h], core)
        return remote(mine(c, h), whole_of(c).at[rows], c, 8 + h, second_dev[h])

    def to_first(c, h):
        rows = rows_of(c, h, first_bit[h], second_bit[h], core)
        return remote(mine(c, h), whole_of(c).at[rows], c, 10 + h, first_dev[h])

    def pass_first(c, h):
        rows = rows_of(c, h, first_bit[h], 1 - second_bit[h], core)
        return remote(whole_of(c).at[rows], whole_of(c).at[rows], c, 12 + h, first_dev[h])

    def to_sibling(c, h, kind):
        first = first_bit[h] if kind < 2 else 1 - first_bit[h]
        second = second_bit[h] if kind % 2 == 0 else 1 - second_bit[h]
        rows = rows_of(c, h, first, second, core)
        source = mine(c, h) if kind == 0 else whole_of(c).at[rows]
        return remote(source, whole_of(c).at[rows], c, 14 + 2 * kind + h, sibling)

    def own_copy(c, h):
        rows = rows_of(c, h, first_bit[h], second_bit[h], core)
        return pltpu.make_async_copy(mine(c, h), whole_of(c).at[rows], own_sem.at[c, h])

    def load_tile(c, half):
        part, kind = chunks[c][1]
        cols = tiles.shape[2]
        place_of = 2 * part + half if kind == 3 else half * parts + part
        source = (gate_back, up_back, act, dp)[kind]
        return pltpu.make_async_copy(
            source.at[:, pl.ds(place_of * cols, cols)], tiles.at[half], tile_sem.at[half]
        )

    def next_tiles(c):
        if c + 1 < count and is_feed(c + 1):
            for half in range(2):
                load_tile(c + 1, half).start()

    def produce(c):
        if not is_feed(c):
            over_core(c).start()
            next_tiles(c)
            return
        index = ringed.index(c)
        kind = chunks[c][1][1]
        keep = keep_of(c)
        rows = n2t.shape[0] // 2
        for half in range(2):
            load_tile(c, half).wait()

        @pl.loop(0, 2)
        def _(r):
            target = aligned(r * rows, rows)
            for ref, side in ((keep, core), (give_buffer, 1 - core)):
                if kind == 2:
                    block = kernel_dot(et[target, :], tiles[side])
                else:
                    left = n1t if kind == 3 else n2t
                    block = kernel_dot(left[aligned(side * rows, rows), :], tiles[r])
                ref[target, :] = block.astype(jnp.bfloat16)

        next_tiles(c)
        if index >= GOT_SLOTS:
            pl.semaphore_wait(credit, 1)
        over_core(c).start()

    def sum_core(c):
        over_core(c).wait()
        add_into(keep_of(c), 0, keep_of(c), 0, got_of(c), 0, chunks[c][2])
        if is_feed(c) and ringed.index(c) + GOT_SLOTS < len(ringed):
            pl.semaphore_signal(credit, inc=1, device_id=sibling, device_id_type=MESH)
        for h in range(2):
            over_first(c, h).start()

    def sum_first(c):
        unit = unit_of(c)
        for h in range(2):
            over_first(c, h).wait()
            row = (h * 2 + first_bit[h]) * 2 * unit
            add_into(keep_of(c), row, keep_of(c), row, first_in[c], h * 2 * unit, 2 * unit)
            over_second(c, h).start()

    def sum_second(c):
        unit = unit_of(c)
        for h in range(2):
            over_second(c, h).wait()
            row = ((h * 2 + first_bit[h]) * 2 + second_bit[h]) * unit
            add_into(pieces[c], h * unit, pieces[c], h * unit, keep_of(c), row, unit)

        @pl.when(is_end)
        def _():
            z_in(c).start()

    def sum_end(c):
        @pl.when(is_mid)
        def _():
            z_in(c).wait_recv()
            add_into(done[c], 0, pieces[c], 0, done[c], 0, 2 * unit_of(c))
            z_mid(c).start()

    def sum_middle(c):
        @pl.when(is_mid)
        def _():
            z_mid(c).wait()
            add_into(done[c], 0, done[c], 0, from_mid[c], 0, 2 * unit_of(c))
            z_out(c).start()

        @pl.when(is_end)
        def _():
            z_in(c).wait_send()
            z_out(c).wait_recv()

        for h in range(2):
            to_second(c, h).start()
            to_first(c, h).start()
            to_sibling(c, h, 0).start()
            own_copy(c, h).start()
        add_squares(c)

    def forward(c):
        for h in range(2):
            to_second(c, h).wait_recv()
            pass_first(c, h).start()
            to_sibling(c, h, 1).start()

    def last_hop(c):
        for h in range(2):
            to_first(c, h).wait_recv()
            to_sibling(c, h, 2).start()
            pass_first(c, h).wait_recv()
            to_sibling(c, h, 3).start()

    def drain(c):
        @pl.when(is_mid)
        def _():
            z_out(c).wait_send()

        for h in range(2):
            to_second(c, h).wait_send()
            to_first(c, h).wait_send()
            pass_first(c, h).wait_send()
            own_copy(c, h).wait()
            for kind in range(4):
                to_sibling(c, h, kind).wait()

    small_route = (sibling, over_x, over_y, z_near, z_far)

    def small_copy(k):
        return pltpu.make_async_remote_copy(
            src_ref=small_out,
            dst_ref=small_in.at[k],
            send_sem=small_send.at[k],
            recv_sem=small_recv.at[k],
            device_id=small_route[k],
            device_id_type=MESH,
        )

    def square_copy(k):
        return pltpu.make_async_remote_copy(
            src_ref=square_out,
            dst_ref=square_in.at[k],
            send_sem=square_send.at[k],
            recv_sem=square_recv.at[k],
            device_id=small_route[k],
            device_id_type=MESH,
        )

    width = n2t.shape[0]
    low, full = jnp.bfloat16, jnp.float32
    blocks = x.shape[0] // TILE_ROWS
    gain_one, gain_two = gains[0:1, :], gains[1:2, :]
    tile = lambda cols, k=0: pl.BlockSpec((TILE_ROWS, cols), lambda i: (i, k))
    turned = lambda cols, k=0: pl.BlockSpec((TILE_ROWS, cols), lambda i: (blocks - 1 - i, k))
    to_before = pltpu.make_async_remote_copy(
        src_ref=conv_grad.at[pl.ds(0, 8)],
        dst_ref=edge,
        send_sem=edge_send,
        recv_sem=edge_recv,
        device_id=(group, lax.rem(place + 3, 4), core),
        device_id_type=MESH,
    )

    def run_out_back():
        def scope(total, w_out_here):
            load = pltpu.make_async_copy(w_out, w_out_here, load_sem)
            load.start()
            total[...] = jnp.zeros_like(total)
            load.wait()

            def body(h_ref, c_ref, gc_ref, e_ref, back_ref, zt_ref, dh_ref, dgc_ref, dc_ref):
                values = h_ref[...]
                upstream = back_ref[...]
                scale = scale_of(values)
                inner = jnp.mean(values * gain_two * upstream, axis=-1, keepdims=True)
                grad = (
                    e_ref[...].astype(full)
                    + scale * gain_two * upstream
                    - values * (scale * scale * scale * inner)
                )
                dh_ref[...] = grad
                rounded = grad.astype(low)
                small_out[4:5, :] += jnp.sum(upstream * values * scale, axis=0, keepdims=True)
                mixer_grad = kernel_dot(rounded, w_out_here[...], BACK_DOT)
                dgc_ref[...] = (mixer_grad * c_ref[...]).astype(low)
                dc_ref[...] = mixer_grad * gc_ref[...]
                total[...] += kernel_dot(zt_ref[...], rounded)

            pltpu.emit_pipeline(
                body,
                grid=(blocks,),
                in_specs=[tile(width), tile(width), tile(width, 1), tile(width), tile(width)]
                + [pl.BlockSpec((width, TILE_ROWS), lambda i: (0, i))],
                out_specs=[tile(width)] * 3,
            )(hidden, convolved, proj, e, back, zt, hidden_grad, gc_grad, conv_grad)
            rows = width // 2
            for target, side in ((out_keep, core), (out_give, 1 - core)):
                target[...] = total[aligned(side * rows, rows), :].astype(low)

        pl.run_scoped(scope, pltpu.VMEM((width, width), full), pltpu.VMEM((width, width), low))

        @pl.when(place > 0)
        def _():
            to_before.start()

    def run_conv_back():
        @pl.when(place == 3)
        def _():
            edge[...] = jnp.zeros_like(edge)

        @pl.when(place < 3)
        def _():
            to_before.wait_recv()

        @pl.when(place > 0)
        def _():
            to_before.wait_send()

        def body(dc_ref, dgc_ref, gb_ref, v_ref, masks_ref, dp_ref):
            grad = dc_ref[...]
            beside = edge[...]
            next_one = masks_ref[:, 2:3] * shifted(grad, beside, 1)
            next_two = masks_ref[:, 3:4] * shifted(grad, beside, 2)
            edge[...] = grad[:8, :]
            gate_b, values = gb_ref[...], v_ref[...]
            mixed = gate_b * values
            for row, term in ((1, next_two), (2, next_one), (3, grad)):
                small_out[row : row + 1, :] += jnp.sum(term * mixed, axis=0, keepdims=True)
            mixed_grad = (
                gains[4:5, :] * grad + gains[3:4, :] * next_one + gains[2:3, :] * next_two
            )
            dp_ref[:, :width] = (mixed_grad * values).astype(low)
            dp_ref[:, width : 2 * width] = dgc_ref[...]
            dp_ref[:, 2 * width :] = (mixed_grad * gate_b).astype(low)

        pltpu.emit_pipeline(
            body,
            grid=(blocks,),
            in_specs=[
                turned(width),
                turned(width),
                turned(width),
                turned(width, 2),
                turned(masks.shape[1]),
            ],
            out_specs=[turned(3 * width)],
        )(conv_grad, gc_grad, proj, proj, masks, dp)

    def run_in_back():
        def scope(w_in_here):
            load = pltpu.make_async_copy(w_in, w_in_here, load_sem)
            load.start()
            load.wait()

            def body(dp_ref, x_ref, dh_ref, grad_ref):
                upstream = kernel_dot(dp_ref[...], w_in_here[...], BACK_DOT)
                values = x_ref[...].astype(full)
                scale = scale_of(values)
                inner = jnp.mean(values * gain_one * upstream, axis=-1, keepdims=True)
                grad_ref[...] = (
                    dh_ref[...]
                    + scale * gain_one * upstream
                    - values * (scale * scale * scale * inner)
                ).astype(low)
                small_out[0:1, :] += jnp.sum(upstream * values * scale, axis=0, keepdims=True)

            pltpu.emit_pipeline(
                body,
                grid=(blocks,),
                in_specs=[tile(3 * width), tile(width), tile(width)],
                out_specs=[tile(width)],
            )(dp, x, hidden_grad, input_grad)

        pl.run_scoped(scope, pltpu.VMEM(w_in.shape, low))

    def base_copy(n):
        return pltpu.make_async_remote_copy(
            src_ref=bases[n],
            dst_ref=bases_other[n],
            send_sem=base_send.at[n],
            recv_sem=base_recv.at[n],
            device_id=sibling,
            device_id_type=MESH,
        )

    def run_base(n):
        rows, cols = masters[n].shape
        step = 128 if cols <= 1024 else 32
        decay = 1.0 - rate[0] * WEIGHT_DECAY
        slope = rate[0] * MOMENTUM_BETA

        def body(master, moment, base):
            base[...] = (master[...] * decay - slope * moment[...]).astype(low)

        block = pl.BlockSpec((step, cols), lambda i: (i, 0))
        pltpu.emit_pipeline(
            body, grid=(rows // step,), in_specs=[block, block], out_specs=[block]
        )(masters[n], moments[n], bases[n])
        base_copy(n).start()

    work = {
        3: [run_out_back],
        4: [run_conv_back],
        5: [run_in_back],
        6: [functools.partial(run_base, 2)],
        7: [functools.partial(run_base, 3)],
        8: [functools.partial(run_base, 4)],
        9: [functools.partial(run_base, 0), functools.partial(run_base, 1)],
    }
    small_from, squares_from = 8, count + 3

    small_out[...] = jnp.zeros_like(small_out)
    square_out[...] = jnp.zeros_like(square_out)
    for half in range(2):
        load_tile(0, half).start()

    def at(step, action):
        if 0 <= step < count:
            action(step)

    for t in range(count + 7):
        at(t, produce)
        if small_from <= t <= small_from + 5:
            k = t - small_from
            if k >= 1:
                small_copy(k - 1).wait()
                small_out[...] += small_in[k - 1]
            if k < 5:
                small_copy(k).start()
        at(t - 1, sum_first)
        at(t - 2, sum_second)
        at(t - 3, sum_middle)
        if squares_from <= t < squares_from + 4:
            k = t - squares_from
            if k >= 1:
                square_copy(k - 1).wait()
                square_out[...] += square_in[k - 1]
            if k < 3:
                square_copy(k).start()
        at(t - 5, last_hop)
        at(t, sum_core)
        at(t - 2, sum_end)
        at(t - 4, forward)
        for item in work.get(t, ()):
            item()
    for c in range(count):
        drain(c)
    for n in range(5):
        base_copy(n).wait()


def finish(feed_ins, mixer_ins, masters, moments, parts):
    n2t, et, gate_back, up_back, act, back = feed_ins
    n1t, zt, hidden, convolved, proj, masks, gains, e, x, w_in, w_out, rate = mixer_ins
    rows, width = x.shape
    half = width // 2
    cols = gate_back.shape[1] // (2 * parts)
    in_cols = w_in.shape[1]
    chunks = []
    for part in range(parts):
        for kind in range(3):
            first = (part * 3 + kind) * 2 * width
            chunks.append(("feed", (part, kind), width, 2, first, width, 0, cols))
    chunks.append(("out", None, half, 0, 0, half, 0, width))
    in_parts = in_cols // (2 * cols)
    for part in range(in_parts):
        chunks.append(("feed", (part, 3), width, 1, part * 2 * width, width, 0, cols))
    count = len(chunks)
    low, full = jnp.bfloat16, jnp.float32
    shape = jax.ShapeDtypeStruct
    semaphore = pltpu.SemaphoreType.DMA
    wholes = [(width, width), (in_parts * 2 * width, cols), (parts * 3 * 2 * width, cols)]
    eighths = [(chunk[2] // 8, chunk[7]) for chunk in chunks]
    pair = [pltpu.VMEM((2 * r, c), low) for r, c in eighths]
    outs = pl.pallas_call(
        functools.partial(finish_kernel, tuple(chunks), parts, len(wholes)),
        out_shape=[shape(whole, low) for whole in wholes]
        + [
            shape((8, width), full),
            shape((8, 128), full),
            shape((rows, width), low),
            shape((rows, width), full),
            shape((rows, width), low),
            shape((rows, width), full),
            shape((rows, in_cols), low),
        ]
        + [shape(master.shape, low) for master in masters] * 2,
        in_specs=[INTO_VMEM] * 3
        + [ANY, INTO_VMEM, pl.BlockSpec(memory_space=pltpu.SMEM)]
        + [ANY] * (12 + 2 * len(masters)),
        out_specs=[ANY] * len(wholes) + [INTO_VMEM] * 2 + [ANY] * (5 + 2 * len(masters)),
        scratch_shapes=[pltpu.VMEM((half, width), low)] * 3
        + [
            pltpu.VMEM((KEEP_SLOTS, width, cols), low),
            pltpu.VMEM((GOT_SLOTS, width, cols), low),
            pltpu.VMEM((width, cols), low),
            pltpu.VMEM((2, rows, cols), low),
            pltpu.VMEM((8, width), full),
        ]
        + [pltpu.VMEM((4 * r, c), low) for r, c in eighths]
        + pair * 3
        + [
            pltpu.VMEM((5, 8, width), full),
            pltpu.VMEM((3, 8, 128), full),
            semaphore((count, 22)),
            semaphore((count, 22)),
            semaphore((5,)),
            semaphore((5,)),
            semaphore((3,)),
            semaphore((3,)),
            semaphore((count, 2)),
            semaphore,
            semaphore((2,)),
            semaphore((5,)),
            semaphore((5,)),
            semaphore,
            semaphore,
            pltpu.SemaphoreType.REGULAR,
        ],
        compiler_params=pltpu.CompilerParams(
            collective_id=0, has_side_effects=True, vmem_limit_bytes=62 * 1024 * 1024
        ),
    )(
        n2t,
        et,
        n1t,
        masks,
        gains,
        rate,
        gate_back,
        up_back,
        act,
        hidden,
        convolved,
        proj,
        e,
        back,
        zt,
        x,
        w_in,
        w_out,
        *masters,
        *moments,
    )
    return outs[:3], outs[3], outs[4], outs[5], outs[10:15], outs[15:20]


def feed_kernel(step, n2, e, hidden, wg, wu, wd, block_out, back, act, gate_back, up_back, et, out):
    @pl.when(pl.program_id(0) == 0)
    def _():
        et[...] = e[...].T
        out[...] = hidden[...]
        back[...] = jnp.zeros_like(back)

    @pl.loop(0, n2.shape[0] // step)
    def _(t):
        rows = pl.ds(pl.multiple_of(t * step, step), step)
        gate = kernel_dot(n2[rows, :], wg[...])
        up = kernel_dot(n2[rows, :], wu[...])
        grad = kernel_dot(e[rows, :], wd[...], BACK_DOT)
        sigmoid = 0.5 * jnp.tanh(0.5 * gate) + 0.5
        silu = gate * sigmoid
        low_act = (silu * up).astype(jnp.bfloat16)
        low_up = (grad * silu).astype(jnp.bfloat16)
        low_gate = (grad * up * (sigmoid + silu * (1.0 - sigmoid))).astype(jnp.bfloat16)
        act[rows, :] = low_act
        gate_back[rows, :] = low_gate
        up_back[rows, :] = low_up
        out[rows, :] += kernel_dot(low_act, wd[...])
        back[rows, :] += kernel_dot(low_gate, wg[...], BACK_DOT) + kernel_dot(
            low_up, wu[...], BACK_DOT
        )

    @pl.when(pl.program_id(0) == pl.num_programs(0) - 1)
    def _():
        block_out[...] = out[...].astype(jnp.bfloat16)


def feed(n2, e, hidden, gate_matrix, up_matrix, down_matrix, tiles):
    rows, width = n2.shape
    assert rows == width
    cols = gate_matrix.shape[1] // tiles
    whole = pl.BlockSpec((rows, width), lambda i: (0, 0), pipeline_mode=pl.Buffered(1))
    tile = pl.BlockSpec((rows, cols), lambda i: (0, i))
    return pl.pallas_call(
        functools.partial(feed_kernel, rows // 2),
        grid=(tiles,),
        in_specs=[whole, whole, whole]
        + [pl.BlockSpec((width, cols), lambda i: (0, i))] * 2
        + [pl.BlockSpec((cols, width), lambda i: (i, 0))],
        out_specs=[whole, whole, tile, tile, tile, whole],
        out_shape=[
            jax.ShapeDtypeStruct((rows, width), jnp.bfloat16),
            jax.ShapeDtypeStruct((rows, width), jnp.float32),
        ]
        + [jax.ShapeDtypeStruct((rows, tiles * cols), jnp.bfloat16)] * 3
        + [jax.ShapeDtypeStruct((width, rows), jnp.bfloat16)],
        scratch_shapes=[pltpu.VMEM((rows, width), jnp.float32)],
        cost_estimate=pl.CostEstimate(
            flops=12 * rows * width * cols * tiles,
            bytes_accessed=70 * 1024 * 1024,
            transcendentals=rows * cols * tiles,
        ),
        compiler_params=pltpu.CompilerParams(vmem_limit_bytes=56 * 1024 * 1024),
    )(n2, e, hidden, gate_matrix, up_matrix, down_matrix)


def scale_of(values):
    return lax.rsqrt(jnp.mean(values * values, axis=-1, keepdims=True) + EPSILON)


def shifted(values, edge, distance):
    rows = values.shape[0]
    moved = pltpu.roll(values, (-distance) % rows, 0)
    index = lax.broadcasted_iota(jnp.int32, values.shape, 0)
    if distance < 0:
        for row in range(-distance):
            moved = jnp.where(index == row, edge[8 + distance + row : 9 + distance + row, :], moved)
    else:
        for row in range(distance):
            moved = jnp.where(index == rows - distance + row, edge[row : row + 1, :], moved)
    return moved


STEPS = 4


def mixer_kernel(
    x_ref,
    x_all,
    masks,
    pack,
    in_master,
    out_master,
    gate_master,
    up_master,
    down_master,
    proj,
    conv,
    hid,
    n1t,
    zt,
    n2,
    n2t,
    gains,
    in_whole,
    out_whole,
    gate_whole,
    up_whole,
    down_whole,
    carry,
    edge,
    pack_in,
    w_in,
    w_out,
    in_stage,
    out_stage,
    gate_stage,
    up_stage,
    down_stage,
    gate_low,
    up_low,
    down_low,
    load_sem,
    send,
    recv,
    keep_sem,
    part_load,
    part_send,
    part_recv,
    part_keep,
):
    width = x_ref.shape[1]
    half = width // 2
    low = jnp.bfloat16
    step = pl.program_id(0)
    group = lax.axis_index("dp")
    place = lax.axis_index("seq")
    core = lax.axis_index("shard")
    places = lax.axis_size("seq")
    sibling = (group, place, 1 - core)
    after = (group, lax.rem(place + 1, places), core)
    before = (group, lax.rem(place + places - 1, places), core)

    def remote(source, target, k, device):
        return pltpu.make_async_remote_copy(
            src_ref=source,
            dst_ref=target,
            send_sem=send.at[k],
            recv_sem=recv.at[k],
            device_id=device,
            device_id_type=MESH,
        )

    def own_rows(rows, start=0, count=None):
        return pl.ds(pl.multiple_of(core * rows + start, 16), rows if count is None else count)

    def cast(target, target_row, source, source_row, rows):
        block = 16

        def body(i, carry_):
            put = pl.ds(pl.multiple_of(target_row + i * block, block), block)
            get = pl.ds(pl.multiple_of(source_row + i * block, block), block)
            target[put, :] = source[get, :].astype(low)
            return carry_

        lax.fori_loop(0, rows // block, body, 0)

    stages = (gate_stage, up_stage, down_stage)
    masters = (gate_master, up_master, down_master)
    wholes = (gate_whole, up_whole, down_whole)
    lows = (gate_low, up_low, down_low)

    def part_in(m, i):
        rows = stages[m].shape[0]
        return pltpu.make_async_copy(
            masters[m].at[pl.ds(pl.multiple_of(i * rows, 16), rows)], stages[m], part_load.at[m]
        )

    def part_rows(m, i):
        rows = stages[m].shape[0]
        return pl.ds(pl.multiple_of(core * (STEPS * rows) + i * rows, 16), rows)

    def part_out(m, i):
        slot = lax.rem(i, 2)
        return pltpu.make_async_remote_copy(
            src_ref=lows[m].at[slot],
            dst_ref=wholes[m].at[part_rows(m, i)],
            send_sem=part_send.at[i, m],
            recv_sem=part_recv.at[i, m],
            device_id=sibling,
            device_id_type=MESH,
        )

    def part_own(m, i):
        slot = lax.rem(i, 2)
        return pltpu.make_async_copy(
            lows[m].at[slot], wholes[m].at[part_rows(m, i)], part_keep.at[i, m]
        )

    quarter = half // 2
    copies = []
    for k in range(2):
        rows = own_rows(half, k * quarter, quarter)
        copies.append(remote(w_in.at[rows], w_in.at[rows], k, sibling))
    rows = own_rows(half)
    copies.append(remote(w_out.at[rows], w_out.at[rows], 2, sibling))
    copies.append(remote(pack, pack_in, 3, sibling))
    to_after = remote(x_all.at[pl.ds(x_all.shape[0] - 16, 16)], edge, 4, after)
    in_loads = [
        pltpu.make_async_copy(
            in_master.at[pl.ds(k * quarter, quarter)],
            in_stage.at[pl.ds(k * quarter, quarter)],
            load_sem.at[k],
        )
        for k in range(2)
    ]
    out_load = pltpu.make_async_copy(out_master, out_stage, load_sem.at[2])
    keeps = [
        pltpu.make_async_copy(w_in, in_whole, keep_sem.at[0]),
        pltpu.make_async_copy(w_out, out_whole, keep_sem.at[1]),
    ]

    def project(values, first, count=1):
        return kernel_dot(values, w_in[:, first * width : (first + count) * width])

    def normed(values):
        return (values * scale_of(values) * gains[0:1, :]).astype(low)

    @pl.when(step == 0)
    def _():
        for load in (*in_loads, out_load):
            load.start()
        for m in range(3):
            part_in(m, 0).start()
        barrier = pltpu.get_barrier_semaphore()
        for device in (sibling, after, before):
            pl.semaphore_signal(barrier, inc=1, device_id=device, device_id_type=MESH)
        pl.semaphore_wait(barrier, 3)
        copies[3].start()

        @pl.when(place < places - 1)
        def _():
            to_after.start()

        for k in range(2):
            in_loads[k].wait()
            cast(w_in, core * half + k * quarter, in_stage, k * quarter, quarter)
            copies[k].start()
        out_load.wait()
        cast(w_out, core * half, out_stage, 0, half)
        copies[2].start()

        @pl.when(place == 0)
        def _():
            edge[...] = jnp.zeros_like(edge)

        @pl.when(place > 0)
        def _():
            to_after.wait_recv()

        @pl.when(place < places - 1)
        def _():
            to_after.wait_send()

        for copy in copies:
            copy.wait()
        gains[:, pl.ds(pl.multiple_of(core * half, half), half)] = pack[...]
        gains[:, pl.ds(pl.multiple_of((1 - core) * half, half), half)] = pack_in[...]
        for copy in keeps:
            copy.start()
        rows = normed(edge[...].astype(jnp.float32))
        mixed = project(rows, 0) * project(rows, 2)
        carry[...] = mixed[8:, :]

    @pl.when(step > 0)
    def _():
        i = step - 1

        @pl.when(i >= 2)
        def _():
            for m in range(3):
                part_out(m, i - 2).wait_send()
                part_own(m, i - 2).wait()

        for m in range(3):
            part_in(m, i).wait()
            cast(lows[m].at[lax.rem(i, 2)], 0, stages[m], 0, stages[m].shape[0])
            part_out(m, i).start()
            part_own(m, i).start()

        @pl.when(i + 1 < STEPS)
        def _():
            for m in range(3):
                part_in(m, i + 1).start()

        x = x_ref[...].astype(jnp.float32)
        first = normed(x)
        n1t[...] = first.T
        gate_b, gate_c, values = project(first, 0), project(first, 1), project(first, 2)
        proj[:, :width] = gate_b
        proj[:, width : 2 * width] = gate_c
        proj[:, 2 * width :] = values
        mixed = gate_b * values
        beside = carry[...]
        convolved = (
            gains[4:5, :] * mixed
            + gains[3:4, :] * masks[:, 0:1] * shifted(mixed, beside, -1)
            + gains[2:3, :] * masks[:, 1:2] * shifted(mixed, beside, -2)
        )
        carry[...] = mixed[mixed.shape[0] - 8 :, :]
        conv[...] = convolved
        mixer_out = (gate_c * convolved).astype(low)
        zt[...] = mixer_out.T
        hidden = x + kernel_dot(mixer_out, w_out[...])
        hid[...] = hidden
        second = (hidden * scale_of(hidden) * gains[1:2, :]).astype(low)
        n2[...] = second
        n2t[...] = second.T

    @pl.when(step == STEPS)
    def _():
        for copy in keeps:
            copy.wait()
        for i in range(STEPS):
            for m in range(3):
                if i >= STEPS - 2:
                    part_out(m, i).wait_send()
                    part_own(m, i).wait()
                part_out(m, i).wait_recv()


def resident(shape):
    return pl.BlockSpec(shape, lambda i: (0,) * len(shape), pipeline_mode=pl.Buffered(1))


def mixer(x, masks, pack, masters):
    rows, width = x.shape
    step = rows // STEPS
    at = lambda i: jnp.maximum(i - 1, 0)
    tile = lambda cols: pl.BlockSpec((step, cols), lambda i: (at(i), 0))
    turned = pl.BlockSpec((width, step), lambda i: (0, at(i)))
    low, full = jnp.bfloat16, jnp.float32
    shape = jax.ShapeDtypeStruct
    in_master, out_master = masters[:2]
    large = masters[2:]
    whole = [shape((2 * m.shape[0], m.shape[1]), low) for m in masters]
    parts = [(m.shape[0] // STEPS, m.shape[1]) for m in large]
    semaphore = pltpu.SemaphoreType.DMA
    return pl.pallas_call(
        mixer_kernel,
        grid=(STEPS + 1,),
        in_specs=[tile(width), ANY, tile(masks.shape[1]), resident(pack.shape)] + [ANY] * 5,
        out_specs=[tile(3 * width), tile(width), tile(width), turned, turned, tile(width), turned]
        + [resident((8, width))]
        + [ANY] * 5,
        out_shape=[
            shape((rows, 3 * width), full),
            shape((rows, width), full),
            shape((rows, width), full),
            shape((width, rows), low),
            shape((width, rows), low),
            shape((rows, width), low),
            shape((width, rows), low),
            shape((8, width), full),
        ]
        + whole,
        scratch_shapes=[
            pltpu.VMEM((8, width), full),
            pltpu.VMEM((16, width), low),
            pltpu.VMEM(pack.shape, full),
            pltpu.VMEM(whole[0].shape, low),
            pltpu.VMEM(whole[1].shape, low),
            pltpu.VMEM(in_master.shape, full),
            pltpu.VMEM(out_master.shape, full),
        ]
        + [pltpu.VMEM(part, full) for part in parts]
        + [pltpu.VMEM((2, *part), low) for part in parts]
        + [
            semaphore((3,)),
            semaphore((5,)),
            semaphore((5,)),
            semaphore((2,)),
            semaphore((3,)),
            semaphore((STEPS, 3)),
            semaphore((STEPS, 3)),
            semaphore((STEPS, 3)),
        ],
        compiler_params=pltpu.CompilerParams(
            collective_id=1, has_side_effects=True, vmem_limit_bytes=60 * 1024 * 1024
        ),
    )(x, x, masks, pack, *masters)


def update_kernel(bits, scalars, *refs):
    core = bits[2]
    clip, scale = scalars[0], scalars[1]
    count = len(refs) // 7
    for n in range(count):
        own, other, base_own, base_other, moment = refs[5 * n : 5 * n + 5]
        weight, new_moment = refs[5 * count + 2 * n : 5 * count + 2 * n + 2]
        rows = own.shape[0]
        gradient = own[...].astype(jnp.float32)
        new_moment[...] = MOMENTUM_BETA * moment[...] + clip * gradient
        mine = pl.ds(pl.multiple_of(core * rows, rows), rows)
        theirs = pl.ds(pl.multiple_of((1 - core) * rows, rows), rows)
        weight[mine, :] = (base_own[...].astype(jnp.float32) - scale * gradient).astype(jnp.bfloat16)
        weight[theirs, :] = (
            base_other[...].astype(jnp.float32) - scale * other[...].astype(jnp.float32)
        ).astype(jnp.bfloat16)


def update_rows(bits, scalars, grid, block, matrices):
    width = block[1]
    in_specs, out_specs, out_shape, operands = [], [], [], []
    total = 0
    for gradient, source, column, base, base_other, moment in matrices:
        in_specs += [
            pl.BlockSpec(block, lambda *a, source=source: source(a[-1][2], *a[:-1])),
            pl.BlockSpec(block, lambda *a, source=source: source(1 - a[-1][2], *a[:-1])),
        ]
        in_specs += [pl.BlockSpec(block, lambda *a, column=column: (0, column(*a[:-1])))] * 3
        out_specs += [
            pl.BlockSpec((2 * block[0], width), lambda *a, column=column: (0, column(*a[:-1]))),
            pl.BlockSpec(block, lambda *a, column=column: (0, column(*a[:-1]))),
        ]
        rows, cols = moment.shape
        total += rows * cols
        out_shape += [
            jax.ShapeDtypeStruct((2 * rows, cols), jnp.bfloat16),
            jax.ShapeDtypeStruct((rows, cols), jnp.float32),
        ]
        operands += [gradient, gradient, base, base_other, moment]
    in_specs = [pl.BlockSpec(memory_space=pltpu.SMEM)] + in_specs
    return pl.pallas_call(
        update_kernel,
        grid_spec=pltpu.PrefetchScalarGridSpec(
            num_scalar_prefetch=1, grid=grid, in_specs=in_specs, out_specs=out_specs
        ),
        out_shape=out_shape,
        compiler_params=pltpu.CompilerParams(vmem_limit_bytes=48 * 1024 * 1024),
        cost_estimate=pl.CostEstimate(flops=8 * total, bytes_accessed=20 * total, transcendentals=0),
    )(bits, scalars, *operands)


def update_down_kernel(bits, scalars, own, other, base_own, base_other, moment, weight, new_moment):
    core = bits[2]
    clip, scale = scalars[0], scalars[1]
    gradient = own[...].astype(jnp.float32).T
    new_moment[...] = MOMENTUM_BETA * moment[...] + clip * gradient
    weight[core] = (base_own[...].astype(jnp.float32) - scale * gradient).astype(jnp.bfloat16)
    gradient = other[...].astype(jnp.float32).T
    weight[1 - core] = (base_other[...].astype(jnp.float32) - scale * gradient).astype(jnp.bfloat16)


def update_down(bits, scalars, gradient, parts, base, base_other, moment):
    rows, width = moment.shape
    cols = gradient.shape[1]
    subs = 2
    step = cols // subs
    row = pl.BlockSpec((step, width), lambda k, t, b: (k * subs + t, 0))
    weight, new_moment = pl.pallas_call(
        update_down_kernel,
        grid_spec=pltpu.PrefetchScalarGridSpec(
            num_scalar_prefetch=1,
            grid=(parts, subs),
            in_specs=[
                pl.BlockSpec(memory_space=pltpu.SMEM),
                pl.BlockSpec((width, step), lambda k, t, b: ((k * 3 + 2) * 2 + b[2], t)),
                pl.BlockSpec((width, step), lambda k, t, b: ((k * 3 + 2) * 2 + 1 - b[2], t)),
                row,
                row,
                row,
            ],
            out_specs=[pl.BlockSpec((2, step, width), lambda k, t, b: (0, k * subs + t, 0)), row],
        ),
        out_shape=[
            jax.ShapeDtypeStruct((2, rows, width), jnp.bfloat16),
            jax.ShapeDtypeStruct((rows, width), jnp.float32),
        ],
        compiler_params=pltpu.CompilerParams(vmem_limit_bytes=48 * 1024 * 1024),
        cost_estimate=pl.CostEstimate(
            flops=8 * rows * width, bytes_accessed=20 * rows * width, transcendentals=0
        ),
    )(bits, scalars, gradient, gradient, base, base_other, moment)
    return weight.reshape(2 * rows, width), new_moment


def local_fast(
    tokens,
    segments,
    cotangent,
    norm_one,
    in_weight,
    conv_weight,
    out_weight,
    norm_two,
    gate_weight,
    up_weight,
    down_weight,
    moment_norm_one,
    moment_in,
    moment_conv,
    moment_out,
    moment_norm_two,
    moment_gate,
    moment_up,
    moment_down,
    learn_rate,
    step_number,
):
    masters = (
        norm_one,
        in_weight,
        conv_weight,
        out_weight,
        norm_two,
        gate_weight,
        up_weight,
        down_weight,
    )
    moments = (
        moment_norm_one,
        moment_in,
        moment_conv,
        moment_out,
        moment_norm_two,
        moment_gate,
        moment_up,
        moment_down,
    )
    seq_count, span, model_width = tokens.shape
    row_count = seq_count * span
    x = tokens.reshape(row_count, model_width)
    e = cotangent.reshape(row_count, model_width)
    core = lax.axis_index("shard")
    group = lax.axis_index("dp")
    bits = jnp.stack([lax.rem(group, 2), lax.div(group, 2), core]).astype(jnp.int32)
    start = lax.axis_index("seq") * span
    padding = jnp.full((seq_count, 2), -1, jnp.int32)
    extended = jnp.concatenate([padding, segments, padding], 1)
    current = segment_window(extended, start, 0, span)
    masks = jnp.stack(
        [
            (segment_window(extended, start, offset, span) == current).reshape(row_count)
            for offset in (-1, -2, 1, 2)
        ],
        1,
    ).astype(jnp.float32)
    pack = jnp.concatenate(
        [norm_one[None], norm_two[None], conv_weight, jnp.zeros((3, norm_one.size))], 0
    )
    pack = pack.astype(jnp.bfloat16).astype(jnp.float32)
    (
        proj,
        convolved,
        hidden,
        n1t,
        zt,
        n2,
        n2t,
        gains,
        in_matrix,
        out_matrix,
        gate_matrix,
        up_matrix,
        down_matrix,
    ) = mixer(x, masks, pack, (in_weight, out_weight, gate_weight, up_weight, down_weight))
    block_out, back, act, gate_back, up_back, et = feed(
        n2, e, hidden, gate_matrix, up_matrix, down_matrix, 2 * FEED_PARTS
    )
    rate_now = learn_rate * jnp.minimum(1.0, (step_number + 1).astype(jnp.float32) / WARMUP)
    large = (1, 3, 5, 6, 7)
    wholes, small_sum, squares, input_grad, bases, bases_other = finish(
        (n2t, et, gate_back, up_back, act, back),
        (
            n1t,
            zt,
            hidden,
            convolved,
            proj,
            masks,
            gains,
            e,
            x,
            in_matrix,
            out_matrix,
            rate_now.reshape(1),
        ),
        [masters[place] for place in large],
        [moments[place] for place in large],
        FEED_PARTS,
    )
    base = dict(zip(large, bases))
    base_other = dict(zip(large, bases_other))
    cols = gate_matrix.shape[1] // (2 * FEED_PARTS)
    input_grad = input_grad.reshape(tokens.shape)
    block_out = block_out.reshape(tokens.shape)
    param_count = 2 * sum((member.size for member in masters))
    clip_level = CLIP_RATIO * math.sqrt(param_count)
    grad_norm = jnp.sqrt(jnp.sum(squares) + jnp.sum(small_sum * small_sum))
    clip_factor = clip_level / jnp.maximum(grad_norm, clip_level)
    scalars = jnp.stack([clip_factor, rate_now * clip_factor])
    half = model_width // 2
    narrow = cols // 2

    def feed_matrix(place, kind):
        return (
            wholes[2],
            lambda side, k, i, t: ((k * 3 + kind) * 4 + side * 2 + i, t),
            lambda k, i, t: (i * FEED_PARTS + k) * 2 + t,
            base[place],
            base_other[place],
            moments[place],
        )

    def plain_matrix(place, gradient):
        return (
            gradient,
            lambda side, t: (side, t),
            lambda t: t,
            base[place],
            base_other[place],
            moments[place],
        )

    new_weight, new_moment = {}, {}
    new_weight[3], new_moment[3] = update_rows(
        bits, scalars, (2,), (half, half), [plain_matrix(3, wholes[0])]
    )
    new_weight[5], new_moment[5], new_weight[6], new_moment[6] = update_rows(
        bits,
        scalars,
        (FEED_PARTS, 2, 2),
        (half, narrow),
        [feed_matrix(5, 0), feed_matrix(6, 1)],
    )
    new_weight[7], new_moment[7] = update_down(
        bits, scalars, wholes[2], FEED_PARTS, base[7], base_other[7], moments[7]
    )
    new_weight[1], new_moment[1] = update_rows(
        bits,
        scalars,
        (in_matrix.shape[1] // narrow // 4, 2, 2),
        (half, narrow),
        [
            (
                wholes[1],
                lambda side, k, i, t: (k * 4 + side * 2 + i, t),
                lambda k, i, t: (k * 2 + i) * 2 + t,
                base[1],
                base_other[1],
                moments[1],
            )
        ],
    )
    small_own = lax.dynamic_slice_in_dim(small_sum, core * half, half, 1)
    for place, gradient in ((0, small_own[0]), (2, small_own[1:4]), (4, small_own[4])):
        new_moment[place] = MOMENTUM_BETA * moments[place] + clip_factor * gradient
    return (
        (block_out, input_grad, grad_norm)
        + tuple(new_moment[place] for place in range(8))
        + tuple(new_weight[place] for place in (1, 3, 5, 6, 7))
    )


def local(
    tokens,
    segments,
    cotangent,
    norm_one,
    in_weight,
    conv_weight,
    out_weight,
    norm_two,
    gate_weight,
    up_weight,
    down_weight,
    moment_norm_one,
    moment_in,
    moment_conv,
    moment_out,
    moment_norm_two,
    moment_gate,
    moment_up,
    moment_down,
    learn_rate,
    step_number,
):
    masters = (
        norm_one,
        in_weight,
        conv_weight,
        out_weight,
        norm_two,
        gate_weight,
        up_weight,
        down_weight,
    )
    moments = (
        moment_norm_one,
        moment_in,
        moment_conv,
        moment_out,
        moment_norm_two,
        moment_gate,
        moment_up,
        moment_down,
    )
    whole = (
        lax.all_gather(norm_one.astype(jnp.bfloat16), "shard", axis=0, tiled=True),
        lax.all_gather(in_weight.astype(jnp.bfloat16), "shard", axis=0, tiled=True),
        lax.all_gather(conv_weight.astype(jnp.bfloat16), "shard", axis=1, tiled=True),
        lax.all_gather(out_weight.astype(jnp.bfloat16), "shard", axis=0, tiled=True),
        lax.all_gather(norm_two.astype(jnp.bfloat16), "shard", axis=0, tiled=True),
        lax.all_gather(gate_weight.astype(jnp.bfloat16), "shard", axis=0, tiled=True),
        lax.all_gather(up_weight.astype(jnp.bfloat16), "shard", axis=0, tiled=True),
        lax.all_gather(down_weight.astype(jnp.bfloat16), "shard", axis=0, tiled=True),
    )
    gain_one = whole[0].astype(jnp.float32)
    in_matrix = whole[1]
    conv_taps = whole[2].astype(jnp.float32)
    out_matrix = whole[3]
    gain_two = whole[4].astype(jnp.float32)
    gate_matrix = whole[5]
    up_matrix = whole[6]
    down_matrix = whole[7]
    seq_count, span, model_width = tokens.shape
    row_count = seq_count * span
    hidden_in = tokens.reshape(row_count, model_width).astype(jnp.float32)
    start = lax.axis_index("seq") * span
    padding = jnp.full((seq_count, 2), -1, jnp.int32)
    extended = jnp.concatenate([padding, segments, padding], 1)
    current = segment_window(extended, start, 0, span)
    keep_one = (
        (segment_window(extended, start, -1, span) == current)
        .astype(jnp.float32)
        .reshape(row_count, 1)
    )
    keep_two = (
        (segment_window(extended, start, -2, span) == current)
        .astype(jnp.float32)
        .reshape(row_count, 1)
    )
    next_one = (
        (segment_window(extended, start, 1, span) == current)
        .astype(jnp.float32)
        .reshape(row_count, 1)
    )
    next_two = (
        (segment_window(extended, start, 2, span) == current)
        .astype(jnp.float32)
        .reshape(row_count, 1)
    )
    normed_f, scale_one = norm_forward(hidden_in, gain_one)
    normed_one = normed_f.astype(jnp.bfloat16)
    projected = rows_dot(normed_one, in_matrix)
    gate_b = projected[:, :model_width]
    gate_c = projected[:, model_width : 2 * model_width]
    values = projected[:, 2 * model_width :]
    mixed_in = gate_b * values
    mixed_grid = mixed_in.reshape(seq_count, span, model_width)
    before_edge = from_behind(mixed_grid[:, span - 2 :, :], "seq", 1)
    before = jnp.concatenate([before_edge, mixed_grid], 1)
    before_one = before[:, 1:-1, :].reshape(row_count, model_width)
    before_two = before[:, :-2, :].reshape(row_count, model_width)
    convolved = (
        conv_taps[2] * mixed_in
        + conv_taps[1] * keep_one * before_one
        + conv_taps[0] * keep_two * before_two
    )
    mixer_out = (gate_c * convolved).astype(jnp.bfloat16)
    hidden = hidden_in + rows_dot(mixer_out, out_matrix)
    normed_g, scale_two = norm_forward(hidden, gain_two)
    normed_two = normed_g.astype(jnp.bfloat16)
    gate_pre = rows_dot(normed_two, gate_matrix)
    upward = rows_dot(normed_two, up_matrix)
    sigmoid_gate = jax.nn.sigmoid(gate_pre)
    activated = (gate_pre * sigmoid_gate * upward).astype(jnp.bfloat16)
    block_out = (
        (hidden + rows_dot(activated, down_matrix)).astype(jnp.bfloat16).reshape(tokens.shape)
    )
    cotangent_rows = cotangent.reshape(row_count, model_width)
    down_grad = outer_dot(activated, cotangent_rows)
    act_grad = back_dot(cotangent_rows, down_matrix)
    gate_back = (act_grad * upward * sigmoid_gate * (1.0 + gate_pre * (1.0 - sigmoid_gate))).astype(
        jnp.bfloat16
    )
    up_back = (act_grad * gate_pre * sigmoid_gate).astype(jnp.bfloat16)
    gate_grad = outer_dot(normed_two, gate_back)
    up_grad = outer_dot(normed_two, up_back)
    normed_two_grad = back_dot(gate_back, gate_matrix) + back_dot(up_back, up_matrix)
    hidden_part, gain_two_grad = norm_backward(hidden, scale_two, gain_two, normed_two_grad)
    hidden_grad = cotangent_rows.astype(jnp.float32) + hidden_part
    hidden_low = hidden_grad.astype(jnp.bfloat16)
    out_grad = outer_dot(mixer_out, hidden_low)
    mixer_grad = back_dot(hidden_low, out_matrix)
    gate_c_grad = mixer_grad * convolved
    conv_out_grad = mixer_grad * gate_c
    conv_grid = conv_out_grad.reshape(seq_count, span, model_width)
    after_edge = from_behind(conv_grid[:, :2, :], "seq", -1)
    after = jnp.concatenate([conv_grid, after_edge], 1)
    follow_one = after[:, 1:-1, :].reshape(row_count, model_width)
    follow_two = after[:, 2:, :].reshape(row_count, model_width)
    mixed_grad = (
        conv_taps[2] * conv_out_grad
        + conv_taps[1] * next_one * follow_one
        + conv_taps[0] * next_two * follow_two
    )
    conv_grad = jnp.stack(
        [
            jnp.sum(conv_out_grad * keep_two * before_two, axis=0),
            jnp.sum(conv_out_grad * keep_one * before_one, axis=0),
            jnp.sum(conv_out_grad * mixed_in, axis=0),
        ],
        0,
    )
    proj_back = jnp.concatenate([mixed_grad * values, gate_c_grad, mixed_grad * gate_b], 1).astype(
        jnp.bfloat16
    )
    in_grad = outer_dot(normed_one, proj_back)
    normed_one_grad = back_dot(proj_back, in_matrix)
    input_part, gain_one_grad = norm_backward(hidden_in, scale_one, gain_one, normed_one_grad)
    input_grad = (hidden_grad + input_part).astype(jnp.bfloat16).reshape(tokens.shape)
    shares = (
        lax.psum_scatter(gain_one_grad, "shard", scatter_dimension=0, tiled=True),
        lax.psum_scatter(in_grad, "shard", scatter_dimension=0, tiled=True),
        lax.psum_scatter(conv_grad, "shard", scatter_dimension=1, tiled=True),
        lax.psum_scatter(out_grad, "shard", scatter_dimension=0, tiled=True),
        lax.psum_scatter(gain_two_grad, "shard", scatter_dimension=0, tiled=True),
        lax.psum_scatter(gate_grad, "shard", scatter_dimension=0, tiled=True),
        lax.psum_scatter(up_grad, "shard", scatter_dimension=0, tiled=True),
        lax.psum_scatter(down_grad, "shard", scatter_dimension=0, tiled=True),
    )
    param_count = sum((member.size for member in whole))
    clip_level = CLIP_RATIO * math.sqrt(param_count)
    rate_now = learn_rate * jnp.minimum(1.0, (step_number + 1).astype(jnp.float32) / WARMUP)
    large_places = (1, 3, 5, 6, 7)
    summed = lax.psum(
        (shares[0], shares[1], shares[2], shares[3], shares[4], shares[5], shares[6], shares[7]),
        ("dp", "seq"),
    )
    squares_local = sum((jnp.sum(member * member) for member in summed))
    squares_sum = lax.psum(squares_local, "shard")
    grad_norm = jnp.sqrt(squares_sum)
    clip_factor = clip_level / jnp.maximum(grad_norm, clip_level)
    next_moments = new_moments(summed, moments, clip_factor)
    large_low = new_weights(
        tuple((masters[place] for place in large_places)),
        tuple((next_moments[place] for place in large_places)),
        rate_now,
    )
    weights = (
        lax.all_gather(large_low[0], "shard", axis=0, tiled=True),
        lax.all_gather(large_low[1], "shard", axis=0, tiled=True),
        lax.all_gather(large_low[2], "shard", axis=0, tiled=True),
        lax.all_gather(large_low[3], "shard", axis=0, tiled=True),
        lax.all_gather(large_low[4], "shard", axis=0, tiled=True),
    )
    return (
        block_out,
        input_grad,
        grad_norm,
        next_moments[0],
        next_moments[1],
        next_moments[2],
        next_moments[3],
        next_moments[4],
        next_moments[5],
        next_moments[6],
        next_moments[7],
        weights[0],
        weights[1],
        weights[2],
        weights[3],
        weights[4],
    )


def solution(mesh):
    placed = (
        P(("dp", "shard"), "seq", None),
        P(("dp", "shard"), None),
        P(("dp", "shard"), "seq", None),
        P("shard"),
        P("shard", None),
        P(None, "shard"),
        P("shard", None),
        P("shard"),
        P("shard", None),
        P("shard", None),
        P("shard", None),
        P("shard"),
        P("shard", None),
        P(None, "shard"),
        P("shard", None),
        P("shard"),
        P("shard", None),
        P("shard", None),
        P("shard", None),
        P(),
        P(),
    )
    sizes = (mesh.shape["dp"], mesh.shape["seq"], mesh.shape["shard"])
    return jax.shard_map(
        local_fast if sizes == (4, 4, 2) else local,
        mesh=mesh,
        in_specs=placed,
        out_specs=(
            P(("dp", "shard"), "seq", None),
            P(("dp", "shard"), "seq", None),
            P(),
            P("shard"),
            P("shard", None),
            P(None, "shard"),
            P("shard", None),
            P("shard"),
            P("shard", None),
            P("shard", None),
            P("shard", None),
            P(),
            P(),
            P(),
            P(),
            P(),
        ),
        check_vma=False,
    )
```

```python
import functools
import math

import jax
import jax.numpy as jnp
from jax import lax
from jax.experimental import pallas as pl
from jax.experimental.pallas import tpu as pltpu
from jax.sharding import PartitionSpec as P

WARMUP = 2000


EPSILON = 1e-05
MOMENTUM_BETA = 0.9
WEIGHT_DECAY = 0.1
CLIP_RATIO = 0.25

FEED_PARTS = 3


def from_behind(block, axis, distance):
    devices = range(lax.axis_size(axis))
    route = [(i - distance, i) for i in devices if i - distance in devices]
    return lax.ppermute(block, axis, route)


def rows_dot(left, right):
    return jnp.dot(left, right, preferred_element_type=jnp.float32)


def outer_dot(left, right):
    return lax.dot_general(
        left, right, (((0,), (0,)), ((), ())), preferred_element_type=jnp.float32
    )


def back_dot(left, right):
    return lax.dot_general(
        left, right, (((1,), (1,)), ((), ())), preferred_element_type=jnp.float32
    )


def norm_forward(values, gain):
    scale = lax.rsqrt(jnp.mean(values * values, axis=-1, keepdims=True) + EPSILON)
    return (values * scale * gain, scale)


def norm_backward(values, scale, gain, upstream):
    gain_grad = jnp.sum(upstream * values * scale, axis=0)
    inner = jnp.mean(values * gain * upstream, axis=-1, keepdims=True)
    return (scale * gain * upstream - values * scale * scale * scale * inner, gain_grad)


def segment_window(extended, start, offset, length):
    return lax.dynamic_slice_in_dim(extended, start + 2 + offset, length, 1)


def new_moments(gradients, moments, clip_factor):
    return tuple(
        (
            MOMENTUM_BETA * moment + clip_factor * gradient
            for moment, gradient in zip(moments, gradients)
        )
    )


def new_weights(masters, next_moments, rate_now):
    return tuple(
        (
            (master * (1.0 - rate_now * WEIGHT_DECAY) - rate_now * moment).astype(jnp.bfloat16)
            for master, moment in zip(masters, next_moments)
        )
    )


MESH = pl.DeviceIdType.MESH
ANY = pl.BlockSpec(memory_space=pl.ANY)
INTO_VMEM = pl.BlockSpec(memory_space=pltpu.VMEM)
ROWS_DOT = (((1,), (0,)), ((), ()))
BACK_DOT = (((1,), (1,)), ((), ()))
KEEP_SLOTS, GOT_SLOTS, TILE_ROWS = 3, 2, 128


def kernel_dot(left, right, dims=ROWS_DOT):
    return lax.dot_general(left, right, dims, preferred_element_type=jnp.float32)


def finish_kernel(chunks, parts, wholes_count, *refs):
    count = len(chunks)
    (
        n2t,
        et,
        n1t,
        masks,
        gains,
        rate,
        gate_back,
        up_back,
        act,
        hidden,
        convolved,
        proj,
        e,
        back,
        zt,
        x,
        w_in,
        w_out,
    ) = refs[:18]
    masters, moments = refs[18:23], refs[23:28]
    refs = refs[28:]
    whole_refs = refs[:wholes_count]
    small_out, square_out, input_grad, hidden_grad, gc_grad, conv_grad, dp = refs[
        wholes_count : wholes_count + 7
    ]
    refs = refs[wholes_count + 7 :]
    bases, bases_other = refs[:5], refs[5:10]
    rest = refs[10:]
    out_keep, out_give, out_got = rest[:3]
    keep_ring, got_ring, give_buffer, tiles, edge = rest[3:8]
    rest = rest[8:]
    first_in = rest[:count]
    pieces = rest[count : 2 * count]
    done = rest[2 * count : 3 * count]
    from_mid = rest[3 * count : 4 * count]
    small_in, square_in = rest[4 * count : 4 * count + 2]
    (
        send,
        recv,
        small_send,
        small_recv,
        square_send,
        square_recv,
        own_sem,
        load_sem,
        tile_sem,
        base_send,
        base_recv,
        edge_send,
        edge_recv,
        credit,
    ) = rest[4 * count + 2 :]

    group = lax.axis_index("dp")
    place = lax.axis_index("seq")
    core = lax.axis_index("shard")
    x_bit = lax.rem(group, 2)
    y_bit = lax.div(group, 2)
    over_x = (group + 1 - 2 * x_bit, place, core)
    over_y = (group + 2 - 4 * y_bit, place, core)
    sibling = (group, place, 1 - core)
    z_near = (group, place + 1 - 2 * lax.rem(place, 2), core)
    z_far = (group, 3 - place, core)
    is_mid = jnp.logical_or(place == 1, place == 2)
    is_end = jnp.logical_not(is_mid)
    first_dev, second_dev = (over_x, over_y), (over_y, over_x)
    first_bit, second_bit = (x_bit, y_bit), (y_bit, x_bit)

    barrier = pltpu.get_barrier_semaphore()
    for device in (over_x, over_y, sibling, z_near, z_far):
        pl.semaphore_signal(barrier, inc=1, device_id=device, device_id_type=MESH)
    pl.semaphore_wait(barrier, 5)

    def unit_of(c):
        return chunks[c][2] // 8

    ringed = [c for c in range(count) if chunks[c][0] == "feed"]

    def is_feed(c):
        return chunks[c][0] == "feed"

    def keep_of(c):
        return keep_ring.at[ringed.index(c) % KEEP_SLOTS] if is_feed(c) else out_keep

    def got_of(c):
        return got_ring.at[ringed.index(c) % GOT_SLOTS] if is_feed(c) else out_got

    def remote(source, target, c, k, device):
        return pltpu.make_async_remote_copy(
            src_ref=source,
            dst_ref=target,
            send_sem=send.at[c, k],
            recv_sem=recv.at[c, k],
            device_id=device,
            device_id_type=MESH,
        )

    def aligned(start, size):
        return pl.ds(pl.multiple_of(start, 16), size)

    def rows_of(c, h, first, second, owner):
        unit = unit_of(c)
        _, _, _, _, base, stride = chunks[c][:6]
        return aligned(base + owner * stride + ((h * 2 + first) * 2 + second) * unit, unit)

    def local_rows(c, h, first, second=None):
        unit = unit_of(c)
        if second is None:
            return aligned((h * 2 + first) * 2 * unit, 2 * unit)
        return aligned(((h * 2 + first) * 2 + second) * unit, unit)

    def whole_of(c):
        return whole_refs[chunks[c][3 + 0]]

    def mine(c, h):
        unit = unit_of(c)
        return done[c].at[pl.ds(h * unit, unit)]

    def add_into(target, target_row, one, one_row, two, two_row, rows):
        def body(i, carry):
            at = lambda start: aligned(start + i * 16, 16)
            total = one[at(one_row), :].astype(jnp.float32) + two[at(two_row), :].astype(
                jnp.float32
            )
            target[at(target_row), :] = total.astype(jnp.bfloat16)
            return carry

        lax.fori_loop(0, rows // 16, body, 0)

    def add_squares(c):
        width = chunks[c][7]

        def body(i, total):
            block = done[c][aligned(i * 16, 16), :].astype(jnp.float32)
            block = block * block
            block = block[:8] + block[8:]
            for j in range(width // 128):
                total = total + block[:, j * 128 : (j + 1) * 128]
            return total

        square_out[...] += lax.fori_loop(
            0, 2 * unit_of(c) // 16, body, jnp.zeros((8, 128), jnp.float32)
        )

    def over_core(c):
        return remote(give_buffer if is_feed(c) else out_give, got_of(c), c, 0, sibling)

    def over_first(c, h):
        unit = unit_of(c)
        source = keep_of(c).at[local_rows(c, h, 1 - first_bit[h])]
        return remote(source, first_in[c].at[pl.ds(h * 2 * unit, 2 * unit)], c, 1 + h, first_dev[h])

    def over_second(c, h):
        unit = unit_of(c)
        source = keep_of(c).at[local_rows(c, h, first_bit[h], 1 - second_bit[h])]
        return remote(source, pieces[c].at[pl.ds(h * unit, unit)], c, 3 + h, second_dev[h])

    def z_in(c):
        return remote(pieces[c], done[c], c, 5, z_near)

    def z_mid(c):
        return remote(done[c], from_mid[c], c, 6, z_far)

    def z_out(c):
        return remote(done[c], done[c], c, 7, z_near)

    def to_second(c, h):
        rows = rows_of(c, h, first_bit[h], second_bit[h], core)
        return remote(mine(c, h), whole_of(c).at[rows], c, 8 + h, second_dev[h])

    def to_first(c, h):
        rows = rows_of(c, h, first_bit[h], second_bit[h], core)
        return remote(mine(c, h), whole_of(c).at[rows], c, 10 + h, first_dev[h])

    def pass_first(c, h):
        rows = rows_of(c, h, first_bit[h], 1 - second_bit[h], core)
        return remote(whole_of(c).at[rows], whole_of(c).at[rows], c, 12 + h, first_dev[h])

    def to_sibling(c, h, kind):
        first = first_bit[h] if kind < 2 else 1 - first_bit[h]
        second = second_bit[h] if kind % 2 == 0 else 1 - second_bit[h]
        rows = rows_of(c, h, first, second, core)
        source = mine(c, h) if kind == 0 else whole_of(c).at[rows]
        return remote(source, whole_of(c).at[rows], c, 14 + 2 * kind + h, sibling)

    def own_copy(c, h):
        rows = rows_of(c, h, first_bit[h], second_bit[h], core)
        return pltpu.make_async_copy(mine(c, h), whole_of(c).at[rows], own_sem.at[c, h])

    def load_tile(c, half):
        part, kind = chunks[c][1]
        cols = tiles.shape[2]
        place_of = 2 * part + half if kind == 3 else half * parts + part
        source = (gate_back, up_back, act, dp)[kind]
        return pltpu.make_async_copy(
            source.at[:, pl.ds(place_of * cols, cols)], tiles.at[half], tile_sem.at[half]
        )

    def next_tiles(c):
        if c + 1 < count and is_feed(c + 1):
            for half in range(2):
                load_tile(c + 1, half).start()

    def produce(c):
        if not is_feed(c):
            over_core(c).start()
            next_tiles(c)
            return
        index = ringed.index(c)
        kind = chunks[c][1][1]
        keep = keep_of(c)
        rows = n2t.shape[0] // 2
        for half in range(2):
            load_tile(c, half).wait()

        @pl.loop(0, 2)
        def _(r):
            target = aligned(r * rows, rows)
            for ref, side in ((keep, core), (give_buffer, 1 - core)):
                if kind == 2:
                    block = kernel_dot(et[target, :], tiles[side])
                else:
                    left = n1t if kind == 3 else n2t
                    block = kernel_dot(left[aligned(side * rows, rows), :], tiles[r])
                ref[target, :] = block.astype(jnp.bfloat16)

        next_tiles(c)
        if index >= GOT_SLOTS:
            pl.semaphore_wait(credit, 1)
        over_core(c).start()

    def sum_core(c):
        over_core(c).wait()
        add_into(keep_of(c), 0, keep_of(c), 0, got_of(c), 0, chunks[c][2])
        if is_feed(c) and ringed.index(c) + GOT_SLOTS < len(ringed):
            pl.semaphore_signal(credit, inc=1, device_id=sibling, device_id_type=MESH)
        for h in range(2):
            over_first(c, h).start()

    def sum_first(c):
        unit = unit_of(c)
        for h in range(2):
            over_first(c, h).wait()
            row = (h * 2 + first_bit[h]) * 2 * unit
            add_into(keep_of(c), row, keep_of(c), row, first_in[c], h * 2 * unit, 2 * unit)
            over_second(c, h).start()

    def sum_second(c):
        unit = unit_of(c)
        for h in range(2):
            over_second(c, h).wait()
            row = ((h * 2 + first_bit[h]) * 2 + second_bit[h]) * unit
            add_into(pieces[c], h * unit, pieces[c], h * unit, keep_of(c), row, unit)

        @pl.when(is_end)
        def _():
            z_in(c).start()

    def sum_end(c):
        @pl.when(is_mid)
        def _():
            z_in(c).wait_recv()
            add_into(done[c], 0, pieces[c], 0, done[c], 0, 2 * unit_of(c))
            z_mid(c).start()

    def sum_middle(c):
        @pl.when(is_mid)
        def _():
            z_mid(c).wait()
            add_into(done[c], 0, done[c], 0, from_mid[c], 0, 2 * unit_of(c))
            z_out(c).start()

        @pl.when(is_end)
        def _():
            z_in(c).wait_send()
            z_out(c).wait_recv()

        for h in range(2):
            to_second(c, h).start()
            to_first(c, h).start()
            to_sibling(c, h, 0).start()
            own_copy(c, h).start()
        add_squares(c)

    def forward(c):
        for h in range(2):
            to_second(c, h).wait_recv()
            pass_first(c, h).start()
            to_sibling(c, h, 1).start()

    def last_hop(c):
        for h in range(2):
            to_first(c, h).wait_recv()
            to_sibling(c, h, 2).start()
            pass_first(c, h).wait_recv()
            to_sibling(c, h, 3).start()

    def drain(c):
        @pl.when(is_mid)
        def _():
            z_out(c).wait_send()

        for h in range(2):
            to_second(c, h).wait_send()
            to_first(c, h).wait_send()
            pass_first(c, h).wait_send()
            own_copy(c, h).wait()
            for kind in range(4):
                to_sibling(c, h, kind).wait()

    small_route = (sibling, over_x, over_y, z_near, z_far)

    def small_copy(k):
        return pltpu.make_async_remote_copy(
            src_ref=small_out,
            dst_ref=small_in.at[k],
            send_sem=small_send.at[k],
            recv_sem=small_recv.at[k],
            device_id=small_route[k],
            device_id_type=MESH,
        )

    def square_copy(k):
        return pltpu.make_async_remote_copy(
            src_ref=square_out,
            dst_ref=square_in.at[k],
            send_sem=square_send.at[k],
            recv_sem=square_recv.at[k],
            device_id=small_route[k],
            device_id_type=MESH,
        )

    width = n2t.shape[0]
    low, full = jnp.bfloat16, jnp.float32
    blocks = x.shape[0] // TILE_ROWS
    gain_one, gain_two = gains[0:1, :], gains[1:2, :]
    tile = lambda cols, k=0: pl.BlockSpec((TILE_ROWS, cols), lambda i: (i, k))
    turned = lambda cols, k=0: pl.BlockSpec((TILE_ROWS, cols), lambda i: (blocks - 1 - i, k))
    to_before = pltpu.make_async_remote_copy(
        src_ref=conv_grad.at[pl.ds(0, 8)],
        dst_ref=edge,
        send_sem=edge_send,
        recv_sem=edge_recv,
        device_id=(group, lax.rem(place + 3, 4), core),
        device_id_type=MESH,
    )

    def run_out_back():
        def scope(total, w_out_here):
            load = pltpu.make_async_copy(w_out, w_out_here, load_sem)
            load.start()
            total[...] = jnp.zeros_like(total)
            load.wait()

            def body(h_ref, c_ref, gc_ref, e_ref, back_ref, zt_ref, dh_ref, dgc_ref, dc_ref):
                values = h_ref[...]
                upstream = back_ref[...]
                scale = scale_of(values)
                inner = jnp.mean(values * gain_two * upstream, axis=-1, keepdims=True)
                grad = (
                    e_ref[...].astype(full)
                    + scale * gain_two * upstream
                    - values * (scale * scale * scale * inner)
                )
                dh_ref[...] = grad
                rounded = grad.astype(low)
                small_out[4:5, :] += jnp.sum(upstream * values * scale, axis=0, keepdims=True)
                mixer_grad = kernel_dot(rounded, w_out_here[...], BACK_DOT)
                dgc_ref[...] = (mixer_grad * c_ref[...]).astype(low)
                dc_ref[...] = mixer_grad * gc_ref[...]
                total[...] += kernel_dot(zt_ref[...], rounded)

            pltpu.emit_pipeline(
                body,
                grid=(blocks,),
                in_specs=[tile(width), tile(width), tile(width, 1), tile(width), tile(width)]
                + [pl.BlockSpec((width, TILE_ROWS), lambda i: (0, i))],
                out_specs=[tile(width)] * 3,
            )(hidden, convolved, proj, e, back, zt, hidden_grad, gc_grad, conv_grad)
            rows = width // 2
            for target, side in ((out_keep, core), (out_give, 1 - core)):
                target[...] = total[aligned(side * rows, rows), :].astype(low)

        pl.run_scoped(scope, pltpu.VMEM((width, width), full), pltpu.VMEM((width, width), low))

        @pl.when(place > 0)
        def _():
            to_before.start()

    def run_conv_back():
        @pl.when(place == 3)
        def _():
            edge[...] = jnp.zeros_like(edge)

        @pl.when(place < 3)
        def _():
            to_before.wait_recv()

        @pl.when(place > 0)
        def _():
            to_before.wait_send()

        def body(dc_ref, dgc_ref, gb_ref, v_ref, masks_ref, dp_ref):
            grad = dc_ref[...]
            beside = edge[...]
            next_one = masks_ref[:, 2:3] * shifted(grad, beside, 1)
            next_two = masks_ref[:, 3:4] * shifted(grad, beside, 2)
            edge[...] = grad[:8, :]
            gate_b, values = gb_ref[...], v_ref[...]
            mixed = gate_b * values
            for row, term in ((1, next_two), (2, next_one), (3, grad)):
                small_out[row : row + 1, :] += jnp.sum(term * mixed, axis=0, keepdims=True)
            mixed_grad = (
                gains[4:5, :] * grad + gains[3:4, :] * next_one + gains[2:3, :] * next_two
            )
            dp_ref[:, :width] = (mixed_grad * values).astype(low)
            dp_ref[:, width : 2 * width] = dgc_ref[...]
            dp_ref[:, 2 * width :] = (mixed_grad * gate_b).astype(low)

        pltpu.emit_pipeline(
            body,
            grid=(blocks,),
            in_specs=[
                turned(width),
                turned(width),
                turned(width),
                turned(width, 2),
                turned(masks.shape[1]),
            ],
            out_specs=[turned(3 * width)],
        )(conv_grad, gc_grad, proj, proj, masks, dp)

    def run_in_back():
        def scope(w_in_here):
            load = pltpu.make_async_copy(w_in, w_in_here, load_sem)
            load.start()
            load.wait()

            def body(dp_ref, x_ref, dh_ref, grad_ref):
                upstream = kernel_dot(dp_ref[...], w_in_here[...], BACK_DOT)
                values = x_ref[...].astype(full)
                scale = scale_of(values)
                inner = jnp.mean(values * gain_one * upstream, axis=-1, keepdims=True)
                grad_ref[...] = (
                    dh_ref[...]
                    + scale * gain_one * upstream
                    - values * (scale * scale * scale * inner)
                ).astype(low)
                small_out[0:1, :] += jnp.sum(upstream * values * scale, axis=0, keepdims=True)

            pltpu.emit_pipeline(
                body,
                grid=(blocks,),
                in_specs=[tile(3 * width), tile(width), tile(width)],
                out_specs=[tile(width)],
            )(dp, x, hidden_grad, input_grad)

        pl.run_scoped(scope, pltpu.VMEM(w_in.shape, low))

    def base_copy(n):
        return pltpu.make_async_remote_copy(
            src_ref=bases[n],
            dst_ref=bases_other[n],
            send_sem=base_send.at[n],
            recv_sem=base_recv.at[n],
            device_id=sibling,
            device_id_type=MESH,
        )

    def run_base(n):
        rows, cols = masters[n].shape
        step = 128 if cols <= 1024 else 32
        decay = 1.0 - rate[0] * WEIGHT_DECAY
        slope = rate[0] * MOMENTUM_BETA

        def body(master, moment, base):
            base[...] = (master[...] * decay - slope * moment[...]).astype(low)

        block = pl.BlockSpec((step, cols), lambda i: (i, 0))
        pltpu.emit_pipeline(
            body, grid=(rows // step,), in_specs=[block, block], out_specs=[block]
        )(masters[n], moments[n], bases[n])
        base_copy(n).start()

    work = {
        2: [run_out_back],
        3: [run_conv_back],
        4: [run_in_back],
        5: [functools.partial(run_base, 2)],
        6: [functools.partial(run_base, 3)],
        7: [functools.partial(run_base, 4)],
        8: [functools.partial(run_base, 0), functools.partial(run_base, 1)],
    }
    small_from, squares_from = 6, count + 3

    small_out[...] = jnp.zeros_like(small_out)
    square_out[...] = jnp.zeros_like(square_out)
    for half in range(2):
        load_tile(0, half).start()

    def at(step, action):
        if 0 <= step < count:
            action(step)

    for t in range(count + 7):
        at(t, produce)
        at(t - 4, forward)
        at(t, sum_core)
        if small_from <= t <= small_from + 5:
            k = t - small_from
            if k >= 1:
                small_copy(k - 1).wait()
                small_out[...] += small_in[k - 1]
            if k < 5:
                small_copy(k).start()
        at(t - 1, sum_first)
        at(t - 2, sum_second)
        at(t - 3, sum_middle)
        if squares_from <= t < squares_from + 4:
            k = t - squares_from
            if k >= 1:
                square_copy(k - 1).wait()
                square_out[...] += square_in[k - 1]
            if k < 3:
                square_copy(k).start()
        at(t - 5, last_hop)
        for item in work.get(t, ()):
            item()
        at(t - 2, sum_end)
    for c in range(count):
        drain(c)
    for n in range(5):
        base_copy(n).wait()


def finish(feed_ins, mixer_ins, masters, moments, parts):
    n2t, et, gate_back, up_back, act, back = feed_ins
    n1t, zt, hidden, convolved, proj, masks, gains, e, x, w_in, w_out, rate = mixer_ins
    rows, width = x.shape
    half = width // 2
    cols = gate_back.shape[1] // (2 * parts)
    in_cols = w_in.shape[1]
    chunks = []
    for part in range(parts):
        for kind in range(3):
            first = (part * 3 + kind) * 2 * width
            chunks.append(("feed", (part, kind), width, 2, first, width, 0, cols))
    chunks.append(("out", None, half, 0, 0, half, 0, width))
    in_parts = in_cols // (2 * cols)
    for part in range(in_parts):
        chunks.append(("feed", (part, 3), width, 1, part * 2 * width, width, 0, cols))
    count = len(chunks)
    low, full = jnp.bfloat16, jnp.float32
    shape = jax.ShapeDtypeStruct
    semaphore = pltpu.SemaphoreType.DMA
    wholes = [(width, width), (in_parts * 2 * width, cols), (parts * 3 * 2 * width, cols)]
    eighths = [(chunk[2] // 8, chunk[7]) for chunk in chunks]
    pair = [pltpu.VMEM((2 * r, c), low) for r, c in eighths]
    outs = pl.pallas_call(
        functools.partial(finish_kernel, tuple(chunks), parts, len(wholes)),
        out_shape=[shape(whole, low) for whole in wholes]
        + [
            shape((8, width), full),
            shape((8, 128), full),
            shape((rows, width), low),
            shape((rows, width), full),
            shape((rows, width), low),
            shape((rows, width), full),
            shape((rows, in_cols), low),
        ]
        + [shape(master.shape, low) for master in masters] * 2,
        in_specs=[INTO_VMEM] * 3
        + [ANY, INTO_VMEM, pl.BlockSpec(memory_space=pltpu.SMEM)]
        + [ANY] * (12 + 2 * len(masters)),
        out_specs=[ANY] * len(wholes) + [INTO_VMEM] * 2 + [ANY] * (5 + 2 * len(masters)),
        scratch_shapes=[pltpu.VMEM((half, width), low)] * 3
        + [
            pltpu.VMEM((KEEP_SLOTS, width, cols), low),
            pltpu.VMEM((GOT_SLOTS, width, cols), low),
            pltpu.VMEM((width, cols), low),
            pltpu.VMEM((2, rows, cols), low),
            pltpu.VMEM((8, width), full),
        ]
        + [pltpu.VMEM((4 * r, c), low) for r, c in eighths]
        + pair * 3
        + [
            pltpu.VMEM((5, 8, width), full),
            pltpu.VMEM((3, 8, 128), full),
            semaphore((count, 22)),
            semaphore((count, 22)),
            semaphore((5,)),
            semaphore((5,)),
            semaphore((3,)),
            semaphore((3,)),
            semaphore((count, 2)),
            semaphore,
            semaphore((2,)),
            semaphore((5,)),
            semaphore((5,)),
            semaphore,
            semaphore,
            pltpu.SemaphoreType.REGULAR,
        ],
        compiler_params=pltpu.CompilerParams(
            collective_id=0, has_side_effects=True, vmem_limit_bytes=62 * 1024 * 1024
        ),
    )(
        n2t,
        et,
        n1t,
        masks,
        gains,
        rate,
        gate_back,
        up_back,
        act,
        hidden,
        convolved,
        proj,
        e,
        back,
        zt,
        x,
        w_in,
        w_out,
        *masters,
        *moments,
    )
    return outs[:3], outs[3], outs[4], outs[5], outs[10:15], outs[15:20]


def feed_kernel(step, n2, e, hidden, wg, wu, wd, block_out, back, act, gate_back, up_back, et, out):
    @pl.when(pl.program_id(0) == 0)
    def _():
        et[...] = e[...].T
        out[...] = hidden[...]
        back[...] = jnp.zeros_like(back)

    @pl.loop(0, n2.shape[0] // step)
    def _(t):
        rows = pl.ds(pl.multiple_of(t * step, step), step)
        gate = kernel_dot(n2[rows, :], wg[...])
        up = kernel_dot(n2[rows, :], wu[...])
        grad = kernel_dot(e[rows, :], wd[...], BACK_DOT)
        sigmoid = 0.5 * jnp.tanh(0.5 * gate) + 0.5
        silu = gate * sigmoid
        low_act = (silu * up).astype(jnp.bfloat16)
        low_up = (grad * silu).astype(jnp.bfloat16)
        low_gate = (grad * up * (sigmoid + silu * (1.0 - sigmoid))).astype(jnp.bfloat16)
        act[rows, :] = low_act
        gate_back[rows, :] = low_gate
        up_back[rows, :] = low_up
        out[rows, :] += kernel_dot(low_act, wd[...])
        back[rows, :] += kernel_dot(low_gate, wg[...], BACK_DOT) + kernel_dot(
            low_up, wu[...], BACK_DOT
        )

    @pl.when(pl.program_id(0) == pl.num_programs(0) - 1)
    def _():
        block_out[...] = out[...].astype(jnp.bfloat16)


def feed(n2, e, hidden, gate_matrix, up_matrix, down_matrix, tiles):
    rows, width = n2.shape
    assert rows == width
    cols = gate_matrix.shape[1] // tiles
    whole = pl.BlockSpec((rows, width), lambda i: (0, 0), pipeline_mode=pl.Buffered(1))
    tile = pl.BlockSpec((rows, cols), lambda i: (0, i))
    return pl.pallas_call(
        functools.partial(feed_kernel, rows // 2),
        grid=(tiles,),
        in_specs=[whole, whole, whole]
        + [pl.BlockSpec((width, cols), lambda i: (0, i))] * 2
        + [pl.BlockSpec((cols, width), lambda i: (i, 0))],
        out_specs=[whole, whole, tile, tile, tile, whole],
        out_shape=[
            jax.ShapeDtypeStruct((rows, width), jnp.bfloat16),
            jax.ShapeDtypeStruct((rows, width), jnp.float32),
        ]
        + [jax.ShapeDtypeStruct((rows, tiles * cols), jnp.bfloat16)] * 3
        + [jax.ShapeDtypeStruct((width, rows), jnp.bfloat16)],
        scratch_shapes=[pltpu.VMEM((rows, width), jnp.float32)],
        cost_estimate=pl.CostEstimate(
            flops=12 * rows * width * cols * tiles,
            bytes_accessed=70 * 1024 * 1024,
            transcendentals=rows * cols * tiles,
        ),
        compiler_params=pltpu.CompilerParams(vmem_limit_bytes=56 * 1024 * 1024),
    )(n2, e, hidden, gate_matrix, up_matrix, down_matrix)


def scale_of(values):
    return lax.rsqrt(jnp.mean(values * values, axis=-1, keepdims=True) + EPSILON)


def shifted(values, edge, distance):
    rows = values.shape[0]
    moved = pltpu.roll(values, (-distance) % rows, 0)
    index = lax.broadcasted_iota(jnp.int32, values.shape, 0)
    if distance < 0:
        for row in range(-distance):
            moved = jnp.where(index == row, edge[8 + distance + row : 9 + distance + row, :], moved)
    else:
        for row in range(distance):
            moved = jnp.where(index == rows - distance + row, edge[row : row + 1, :], moved)
    return moved


STEPS = 4


def mixer_kernel(
    x_ref,
    x_all,
    masks,
    pack,
    in_master,
    out_master,
    gate_master,
    up_master,
    down_master,
    proj,
    conv,
    hid,
    n1t,
    zt,
    n2,
    n2t,
    gains,
    in_whole,
    out_whole,
    gate_whole,
    up_whole,
    down_whole,
    carry,
    edge,
    pack_in,
    w_in,
    w_out,
    in_stage,
    out_stage,
    gate_stage,
    up_stage,
    down_stage,
    gate_low,
    up_low,
    down_low,
    load_sem,
    send,
    recv,
    keep_sem,
    part_load,
    part_send,
    part_recv,
    part_keep,
):
    width = x_ref.shape[1]
    half = width // 2
    low = jnp.bfloat16
    step = pl.program_id(0)
    group = lax.axis_index("dp")
    place = lax.axis_index("seq")
    core = lax.axis_index("shard")
    places = lax.axis_size("seq")
    sibling = (group, place, 1 - core)
    after = (group, lax.rem(place + 1, places), core)
    before = (group, lax.rem(place + places - 1, places), core)

    def remote(source, target, k, device):
        return pltpu.make_async_remote_copy(
            src_ref=source,
            dst_ref=target,
            send_sem=send.at[k],
            recv_sem=recv.at[k],
            device_id=device,
            device_id_type=MESH,
        )

    def own_rows(rows, start=0, count=None):
        return pl.ds(pl.multiple_of(core * rows + start, 16), rows if count is None else count)

    def cast(target, target_row, source, source_row, rows):
        block = 16

        def body(i, carry_):
            put = pl.ds(pl.multiple_of(target_row + i * block, block), block)
            get = pl.ds(pl.multiple_of(source_row + i * block, block), block)
            target[put, :] = source[get, :].astype(low)
            return carry_

        lax.fori_loop(0, rows // block, body, 0)

    stages = (gate_stage, up_stage, down_stage)
    masters = (gate_master, up_master, down_master)
    wholes = (gate_whole, up_whole, down_whole)
    lows = (gate_low, up_low, down_low)

    def part_in(m, i):
        rows = stages[m].shape[0]
        return pltpu.make_async_copy(
            masters[m].at[pl.ds(pl.multiple_of(i * rows, 16), rows)], stages[m], part_load.at[m]
        )

    def part_rows(m, i):
        rows = stages[m].shape[0]
        return pl.ds(pl.multiple_of(core * (STEPS * rows) + i * rows, 16), rows)

    def part_out(m, i):
        slot = lax.rem(i, 2)
        return pltpu.make_async_remote_copy(
            src_ref=lows[m].at[slot],
            dst_ref=wholes[m].at[part_rows(m, i)],
            send_sem=part_send.at[i, m],
            recv_sem=part_recv.at[i, m],
            device_id=sibling,
            device_id_type=MESH,
        )

    def part_own(m, i):
        slot = lax.rem(i, 2)
        return pltpu.make_async_copy(
            lows[m].at[slot], wholes[m].at[part_rows(m, i)], part_keep.at[i, m]
        )

    quarter = half // 2
    copies = []
    for k in range(2):
        rows = own_rows(half, k * quarter, quarter)
        copies.append(remote(w_in.at[rows], w_in.at[rows], k, sibling))
    rows = own_rows(half)
    copies.append(remote(w_out.at[rows], w_out.at[rows], 2, sibling))
    copies.append(remote(pack, pack_in, 3, sibling))
    to_after = remote(x_all.at[pl.ds(x_all.shape[0] - 16, 16)], edge, 4, after)
    in_loads = [
        pltpu.make_async_copy(
            in_master.at[pl.ds(k * quarter, quarter)],
            in_stage.at[pl.ds(k * quarter, quarter)],
            load_sem.at[k],
        )
        for k in range(2)
    ]
    out_load = pltpu.make_async_copy(out_master, out_stage, load_sem.at[2])
    keeps = [
        pltpu.make_async_copy(w_in, in_whole, keep_sem.at[0]),
        pltpu.make_async_copy(w_out, out_whole, keep_sem.at[1]),
    ]

    def project(values, first, count=1):
        return kernel_dot(values, w_in[:, first * width : (first + count) * width])

    def normed(values):
        return (values * scale_of(values) * gains[0:1, :]).astype(low)

    @pl.when(step == 0)
    def _():
        for load in (*in_loads, out_load):
            load.start()
        for m in range(3):
            part_in(m, 0).start()
        barrier = pltpu.get_barrier_semaphore()
        for device in (sibling, after, before):
            pl.semaphore_signal(barrier, inc=1, device_id=device, device_id_type=MESH)
        pl.semaphore_wait(barrier, 3)
        copies[3].start()

        @pl.when(place < places - 1)
        def _():
            to_after.start()

        for k in range(2):
            in_loads[k].wait()
            cast(w_in, core * half + k * quarter, in_stage, k * quarter, quarter)
            copies[k].start()
        out_load.wait()
        cast(w_out, core * half, out_stage, 0, half)
        copies[2].start()

        @pl.when(place == 0)
        def _():
            edge[...] = jnp.zeros_like(edge)

        @pl.when(place > 0)
        def _():
            to_after.wait_recv()

        @pl.when(place < places - 1)
        def _():
            to_after.wait_send()

        for copy in copies:
            copy.wait()
        gains[:, pl.ds(pl.multiple_of(core * half, half), half)] = pack[...]
        gains[:, pl.ds(pl.multiple_of((1 - core) * half, half), half)] = pack_in[...]
        for copy in keeps:
            copy.start()
        rows = normed(edge[...].astype(jnp.float32))
        mixed = project(rows, 0) * project(rows, 2)
        carry[...] = mixed[8:, :]

    @pl.when(step > 0)
    def _():
        i = step - 1

        @pl.when(i >= 2)
        def _():
            for m in range(3):
                part_out(m, i - 2).wait_send()
                part_own(m, i - 2).wait()

        for m in range(3):
            part_in(m, i).wait()
            cast(lows[m].at[lax.rem(i, 2)], 0, stages[m], 0, stages[m].shape[0])
            part_out(m, i).start()
            part_own(m, i).start()

        @pl.when(i + 1 < STEPS)
        def _():
            for m in range(3):
                part_in(m, i + 1).start()

        x = x_ref[...].astype(jnp.float32)
        first = normed(x)
        n1t[...] = first.T
        gate_b, gate_c, values = project(first, 0), project(first, 1), project(first, 2)
        proj[:, :width] = gate_b
        proj[:, width : 2 * width] = gate_c
        proj[:, 2 * width :] = values
        mixed = gate_b * values
        beside = carry[...]
        convolved = (
            gains[4:5, :] * mixed
            + gains[3:4, :] * masks[:, 0:1] * shifted(mixed, beside, -1)
            + gains[2:3, :] * masks[:, 1:2] * shifted(mixed, beside, -2)
        )
        carry[...] = mixed[mixed.shape[0] - 8 :, :]
        conv[...] = convolved
        mixer_out = (gate_c * convolved).astype(low)
        zt[...] = mixer_out.T
        hidden = x + kernel_dot(mixer_out, w_out[...])
        hid[...] = hidden
        second = (hidden * scale_of(hidden) * gains[1:2, :]).astype(low)
        n2[...] = second
        n2t[...] = second.T

    @pl.when(step == STEPS)
    def _():
        for copy in keeps:
            copy.wait()
        for i in range(STEPS):
            for m in range(3):
                if i >= STEPS - 2:
                    part_out(m, i).wait_send()
                    part_own(m, i).wait()
                part_out(m, i).wait_recv()


def resident(shape):
    return pl.BlockSpec(shape, lambda i: (0,) * len(shape), pipeline_mode=pl.Buffered(1))


def mixer(x, masks, pack, masters):
    rows, width = x.shape
    step = rows // STEPS
    at = lambda i: jnp.maximum(i - 1, 0)
    tile = lambda cols: pl.BlockSpec((step, cols), lambda i: (at(i), 0))
    turned = pl.BlockSpec((width, step), lambda i: (0, at(i)))
    low, full = jnp.bfloat16, jnp.float32
    shape = jax.ShapeDtypeStruct
    in_master, out_master = masters[:2]
    large = masters[2:]
    whole = [shape((2 * m.shape[0], m.shape[1]), low) for m in masters]
    parts = [(m.shape[0] // STEPS, m.shape[1]) for m in large]
    semaphore = pltpu.SemaphoreType.DMA
    return pl.pallas_call(
        mixer_kernel,
        grid=(STEPS + 1,),
        in_specs=[tile(width), ANY, tile(masks.shape[1]), resident(pack.shape)] + [ANY] * 5,
        out_specs=[tile(3 * width), tile(width), tile(width), turned, turned, tile(width), turned]
        + [resident((8, width))]
        + [ANY] * 5,
        out_shape=[
            shape((rows, 3 * width), full),
            shape((rows, width), full),
            shape((rows, width), full),
            shape((width, rows), low),
            shape((width, rows), low),
            shape((rows, width), low),
            shape((width, rows), low),
            shape((8, width), full),
        ]
        + whole,
        scratch_shapes=[
            pltpu.VMEM((8, width), full),
            pltpu.VMEM((16, width), low),
            pltpu.VMEM(pack.shape, full),
            pltpu.VMEM(whole[0].shape, low),
            pltpu.VMEM(whole[1].shape, low),
            pltpu.VMEM(in_master.shape, full),
            pltpu.VMEM(out_master.shape, full),
        ]
        + [pltpu.VMEM(part, full) for part in parts]
        + [pltpu.VMEM((2, *part), low) for part in parts]
        + [
            semaphore((3,)),
            semaphore((5,)),
            semaphore((5,)),
            semaphore((2,)),
            semaphore((3,)),
            semaphore((STEPS, 3)),
            semaphore((STEPS, 3)),
            semaphore((STEPS, 3)),
        ],
        compiler_params=pltpu.CompilerParams(
            collective_id=1, has_side_effects=True, vmem_limit_bytes=60 * 1024 * 1024
        ),
    )(x, x, masks, pack, *masters)


def update_kernel(bits, scalars, *refs):
    core = bits[2]
    clip, scale = scalars[0], scalars[1]
    count = len(refs) // 7
    for n in range(count):
        own, other, base_own, base_other, moment = refs[5 * n : 5 * n + 5]
        weight, new_moment = refs[5 * count + 2 * n : 5 * count + 2 * n + 2]
        rows = own.shape[0]
        gradient = own[...].astype(jnp.float32)
        new_moment[...] = MOMENTUM_BETA * moment[...] + clip * gradient
        mine = pl.ds(pl.multiple_of(core * rows, rows), rows)
        theirs = pl.ds(pl.multiple_of((1 - core) * rows, rows), rows)
        weight[mine, :] = (base_own[...].astype(jnp.float32) - scale * gradient).astype(jnp.bfloat16)
        weight[theirs, :] = (
            base_other[...].astype(jnp.float32) - scale * other[...].astype(jnp.float32)
        ).astype(jnp.bfloat16)


def update_rows(bits, scalars, grid, block, matrices):
    width = block[1]
    in_specs, out_specs, out_shape, operands = [], [], [], []
    total = 0
    for gradient, source, column, base, base_other, moment in matrices:
        in_specs += [
            pl.BlockSpec(block, lambda *a, source=source: source(a[-1][2], *a[:-1])),
            pl.BlockSpec(block, lambda *a, source=source: source(1 - a[-1][2], *a[:-1])),
        ]
        in_specs += [pl.BlockSpec(block, lambda *a, column=column: (0, column(*a[:-1])))] * 3
        out_specs += [
            pl.BlockSpec((2 * block[0], width), lambda *a, column=column: (0, column(*a[:-1]))),
            pl.BlockSpec(block, lambda *a, column=column: (0, column(*a[:-1]))),
        ]
        rows, cols = moment.shape
        total += rows * cols
        out_shape += [
            jax.ShapeDtypeStruct((2 * rows, cols), jnp.bfloat16),
            jax.ShapeDtypeStruct((rows, cols), jnp.float32),
        ]
        operands += [gradient, gradient, base, base_other, moment]
    in_specs = [pl.BlockSpec(memory_space=pltpu.SMEM)] + in_specs
    return pl.pallas_call(
        update_kernel,
        grid_spec=pltpu.PrefetchScalarGridSpec(
            num_scalar_prefetch=1, grid=grid, in_specs=in_specs, out_specs=out_specs
        ),
        out_shape=out_shape,
        compiler_params=pltpu.CompilerParams(vmem_limit_bytes=48 * 1024 * 1024),
        cost_estimate=pl.CostEstimate(flops=8 * total, bytes_accessed=20 * total, transcendentals=0),
    )(bits, scalars, *operands)


def update_down_kernel(bits, scalars, own, other, base_own, base_other, moment, weight, new_moment):
    core = bits[2]
    clip, scale = scalars[0], scalars[1]
    gradient = own[...].astype(jnp.float32).T
    new_moment[...] = MOMENTUM_BETA * moment[...] + clip * gradient
    weight[core] = (base_own[...].astype(jnp.float32) - scale * gradient).astype(jnp.bfloat16)
    gradient = other[...].astype(jnp.float32).T
    weight[1 - core] = (base_other[...].astype(jnp.float32) - scale * gradient).astype(jnp.bfloat16)


def update_down(bits, scalars, gradient, parts, base, base_other, moment):
    rows, width = moment.shape
    cols = gradient.shape[1]
    subs = 2
    step = cols // subs
    row = pl.BlockSpec((step, width), lambda k, t, b: (k * subs + t, 0))
    weight, new_moment = pl.pallas_call(
        update_down_kernel,
        grid_spec=pltpu.PrefetchScalarGridSpec(
            num_scalar_prefetch=1,
            grid=(parts, subs),
            in_specs=[
                pl.BlockSpec(memory_space=pltpu.SMEM),
                pl.BlockSpec((width, step), lambda k, t, b: ((k * 3 + 2) * 2 + b[2], t)),
                pl.BlockSpec((width, step), lambda k, t, b: ((k * 3 + 2) * 2 + 1 - b[2], t)),
                row,
                row,
                row,
            ],
            out_specs=[pl.BlockSpec((2, step, width), lambda k, t, b: (0, k * subs + t, 0)), row],
        ),
        out_shape=[
            jax.ShapeDtypeStruct((2, rows, width), jnp.bfloat16),
            jax.ShapeDtypeStruct((rows, width), jnp.float32),
        ],
        compiler_params=pltpu.CompilerParams(vmem_limit_bytes=48 * 1024 * 1024),
        cost_estimate=pl.CostEstimate(
            flops=8 * rows * width, bytes_accessed=20 * rows * width, transcendentals=0
        ),
    )(bits, scalars, gradient, gradient, base, base_other, moment)
    return weight.reshape(2 * rows, width), new_moment


def local_fast(
    tokens,
    segments,
    cotangent,
    norm_one,
    in_weight,
    conv_weight,
    out_weight,
    norm_two,
    gate_weight,
    up_weight,
    down_weight,
    moment_norm_one,
    moment_in,
    moment_conv,
    moment_out,
    moment_norm_two,
    moment_gate,
    moment_up,
    moment_down,
    learn_rate,
    step_number,
):
    masters = (
        norm_one,
        in_weight,
        conv_weight,
        out_weight,
        norm_two,
        gate_weight,
        up_weight,
        down_weight,
    )
    moments = (
        moment_norm_one,
        moment_in,
        moment_conv,
        moment_out,
        moment_norm_two,
        moment_gate,
        moment_up,
        moment_down,
    )
    seq_count, span, model_width = tokens.shape
    row_count = seq_count * span
    x = tokens.reshape(row_count, model_width)
    e = cotangent.reshape(row_count, model_width)
    core = lax.axis_index("shard")
    group = lax.axis_index("dp")
    bits = jnp.stack([lax.rem(group, 2), lax.div(group, 2), core]).astype(jnp.int32)
    start = lax.axis_index("seq") * span
    padding = jnp.full((seq_count, 2), -1, jnp.int32)
    extended = jnp.concatenate([padding, segments, padding], 1)
    current = segment_window(extended, start, 0, span)
    masks = jnp.stack(
        [
            (segment_window(extended, start, offset, span) == current).reshape(row_count)
            for offset in (-1, -2, 1, 2)
        ],
        1,
    ).astype(jnp.float32)
    pack = jnp.concatenate(
        [norm_one[None], norm_two[None], conv_weight, jnp.zeros((3, norm_one.size))], 0
    )
    pack = pack.astype(jnp.bfloat16).astype(jnp.float32)
    (
        proj,
        convolved,
        hidden,
        n1t,
        zt,
        n2,
        n2t,
        gains,
        in_matrix,
        out_matrix,
        gate_matrix,
        up_matrix,
        down_matrix,
    ) = mixer(x, masks, pack, (in_weight, out_weight, gate_weight, up_weight, down_weight))
    block_out, back, act, gate_back, up_back, et = feed(
        n2, e, hidden, gate_matrix, up_matrix, down_matrix, 2 * FEED_PARTS
    )
    rate_now = learn_rate * jnp.minimum(1.0, (step_number + 1).astype(jnp.float32) / WARMUP)
    large = (1, 3, 5, 6, 7)
    wholes, small_sum, squares, input_grad, bases, bases_other = finish(
        (n2t, et, gate_back, up_back, act, back),
        (
            n1t,
            zt,
            hidden,
            convolved,
            proj,
            masks,
            gains,
            e,
            x,
            in_matrix,
            out_matrix,
            rate_now.reshape(1),
        ),
        [masters[place] for place in large],
        [moments[place] for place in large],
        FEED_PARTS,
    )
    base = dict(zip(large, bases))
    base_other = dict(zip(large, bases_other))
    cols = gate_matrix.shape[1] // (2 * FEED_PARTS)
    input_grad = input_grad.reshape(tokens.shape)
    block_out = block_out.reshape(tokens.shape)
    param_count = 2 * sum((member.size for member in masters))
    clip_level = CLIP_RATIO * math.sqrt(param_count)
    grad_norm = jnp.sqrt(jnp.sum(squares) + jnp.sum(small_sum * small_sum))
    clip_factor = clip_level / jnp.maximum(grad_norm, clip_level)
    scalars = jnp.stack([clip_factor, rate_now * clip_factor])
    half = model_width // 2
    narrow = cols // 2

    def feed_matrix(place, kind):
        return (
            wholes[2],
            lambda side, k, i, t: ((k * 3 + kind) * 4 + side * 2 + i, t),
            lambda k, i, t: (i * FEED_PARTS + k) * 2 + t,
            base[place],
            base_other[place],
            moments[place],
        )

    def plain_matrix(place, gradient):
        return (
            gradient,
            lambda side, t: (side, t),
            lambda t: t,
            base[place],
            base_other[place],
            moments[place],
        )

    new_weight, new_moment = {}, {}
    new_weight[3], new_moment[3] = update_rows(
        bits, scalars, (2,), (half, half), [plain_matrix(3, wholes[0])]
    )
    new_weight[5], new_moment[5], new_weight[6], new_moment[6] = update_rows(
        bits,
        scalars,
        (FEED_PARTS, 2, 2),
        (half, narrow),
        [feed_matrix(5, 0), feed_matrix(6, 1)],
    )
    new_weight[7], new_moment[7] = update_down(
        bits, scalars, wholes[2], FEED_PARTS, base[7], base_other[7], moments[7]
    )
    new_weight[1], new_moment[1] = update_rows(
        bits,
        scalars,
        (in_matrix.shape[1] // narrow // 4, 2, 2),
        (half, narrow),
        [
            (
                wholes[1],
                lambda side, k, i, t: (k * 4 + side * 2 + i, t),
                lambda k, i, t: (k * 2 + i) * 2 + t,
                base[1],
                base_other[1],
                moments[1],
            )
        ],
    )
    small_own = lax.dynamic_slice_in_dim(small_sum, core * half, half, 1)
    for place, gradient in ((0, small_own[0]), (2, small_own[1:4]), (4, small_own[4])):
        new_moment[place] = MOMENTUM_BETA * moments[place] + clip_factor * gradient
    return (
        (block_out, input_grad, grad_norm)
        + tuple(new_moment[place] for place in range(8))
        + tuple(new_weight[place] for place in (1, 3, 5, 6, 7))
    )


def local(
    tokens,
    segments,
    cotangent,
    norm_one,
    in_weight,
    conv_weight,
    out_weight,
    norm_two,
    gate_weight,
    up_weight,
    down_weight,
    moment_norm_one,
    moment_in,
    moment_conv,
    moment_out,
    moment_norm_two,
    moment_gate,
    moment_up,
    moment_down,
    learn_rate,
    step_number,
):
    masters = (
        norm_one,
        in_weight,
        conv_weight,
        out_weight,
        norm_two,
        gate_weight,
        up_weight,
        down_weight,
    )
    moments = (
        moment_norm_one,
        moment_in,
        moment_conv,
        moment_out,
        moment_norm_two,
        moment_gate,
        moment_up,
        moment_down,
    )
    whole = (
        lax.all_gather(norm_one.astype(jnp.bfloat16), "shard", axis=0, tiled=True),
        lax.all_gather(in_weight.astype(jnp.bfloat16), "shard", axis=0, tiled=True),
        lax.all_gather(conv_weight.astype(jnp.bfloat16), "shard", axis=1, tiled=True),
        lax.all_gather(out_weight.astype(jnp.bfloat16), "shard", axis=0, tiled=True),
        lax.all_gather(norm_two.astype(jnp.bfloat16), "shard", axis=0, tiled=True),
        lax.all_gather(gate_weight.astype(jnp.bfloat16), "shard", axis=0, tiled=True),
        lax.all_gather(up_weight.astype(jnp.bfloat16), "shard", axis=0, tiled=True),
        lax.all_gather(down_weight.astype(jnp.bfloat16), "shard", axis=0, tiled=True),
    )
    gain_one = whole[0].astype(jnp.float32)
    in_matrix = whole[1]
    conv_taps = whole[2].astype(jnp.float32)
    out_matrix = whole[3]
    gain_two = whole[4].astype(jnp.float32)
    gate_matrix = whole[5]
    up_matrix = whole[6]
    down_matrix = whole[7]
    seq_count, span, model_width = tokens.shape
    row_count = seq_count * span
    hidden_in = tokens.reshape(row_count, model_width).astype(jnp.float32)
    start = lax.axis_index("seq") * span
    padding = jnp.full((seq_count, 2), -1, jnp.int32)
    extended = jnp.concatenate([padding, segments, padding], 1)
    current = segment_window(extended, start, 0, span)
    keep_one = (
        (segment_window(extended, start, -1, span) == current)
        .astype(jnp.float32)
        .reshape(row_count, 1)
    )
    keep_two = (
        (segment_window(extended, start, -2, span) == current)
        .astype(jnp.float32)
        .reshape(row_count, 1)
    )
    next_one = (
        (segment_window(extended, start, 1, span) == current)
        .astype(jnp.float32)
        .reshape(row_count, 1)
    )
    next_two = (
        (segment_window(extended, start, 2, span) == current)
        .astype(jnp.float32)
        .reshape(row_count, 1)
    )
    normed_f, scale_one = norm_forward(hidden_in, gain_one)
    normed_one = normed_f.astype(jnp.bfloat16)
    projected = rows_dot(normed_one, in_matrix)
    gate_b = projected[:, :model_width]
    gate_c = projected[:, model_width : 2 * model_width]
    values = projected[:, 2 * model_width :]
    mixed_in = gate_b * values
    mixed_grid = mixed_in.reshape(seq_count, span, model_width)
    before_edge = from_behind(mixed_grid[:, span - 2 :, :], "seq", 1)
    before = jnp.concatenate([before_edge, mixed_grid], 1)
    before_one = before[:, 1:-1, :].reshape(row_count, model_width)
    before_two = before[:, :-2, :].reshape(row_count, model_width)
    convolved = (
        conv_taps[2] * mixed_in
        + conv_taps[1] * keep_one * before_one
        + conv_taps[0] * keep_two * before_two
    )
    mixer_out = (gate_c * convolved).astype(jnp.bfloat16)
    hidden = hidden_in + rows_dot(mixer_out, out_matrix)
    normed_g, scale_two = norm_forward(hidden, gain_two)
    normed_two = normed_g.astype(jnp.bfloat16)
    gate_pre = rows_dot(normed_two, gate_matrix)
    upward = rows_dot(normed_two, up_matrix)
    sigmoid_gate = jax.nn.sigmoid(gate_pre)
    activated = (gate_pre * sigmoid_gate * upward).astype(jnp.bfloat16)
    block_out = (
        (hidden + rows_dot(activated, down_matrix)).astype(jnp.bfloat16).reshape(tokens.shape)
    )
    cotangent_rows = cotangent.reshape(row_count, model_width)
    down_grad = outer_dot(activated, cotangent_rows)
    act_grad = back_dot(cotangent_rows, down_matrix)
    gate_back = (act_grad * upward * sigmoid_gate * (1.0 + gate_pre * (1.0 - sigmoid_gate))).astype(
        jnp.bfloat16
    )
    up_back = (act_grad * gate_pre * sigmoid_gate).astype(jnp.bfloat16)
    gate_grad = outer_dot(normed_two, gate_back)
    up_grad = outer_dot(normed_two, up_back)
    normed_two_grad = back_dot(gate_back, gate_matrix) + back_dot(up_back, up_matrix)
    hidden_part, gain_two_grad = norm_backward(hidden, scale_two, gain_two, normed_two_grad)
    hidden_grad = cotangent_rows.astype(jnp.float32) + hidden_part
    hidden_low = hidden_grad.astype(jnp.bfloat16)
    out_grad = outer_dot(mixer_out, hidden_low)
    mixer_grad = back_dot(hidden_low, out_matrix)
    gate_c_grad = mixer_grad * convolved
    conv_out_grad = mixer_grad * gate_c
    conv_grid = conv_out_grad.reshape(seq_count, span, model_width)
    after_edge = from_behind(conv_grid[:, :2, :], "seq", -1)
    after = jnp.concatenate([conv_grid, after_edge], 1)
    follow_one = after[:, 1:-1, :].reshape(row_count, model_width)
    follow_two = after[:, 2:, :].reshape(row_count, model_width)
    mixed_grad = (
        conv_taps[2] * conv_out_grad
        + conv_taps[1] * next_one * follow_one
        + conv_taps[0] * next_two * follow_two
    )
    conv_grad = jnp.stack(
        [
            jnp.sum(conv_out_grad * keep_two * before_two, axis=0),
            jnp.sum(conv_out_grad * keep_one * before_one, axis=0),
            jnp.sum(conv_out_grad * mixed_in, axis=0),
        ],
        0,
    )
    proj_back = jnp.concatenate([mixed_grad * values, gate_c_grad, mixed_grad * gate_b], 1).astype(
        jnp.bfloat16
    )
    in_grad = outer_dot(normed_one, proj_back)
    normed_one_grad = back_dot(proj_back, in_matrix)
    input_part, gain_one_grad = norm_backward(hidden_in, scale_one, gain_one, normed_one_grad)
    input_grad = (hidden_grad + input_part).astype(jnp.bfloat16).reshape(tokens.shape)
    shares = (
        lax.psum_scatter(gain_one_grad, "shard", scatter_dimension=0, tiled=True),
        lax.psum_scatter(in_grad, "shard", scatter_dimension=0, tiled=True),
        lax.psum_scatter(conv_grad, "shard", scatter_dimension=1, tiled=True),
        lax.psum_scatter(out_grad, "shard", scatter_dimension=0, tiled=True),
        lax.psum_scatter(gain_two_grad, "shard", scatter_dimension=0, tiled=True),
        lax.psum_scatter(gate_grad, "shard", scatter_dimension=0, tiled=True),
        lax.psum_scatter(up_grad, "shard", scatter_dimension=0, tiled=True),
        lax.psum_scatter(down_grad, "shard", scatter_dimension=0, tiled=True),
    )
    param_count = sum((member.size for member in whole))
    clip_level = CLIP_RATIO * math.sqrt(param_count)
    rate_now = learn_rate * jnp.minimum(1.0, (step_number + 1).astype(jnp.float32) / WARMUP)
    large_places = (1, 3, 5, 6, 7)
    summed = lax.psum(
        (shares[0], shares[1], shares[2], shares[3], shares[4], shares[5], shares[6], shares[7]),
        ("dp", "seq"),
    )
    squares_local = sum((jnp.sum(member * member) for member in summed))
    squares_sum = lax.psum(squares_local, "shard")
    grad_norm = jnp.sqrt(squares_sum)
    clip_factor = clip_level / jnp.maximum(grad_norm, clip_level)
    next_moments = new_moments(summed, moments, clip_factor)
    large_low = new_weights(
        tuple((masters[place] for place in large_places)),
        tuple((next_moments[place] for place in large_places)),
        rate_now,
    )
    weights = (
        lax.all_gather(large_low[0], "shard", axis=0, tiled=True),
        lax.all_gather(large_low[1], "shard", axis=0, tiled=True),
        lax.all_gather(large_low[2], "shard", axis=0, tiled=True),
        lax.all_gather(large_low[3], "shard", axis=0, tiled=True),
        lax.all_gather(large_low[4], "shard", axis=0, tiled=True),
    )
    return (
        block_out,
        input_grad,
        grad_norm,
        next_moments[0],
        next_moments[1],
        next_moments[2],
        next_moments[3],
        next_moments[4],
        next_moments[5],
        next_moments[6],
        next_moments[7],
        weights[0],
        weights[1],
        weights[2],
        weights[3],
        weights[4],
    )


def solution(mesh):
    placed = (
        P(("dp", "shard"), "seq", None),
        P(("dp", "shard"), None),
        P(("dp", "shard"), "seq", None),
        P("shard"),
        P("shard", None),
        P(None, "shard"),
        P("shard", None),
        P("shard"),
        P("shard", None),
        P("shard", None),
        P("shard", None),
        P("shard"),
        P("shard", None),
        P(None, "shard"),
        P("shard", None),
        P("shard"),
        P("shard", None),
        P("shard", None),
        P("shard", None),
        P(),
        P(),
    )
    sizes = (mesh.shape["dp"], mesh.shape["seq"], mesh.shape["shard"])
    return jax.shard_map(
        local_fast if sizes == (4, 4, 2) else local,
        mesh=mesh,
        in_specs=placed,
        out_specs=(
            P(("dp", "shard"), "seq", None),
            P(("dp", "shard"), "seq", None),
            P(),
            P("shard"),
            P("shard", None),
            P(None, "shard"),
            P("shard", None),
            P("shard"),
            P("shard", None),
            P("shard", None),
            P("shard", None),
            P(),
            P(),
            P(),
            P(),
            P(),
        ),
        check_vma=False,
    )
```

```python
import functools
import math

import jax
import jax.numpy as jnp
from jax import lax
from jax.experimental import pallas as pl
from jax.experimental.pallas import tpu as pltpu
from jax.sharding import PartitionSpec as P

WARMUP = 2000


EPSILON = 1e-05
MOMENTUM_BETA = 0.9
WEIGHT_DECAY = 0.1
CLIP_RATIO = 0.25

FEED_PARTS = 3


def from_behind(block, axis, distance):
    devices = range(lax.axis_size(axis))
    route = [(i - distance, i) for i in devices if i - distance in devices]
    return lax.ppermute(block, axis, route)


def rows_dot(left, right):
    return jnp.dot(left, right, preferred_element_type=jnp.float32)


def outer_dot(left, right):
    return lax.dot_general(
        left, right, (((0,), (0,)), ((), ())), preferred_element_type=jnp.float32
    )


def back_dot(left, right):
    return lax.dot_general(
        left, right, (((1,), (1,)), ((), ())), preferred_element_type=jnp.float32
    )


def norm_forward(values, gain):
    scale = lax.rsqrt(jnp.mean(values * values, axis=-1, keepdims=True) + EPSILON)
    return (values * scale * gain, scale)


def norm_backward(values, scale, gain, upstream):
    gain_grad = jnp.sum(upstream * values * scale, axis=0)
    inner = jnp.mean(values * gain * upstream, axis=-1, keepdims=True)
    return (scale * gain * upstream - values * scale * scale * scale * inner, gain_grad)


def segment_window(extended, start, offset, length):
    return lax.dynamic_slice_in_dim(extended, start + 2 + offset, length, 1)


def new_moments(gradients, moments, clip_factor):
    return tuple(
        (
            MOMENTUM_BETA * moment + clip_factor * gradient
            for moment, gradient in zip(moments, gradients)
        )
    )


def new_weights(masters, next_moments, rate_now):
    return tuple(
        (
            (master * (1.0 - rate_now * WEIGHT_DECAY) - rate_now * moment).astype(jnp.bfloat16)
            for master, moment in zip(masters, next_moments)
        )
    )


MESH = pl.DeviceIdType.MESH
ANY = pl.BlockSpec(memory_space=pl.ANY)
INTO_VMEM = pl.BlockSpec(memory_space=pltpu.VMEM)
ROWS_DOT = (((1,), (0,)), ((), ()))
BACK_DOT = (((1,), (1,)), ((), ()))
KEEP_SLOTS, GOT_SLOTS, TILE_ROWS = 3, 2, 128


def kernel_dot(left, right, dims=ROWS_DOT):
    return lax.dot_general(left, right, dims, preferred_element_type=jnp.float32)


def finish_kernel(chunks, parts, wholes_count, clip_level, *refs):
    count = len(chunks)
    (
        n2t,
        et,
        n1t,
        masks,
        gains,
        rate,
        gate_back,
        up_back,
        act,
        hidden,
        convolved,
        proj,
        e,
        back,
        zt,
        x,
        w_in,
        w_out,
    ) = refs[:18]
    masters, moments = refs[18:23], refs[23:28]
    refs = refs[28:]
    whole_refs = refs[:wholes_count]
    small_out, square_out, input_grad, hidden_grad, gc_grad, conv_grad, dp = refs[
        wholes_count : wholes_count + 7
    ]
    refs = refs[wholes_count + 7 :]
    bases, bases_other, scalars = refs[:5], refs[5:10], refs[10]
    rest = refs[11:]
    out_keep, out_give, out_got = rest[:3]
    keep_ring, got_ring, give_buffer, tiles, edge = rest[3:8]
    rest = rest[8:]
    first_in = rest[:count]
    pieces = rest[count : 2 * count]
    done = rest[2 * count : 3 * count]
    from_mid = rest[3 * count : 4 * count]
    small_in, square_in = rest[4 * count : 4 * count + 2]
    (
        send,
        recv,
        small_send,
        small_recv,
        square_send,
        square_recv,
        own_sem,
        load_sem,
        tile_sem,
        base_send,
        base_recv,
        edge_send,
        edge_recv,
        credit,
    ) = rest[4 * count + 2 :]

    group = lax.axis_index("dp")
    place = lax.axis_index("seq")
    core = lax.axis_index("shard")
    x_bit = lax.rem(group, 2)
    y_bit = lax.div(group, 2)
    over_x = (group + 1 - 2 * x_bit, place, core)
    over_y = (group + 2 - 4 * y_bit, place, core)
    sibling = (group, place, 1 - core)
    z_near = (group, place + 1 - 2 * lax.rem(place, 2), core)
    z_far = (group, 3 - place, core)
    is_mid = jnp.logical_or(place == 1, place == 2)
    is_end = jnp.logical_not(is_mid)
    first_dev, second_dev = (over_x, over_y), (over_y, over_x)
    first_bit, second_bit = (x_bit, y_bit), (y_bit, x_bit)

    barrier = pltpu.get_barrier_semaphore()
    for device in (over_x, over_y, sibling, z_near, z_far):
        pl.semaphore_signal(barrier, inc=1, device_id=device, device_id_type=MESH)
    pl.semaphore_wait(barrier, 5)

    def unit_of(c):
        return chunks[c][2] // 8

    ringed = [c for c in range(count) if chunks[c][0] == "feed"]

    def is_feed(c):
        return chunks[c][0] == "feed"

    def keep_of(c):
        return keep_ring.at[ringed.index(c) % KEEP_SLOTS] if is_feed(c) else out_keep

    def got_of(c):
        return got_ring.at[ringed.index(c) % GOT_SLOTS] if is_feed(c) else out_got

    def remote(source, target, c, k, device):
        return pltpu.make_async_remote_copy(
            src_ref=source,
            dst_ref=target,
            send_sem=send.at[c, k],
            recv_sem=recv.at[c, k],
            device_id=device,
            device_id_type=MESH,
        )

    def aligned(start, size):
        return pl.ds(pl.multiple_of(start, 16), size)

    def rows_of(c, h, first, second, owner):
        unit = unit_of(c)
        _, _, _, _, base, stride = chunks[c][:6]
        return aligned(base + owner * stride + ((h * 2 + first) * 2 + second) * unit, unit)

    def local_rows(c, h, first, second=None):
        unit = unit_of(c)
        if second is None:
            return aligned((h * 2 + first) * 2 * unit, 2 * unit)
        return aligned(((h * 2 + first) * 2 + second) * unit, unit)

    def whole_of(c):
        return whole_refs[chunks[c][3 + 0]]

    def mine(c, h):
        unit = unit_of(c)
        return done[c].at[pl.ds(h * unit, unit)]

    def add_into(target, target_row, one, one_row, two, two_row, rows):
        def body(i, carry):
            at = lambda start: aligned(start + i * 16, 16)
            target[at(target_row), :] = one[at(one_row), :] + two[at(two_row), :]
            return carry

        lax.fori_loop(0, rows // 16, body, 0)

    def add_squares(c):
        width = chunks[c][7]

        def body(i, total):
            block = done[c][aligned(i * 16, 16), :].astype(jnp.float32)
            block = block * block
            block = block[:8] + block[8:]
            for j in range(width // 128):
                total = total + block[:, j * 128 : (j + 1) * 128]
            return total

        square_out[...] += lax.fori_loop(
            0, 2 * unit_of(c) // 16, body, jnp.zeros((8, 128), jnp.float32)
        )

    def over_core(c):
        return remote(give_buffer if is_feed(c) else out_give, got_of(c), c, 0, sibling)

    def over_first(c, h):
        unit = unit_of(c)
        source = keep_of(c).at[local_rows(c, h, 1 - first_bit[h])]
        return remote(source, first_in[c].at[pl.ds(h * 2 * unit, 2 * unit)], c, 1 + h, first_dev[h])

    def over_second(c, h):
        unit = unit_of(c)
        source = keep_of(c).at[local_rows(c, h, first_bit[h], 1 - second_bit[h])]
        return remote(source, pieces[c].at[pl.ds(h * unit, unit)], c, 3 + h, second_dev[h])

    def z_in(c):
        return remote(pieces[c], done[c], c, 5, z_near)

    def z_mid(c):
        return remote(done[c], from_mid[c], c, 6, z_far)

    def z_out(c):
        return remote(done[c], done[c], c, 7, z_near)

    def to_second(c, h):
        rows = rows_of(c, h, first_bit[h], second_bit[h], core)
        return remote(mine(c, h), whole_of(c).at[rows], c, 8 + h, second_dev[h])

    def to_first(c, h):
        rows = rows_of(c, h, first_bit[h], second_bit[h], core)
        return remote(mine(c, h), whole_of(c).at[rows], c, 10 + h, first_dev[h])

    def pass_first(c, h):
        rows = rows_of(c, h, first_bit[h], 1 - second_bit[h], core)
        return remote(whole_of(c).at[rows], whole_of(c).at[rows], c, 12 + h, first_dev[h])

    def to_sibling(c, h, kind):
        first = first_bit[h] if kind < 2 else 1 - first_bit[h]
        second = second_bit[h] if kind % 2 == 0 else 1 - second_bit[h]
        rows = rows_of(c, h, first, second, core)
        source = mine(c, h) if kind == 0 else whole_of(c).at[rows]
        return remote(source, whole_of(c).at[rows], c, 14 + 2 * kind + h, sibling)

    def own_copy(c, h):
        rows = rows_of(c, h, first_bit[h], second_bit[h], core)
        return pltpu.make_async_copy(mine(c, h), whole_of(c).at[rows], own_sem.at[c, h])

    def load_tile(c, half):
        part, kind = chunks[c][1]
        cols = tiles.shape[2]
        place_of = 2 * part + half if kind == 3 else half * parts + part
        source = (gate_back, up_back, act, dp)[kind]
        return pltpu.make_async_copy(
            source.at[:, pl.ds(place_of * cols, cols)], tiles.at[half], tile_sem.at[half]
        )

    def next_tiles(c):
        if c + 1 < count and is_feed(c + 1):
            for half in range(2):
                load_tile(c + 1, half).start()

    def produce(c):
        if not is_feed(c):
            over_core(c).start()
            next_tiles(c)
            return
        index = ringed.index(c)
        kind = chunks[c][1][1]
        keep = keep_of(c)
        rows = n2t.shape[0] // 2
        for half in range(2):
            load_tile(c, half).wait()

        @pl.loop(0, 2)
        def _(r):
            target = aligned(r * rows, rows)
            for ref, side in ((keep, core), (give_buffer, 1 - core)):
                if kind == 2:
                    block = kernel_dot(et[target, :], tiles[side])
                else:
                    left = n1t if kind == 3 else n2t
                    block = kernel_dot(left[aligned(side * rows, rows), :], tiles[r])
                ref[target, :] = block.astype(jnp.bfloat16)

        next_tiles(c)
        if index >= GOT_SLOTS:
            pl.semaphore_wait(credit, 1)
        over_core(c).start()

    def sum_core(c):
        over_core(c).wait()
        add_into(keep_of(c), 0, keep_of(c), 0, got_of(c), 0, chunks[c][2])
        if is_feed(c) and ringed.index(c) + GOT_SLOTS < len(ringed):
            pl.semaphore_signal(credit, inc=1, device_id=sibling, device_id_type=MESH)
        for h in range(2):
            over_first(c, h).start()

    def sum_first(c):
        unit = unit_of(c)
        for h in range(2):
            over_first(c, h).wait()
            row = (h * 2 + first_bit[h]) * 2 * unit
            add_into(keep_of(c), row, keep_of(c), row, first_in[c], h * 2 * unit, 2 * unit)
            over_second(c, h).start()

    def sum_second(c):
        unit = unit_of(c)
        for h in range(2):
            over_second(c, h).wait()
            row = ((h * 2 + first_bit[h]) * 2 + second_bit[h]) * unit
            add_into(pieces[c], h * unit, pieces[c], h * unit, keep_of(c), row, unit)

        @pl.when(is_end)
        def _():
            z_in(c).start()

    def sum_end(c):
        @pl.when(is_mid)
        def _():
            z_in(c).wait_recv()
            add_into(done[c], 0, pieces[c], 0, done[c], 0, 2 * unit_of(c))
            z_mid(c).start()

    def sum_middle(c):
        @pl.when(is_mid)
        def _():
            z_mid(c).wait()
            add_into(done[c], 0, done[c], 0, from_mid[c], 0, 2 * unit_of(c))
            z_out(c).start()

        @pl.when(is_end)
        def _():
            z_in(c).wait_send()
            z_out(c).wait_recv()

        for h in range(2):
            to_second(c, h).start()
            to_first(c, h).start()
            to_sibling(c, h, 0).start()
            own_copy(c, h).start()
        add_squares(c)

    def forward(c):
        for h in range(2):
            to_second(c, h).wait_recv()
            pass_first(c, h).start()
            to_sibling(c, h, 1).start()

    def last_hop(c):
        for h in range(2):
            to_first(c, h).wait_recv()
            to_sibling(c, h, 2).start()
            pass_first(c, h).wait_recv()
            to_sibling(c, h, 3).start()

    def drain(c):
        @pl.when(is_mid)
        def _():
            z_out(c).wait_send()

        for h in range(2):
            to_second(c, h).wait_send()
            to_first(c, h).wait_send()
            pass_first(c, h).wait_send()
            own_copy(c, h).wait()
            for kind in range(4):
                to_sibling(c, h, kind).wait()

    small_route = (sibling, over_x, over_y, z_near, z_far)

    def small_copy(k):
        return pltpu.make_async_remote_copy(
            src_ref=small_out,
            dst_ref=small_in.at[k],
            send_sem=small_send.at[k],
            recv_sem=small_recv.at[k],
            device_id=small_route[k],
            device_id_type=MESH,
        )

    def square_copy(k):
        return pltpu.make_async_remote_copy(
            src_ref=square_out,
            dst_ref=square_in.at[k],
            send_sem=square_send.at[k],
            recv_sem=square_recv.at[k],
            device_id=small_route[k],
            device_id_type=MESH,
        )

    width = n2t.shape[0]
    low, full = jnp.bfloat16, jnp.float32
    blocks = x.shape[0] // TILE_ROWS
    gain_one, gain_two = gains[0:1, :], gains[1:2, :]
    tile = lambda cols, k=0: pl.BlockSpec((TILE_ROWS, cols), lambda i: (i, k))
    turned = lambda cols, k=0: pl.BlockSpec((TILE_ROWS, cols), lambda i: (blocks - 1 - i, k))
    to_before = pltpu.make_async_remote_copy(
        src_ref=conv_grad.at[pl.ds(0, 8)],
        dst_ref=edge,
        send_sem=edge_send,
        recv_sem=edge_recv,
        device_id=(group, lax.rem(place + 3, 4), core),
        device_id_type=MESH,
    )

    def run_out_back():
        def scope(total, w_out_here):
            load = pltpu.make_async_copy(w_out, w_out_here, load_sem)
            load.start()
            total[...] = jnp.zeros_like(total)
            load.wait()

            def body(h_ref, c_ref, gc_ref, e_ref, back_ref, zt_ref, dh_ref, dgc_ref, dc_ref):
                values = h_ref[...]
                upstream = back_ref[...]
                scale = scale_of(values)
                inner = jnp.mean(values * gain_two * upstream, axis=-1, keepdims=True)
                grad = (
                    e_ref[...].astype(full)
                    + scale * gain_two * upstream
                    - values * (scale * scale * scale * inner)
                )
                dh_ref[...] = grad
                rounded = grad.astype(low)
                small_out[4:5, :] += jnp.sum(upstream * values * scale, axis=0, keepdims=True)
                mixer_grad = kernel_dot(rounded, w_out_here[...], BACK_DOT)
                dgc_ref[...] = (mixer_grad * c_ref[...]).astype(low)
                dc_ref[...] = mixer_grad * gc_ref[...]
                total[...] += kernel_dot(zt_ref[...], rounded)

            pltpu.emit_pipeline(
                body,
                grid=(blocks,),
                in_specs=[tile(width), tile(width), tile(width, 1), tile(width), tile(width)]
                + [pl.BlockSpec((width, TILE_ROWS), lambda i: (0, i))],
                out_specs=[tile(width)] * 3,
            )(hidden, convolved, proj, e, back, zt, hidden_grad, gc_grad, conv_grad)
            rows = width // 2
            for target, side in ((out_keep, core), (out_give, 1 - core)):
                target[...] = total[aligned(side * rows, rows), :].astype(low)

        pl.run_scoped(scope, pltpu.VMEM((width, width), full), pltpu.VMEM((width, width), low))

        @pl.when(place > 0)
        def _():
            to_before.start()

    def run_conv_back():
        @pl.when(place == 3)
        def _():
            edge[...] = jnp.zeros_like(edge)

        @pl.when(place < 3)
        def _():
            to_before.wait_recv()

        @pl.when(place > 0)
        def _():
            to_before.wait_send()

        def body(dc_ref, dgc_ref, gb_ref, v_ref, masks_ref, dp_ref):
            grad = dc_ref[...]
            beside = edge[...]
            next_one = masks_ref[:, 2:3] * shifted(grad, beside, 1)
            next_two = masks_ref[:, 3:4] * shifted(grad, beside, 2)
            edge[...] = grad[:8, :]
            gate_b, values = gb_ref[...], v_ref[...]
            mixed = gate_b * values
            for row, term in ((1, next_two), (2, next_one), (3, grad)):
                small_out[row : row + 1, :] += jnp.sum(term * mixed, axis=0, keepdims=True)
            mixed_grad = (
                gains[4:5, :] * grad + gains[3:4, :] * next_one + gains[2:3, :] * next_two
            )
            dp_ref[:, :width] = (mixed_grad * values).astype(low)
            dp_ref[:, width : 2 * width] = dgc_ref[...]
            dp_ref[:, 2 * width :] = (mixed_grad * gate_b).astype(low)

        pltpu.emit_pipeline(
            body,
            grid=(blocks,),
            in_specs=[
                turned(width),
                turned(width),
                turned(width),
                turned(width, 2),
                turned(masks.shape[1]),
            ],
            out_specs=[turned(3 * width)],
        )(conv_grad, gc_grad, proj, proj, masks, dp)

    def run_in_back():
        def scope(w_in_here):
            load = pltpu.make_async_copy(w_in, w_in_here, load_sem)
            load.start()
            load.wait()

            def body(dp_ref, x_ref, dh_ref, grad_ref):
                upstream = kernel_dot(dp_ref[...], w_in_here[...], BACK_DOT)
                values = x_ref[...].astype(full)
                scale = scale_of(values)
                inner = jnp.mean(values * gain_one * upstream, axis=-1, keepdims=True)
                grad_ref[...] = (
                    dh_ref[...]
                    + scale * gain_one * upstream
                    - values * (scale * scale * scale * inner)
                ).astype(low)
                small_out[0:1, :] += jnp.sum(upstream * values * scale, axis=0, keepdims=True)

            pltpu.emit_pipeline(
                body,
                grid=(blocks,),
                in_specs=[tile(3 * width), tile(width), tile(width)],
                out_specs=[tile(width)],
            )(dp, x, hidden_grad, input_grad)

        pl.run_scoped(scope, pltpu.VMEM(w_in.shape, low))

    def base_copy(n):
        return pltpu.make_async_remote_copy(
            src_ref=bases[n],
            dst_ref=bases_other[n],
            send_sem=base_send.at[n],
            recv_sem=base_recv.at[n],
            device_id=sibling,
            device_id_type=MESH,
        )

    def run_base(n):
        rows, cols = masters[n].shape
        step = 128 if cols <= 1024 else 32
        decay = 1.0 - rate[0] * WEIGHT_DECAY
        slope = rate[0] * MOMENTUM_BETA

        def body(master, moment, base):
            base[...] = (master[...] * decay - slope * moment[...]).astype(low)

        block = pl.BlockSpec((step, cols), lambda i: (i, 0))
        pltpu.emit_pipeline(
            body, grid=(rows // step,), in_specs=[block, block], out_specs=[block]
        )(masters[n], moments[n], bases[n])
        base_copy(n).start()

    work = {
        2: [run_out_back],
        3: [run_conv_back],
        4: [run_in_back],
        5: [functools.partial(run_base, 2)],
        6: [functools.partial(run_base, 3)],
        7: [functools.partial(run_base, 4)],
        8: [functools.partial(run_base, 0), functools.partial(run_base, 1)],
    }
    small_from, squares_from = 6, count + 3

    small_out[...] = jnp.zeros_like(small_out)
    square_out[...] = jnp.zeros_like(square_out)
    for half in range(2):
        load_tile(0, half).start()

    def at(step, action):
        if 0 <= step < count:
            action(step)

    for t in range(count + 7):
        at(t, produce)
        at(t - 4, forward)
        at(t, sum_core)
        if small_from <= t <= small_from + 5:
            k = t - small_from
            if k >= 1:
                small_copy(k - 1).wait()
                small_out[...] += small_in[k - 1]
            if k < 5:
                small_copy(k).start()
        at(t - 1, sum_first)
        at(t - 2, sum_second)
        at(t - 3, sum_middle)
        if squares_from <= t < squares_from + 4:
            k = t - squares_from
            if k >= 1:
                square_copy(k - 1).wait()
                square_out[...] += square_in[k - 1]
            if k < 3:
                square_copy(k).start()
        at(t - 5, last_hop)
        for item in work.get(t, ()):
            item()
        at(t - 2, sum_end)
    grads = small_out[...]
    total = jnp.sum(square_out[...], keepdims=True) + jnp.sum(grads * grads, keepdims=True)
    norm = jnp.sqrt(total)
    clip = clip_level / jnp.maximum(norm, clip_level)
    scalars[...] = jnp.zeros_like(scalars)
    for row, value in enumerate((clip, rate[0] * clip, norm)):
        scalars[row : row + 1, :] = jnp.broadcast_to(value, (1, 128))
    for c in range(count):
        drain(c)
    for n in range(5):
        base_copy(n).wait()


def finish(feed_ins, mixer_ins, masters, moments, clip_level, parts):
    n2t, et, gate_back, up_back, act, back = feed_ins
    n1t, zt, hidden, convolved, proj, masks, gains, e, x, w_in, w_out, rate = mixer_ins
    rows, width = x.shape
    half = width // 2
    cols = gate_back.shape[1] // (2 * parts)
    in_cols = w_in.shape[1]
    chunks = []
    for part in range(parts):
        for kind in range(3):
            first = (part * 3 + kind) * 2 * width
            chunks.append(("feed", (part, kind), width, 2, first, width, 0, cols))
    chunks.append(("out", None, half, 0, 0, half, 0, width))
    in_parts = in_cols // (2 * cols)
    for part in range(in_parts):
        chunks.append(("feed", (part, 3), width, 1, part * 2 * width, width, 0, cols))
    count = len(chunks)
    low, full = jnp.bfloat16, jnp.float32
    shape = jax.ShapeDtypeStruct
    semaphore = pltpu.SemaphoreType.DMA
    wholes = [(width, width), (in_parts * 2 * width, cols), (parts * 3 * 2 * width, cols)]
    eighths = [(chunk[2] // 8, chunk[7]) for chunk in chunks]
    pair = [pltpu.VMEM((2 * r, c), low) for r, c in eighths]
    outs = pl.pallas_call(
        functools.partial(finish_kernel, tuple(chunks), parts, len(wholes), clip_level),
        out_shape=[shape(whole, low) for whole in wholes]
        + [
            shape((8, width), full),
            shape((8, 128), full),
            shape((rows, width), low),
            shape((rows, width), full),
            shape((rows, width), low),
            shape((rows, width), full),
            shape((rows, in_cols), low),
        ]
        + [shape(master.shape, low) for master in masters] * 2
        + [shape((8, 128), full)],
        in_specs=[INTO_VMEM] * 3
        + [ANY, INTO_VMEM, pl.BlockSpec(memory_space=pltpu.SMEM)]
        + [ANY] * (12 + 2 * len(masters)),
        out_specs=[ANY] * len(wholes)
        + [INTO_VMEM] * 2
        + [ANY] * (5 + 2 * len(masters))
        + [INTO_VMEM],
        scratch_shapes=[pltpu.VMEM((half, width), low)] * 3
        + [
            pltpu.VMEM((KEEP_SLOTS, width, cols), low),
            pltpu.VMEM((GOT_SLOTS, width, cols), low),
            pltpu.VMEM((width, cols), low),
            pltpu.VMEM((2, rows, cols), low),
            pltpu.VMEM((8, width), full),
        ]
        + [pltpu.VMEM((4 * r, c), low) for r, c in eighths]
        + pair * 3
        + [
            pltpu.VMEM((5, 8, width), full),
            pltpu.VMEM((3, 8, 128), full),
            semaphore((count, 22)),
            semaphore((count, 22)),
            semaphore((5,)),
            semaphore((5,)),
            semaphore((3,)),
            semaphore((3,)),
            semaphore((count, 2)),
            semaphore,
            semaphore((2,)),
            semaphore((5,)),
            semaphore((5,)),
            semaphore,
            semaphore,
            pltpu.SemaphoreType.REGULAR,
        ],
        compiler_params=pltpu.CompilerParams(
            collective_id=0, has_side_effects=True, vmem_limit_bytes=62 * 1024 * 1024
        ),
    )(
        n2t,
        et,
        n1t,
        masks,
        gains,
        rate,
        gate_back,
        up_back,
        act,
        hidden,
        convolved,
        proj,
        e,
        back,
        zt,
        x,
        w_in,
        w_out,
        *masters,
        *moments,
    )
    return outs[:3], outs[3], outs[5], outs[10:15], outs[15:20], outs[20]


def feed_kernel(step, n2, e, hidden, wg, wu, wd, block_out, back, act, gate_back, up_back, et, out):
    @pl.when(pl.program_id(0) == 0)
    def _():
        et[...] = e[...].T
        out[...] = hidden[...]
        back[...] = jnp.zeros_like(back)

    @pl.loop(0, n2.shape[0] // step)
    def _(t):
        rows = pl.ds(pl.multiple_of(t * step, step), step)
        gate = kernel_dot(n2[rows, :], wg[...])
        up = kernel_dot(n2[rows, :], wu[...])
        grad = kernel_dot(e[rows, :], wd[...], BACK_DOT)
        sigmoid = 0.5 * jnp.tanh(0.5 * gate) + 0.5
        silu = gate * sigmoid
        low_act = (silu * up).astype(jnp.bfloat16)
        low_up = (grad * silu).astype(jnp.bfloat16)
        low_gate = (grad * up * (sigmoid + silu * (1.0 - sigmoid))).astype(jnp.bfloat16)
        act[rows, :] = low_act
        gate_back[rows, :] = low_gate
        up_back[rows, :] = low_up
        out[rows, :] += kernel_dot(low_act, wd[...])
        back[rows, :] += kernel_dot(low_gate, wg[...], BACK_DOT) + kernel_dot(
            low_up, wu[...], BACK_DOT
        )

    @pl.when(pl.program_id(0) == pl.num_programs(0) - 1)
    def _():
        block_out[...] = out[...].astype(jnp.bfloat16)


def feed(n2, e, hidden, gate_matrix, up_matrix, down_matrix, tiles):
    rows, width = n2.shape
    assert rows == width
    cols = gate_matrix.shape[1] // tiles
    whole = pl.BlockSpec((rows, width), lambda i: (0, 0), pipeline_mode=pl.Buffered(1))
    tile = pl.BlockSpec((rows, cols), lambda i: (0, i))
    return pl.pallas_call(
        functools.partial(feed_kernel, rows // 2),
        grid=(tiles,),
        in_specs=[whole, whole, whole]
        + [pl.BlockSpec((width, cols), lambda i: (0, i))] * 2
        + [pl.BlockSpec((cols, width), lambda i: (i, 0))],
        out_specs=[whole, whole, tile, tile, tile, whole],
        out_shape=[
            jax.ShapeDtypeStruct((rows, width), jnp.bfloat16),
            jax.ShapeDtypeStruct((rows, width), jnp.float32),
        ]
        + [jax.ShapeDtypeStruct((rows, tiles * cols), jnp.bfloat16)] * 3
        + [jax.ShapeDtypeStruct((width, rows), jnp.bfloat16)],
        scratch_shapes=[pltpu.VMEM((rows, width), jnp.float32)],
        cost_estimate=pl.CostEstimate(
            flops=12 * rows * width * cols * tiles,
            bytes_accessed=70 * 1024 * 1024,
            transcendentals=rows * cols * tiles,
        ),
        compiler_params=pltpu.CompilerParams(vmem_limit_bytes=56 * 1024 * 1024),
    )(n2, e, hidden, gate_matrix, up_matrix, down_matrix)


def scale_of(values):
    return lax.rsqrt(jnp.mean(values * values, axis=-1, keepdims=True) + EPSILON)


def shifted(values, edge, distance):
    rows = values.shape[0]
    moved = pltpu.roll(values, (-distance) % rows, 0)
    index = lax.broadcasted_iota(jnp.int32, values.shape, 0)
    if distance < 0:
        for row in range(-distance):
            moved = jnp.where(index == row, edge[8 + distance + row : 9 + distance + row, :], moved)
    else:
        for row in range(distance):
            moved = jnp.where(index == rows - distance + row, edge[row : row + 1, :], moved)
    return moved


STEPS = 4


def mixer_kernel(
    x_ref,
    x_all,
    masks,
    pack,
    in_master,
    out_master,
    gate_master,
    up_master,
    down_master,
    proj,
    conv,
    hid,
    n1t,
    zt,
    n2,
    n2t,
    gains,
    in_whole,
    out_whole,
    gate_whole,
    up_whole,
    down_whole,
    carry,
    edge,
    pack_in,
    w_in,
    w_out,
    in_stage,
    out_stage,
    gate_stage,
    up_stage,
    down_stage,
    gate_low,
    up_low,
    down_low,
    load_sem,
    send,
    recv,
    keep_sem,
    part_load,
    part_send,
    part_recv,
    part_keep,
):
    width = x_ref.shape[1]
    half = width // 2
    low = jnp.bfloat16
    step = pl.program_id(0)
    group = lax.axis_index("dp")
    place = lax.axis_index("seq")
    core = lax.axis_index("shard")
    places = lax.axis_size("seq")
    sibling = (group, place, 1 - core)
    after = (group, lax.rem(place + 1, places), core)
    before = (group, lax.rem(place + places - 1, places), core)

    def remote(source, target, k, device):
        return pltpu.make_async_remote_copy(
            src_ref=source,
            dst_ref=target,
            send_sem=send.at[k],
            recv_sem=recv.at[k],
            device_id=device,
            device_id_type=MESH,
        )

    def own_rows(rows, start=0, count=None):
        return pl.ds(pl.multiple_of(core * rows + start, 16), rows if count is None else count)

    def cast(target, target_row, source, source_row, rows):
        block = 16

        def body(i, carry_):
            put = pl.ds(pl.multiple_of(target_row + i * block, block), block)
            get = pl.ds(pl.multiple_of(source_row + i * block, block), block)
            target[put, :] = source[get, :].astype(low)
            return carry_

        lax.fori_loop(0, rows // block, body, 0)

    stages = (gate_stage, up_stage, down_stage)
    masters = (gate_master, up_master, down_master)
    wholes = (gate_whole, up_whole, down_whole)
    lows = (gate_low, up_low, down_low)

    def part_in(m, i):
        rows = stages[m].shape[0]
        return pltpu.make_async_copy(
            masters[m].at[pl.ds(pl.multiple_of(i * rows, 16), rows)], stages[m], part_load.at[m]
        )

    def part_rows(m, i):
        rows = stages[m].shape[0]
        return pl.ds(pl.multiple_of(core * (STEPS * rows) + i * rows, 16), rows)

    def part_out(m, i):
        slot = lax.rem(i, 2)
        return pltpu.make_async_remote_copy(
            src_ref=lows[m].at[slot],
            dst_ref=wholes[m].at[part_rows(m, i)],
            send_sem=part_send.at[i, m],
            recv_sem=part_recv.at[i, m],
            device_id=sibling,
            device_id_type=MESH,
        )

    def part_own(m, i):
        slot = lax.rem(i, 2)
        return pltpu.make_async_copy(
            lows[m].at[slot], wholes[m].at[part_rows(m, i)], part_keep.at[i, m]
        )

    quarter = half // 2
    copies = []
    for k in range(2):
        rows = own_rows(half, k * quarter, quarter)
        copies.append(remote(w_in.at[rows], w_in.at[rows], k, sibling))
    rows = own_rows(half)
    copies.append(remote(w_out.at[rows], w_out.at[rows], 2, sibling))
    copies.append(remote(pack, pack_in, 3, sibling))
    to_after = remote(x_all.at[pl.ds(x_all.shape[0] - 16, 16)], edge, 4, after)
    in_loads = [
        pltpu.make_async_copy(
            in_master.at[pl.ds(k * quarter, quarter)],
            in_stage.at[pl.ds(k * quarter, quarter)],
            load_sem.at[k],
        )
        for k in range(2)
    ]
    out_load = pltpu.make_async_copy(out_master, out_stage, load_sem.at[2])
    keeps = [
        pltpu.make_async_copy(w_in, in_whole, keep_sem.at[0]),
        pltpu.make_async_copy(w_out, out_whole, keep_sem.at[1]),
    ]

    def project(values, first, count=1):
        return kernel_dot(values, w_in[:, first * width : (first + count) * width])

    def normed(values):
        return (values * scale_of(values) * gains[0:1, :]).astype(low)

    @pl.when(step == 0)
    def _():
        for load in (*in_loads, out_load):
            load.start()
        for m in range(3):
            part_in(m, 0).start()
        barrier = pltpu.get_barrier_semaphore()
        for device in (sibling, after, before):
            pl.semaphore_signal(barrier, inc=1, device_id=device, device_id_type=MESH)
        pl.semaphore_wait(barrier, 3)
        copies[3].start()

        @pl.when(place < places - 1)
        def _():
            to_after.start()

        for k in range(2):
            in_loads[k].wait()
            cast(w_in, core * half + k * quarter, in_stage, k * quarter, quarter)
            copies[k].start()
        out_load.wait()
        cast(w_out, core * half, out_stage, 0, half)
        copies[2].start()

        @pl.when(place == 0)
        def _():
            edge[...] = jnp.zeros_like(edge)

        @pl.when(place > 0)
        def _():
            to_after.wait_recv()

        @pl.when(place < places - 1)
        def _():
            to_after.wait_send()

        for copy in copies:
            copy.wait()
        gains[:, pl.ds(pl.multiple_of(core * half, half), half)] = pack[...]
        gains[:, pl.ds(pl.multiple_of((1 - core) * half, half), half)] = pack_in[...]
        for copy in keeps:
            copy.start()
        rows = normed(edge[...].astype(jnp.float32))
        mixed = project(rows, 0) * project(rows, 2)
        carry[...] = mixed[8:, :]

    @pl.when(step > 0)
    def _():
        i = step - 1

        @pl.when(i >= 2)
        def _():
            for m in range(3):
                part_out(m, i - 2).wait_send()
                part_own(m, i - 2).wait()

        for m in range(3):
            part_in(m, i).wait()
            cast(lows[m].at[lax.rem(i, 2)], 0, stages[m], 0, stages[m].shape[0])
            part_out(m, i).start()
            part_own(m, i).start()

        @pl.when(i + 1 < STEPS)
        def _():
            for m in range(3):
                part_in(m, i + 1).start()

        x = x_ref[...].astype(jnp.float32)
        first = normed(x)
        n1t[...] = first.T
        gate_b, gate_c, values = project(first, 0), project(first, 1), project(first, 2)
        proj[:, :width] = gate_b
        proj[:, width : 2 * width] = gate_c
        proj[:, 2 * width :] = values
        mixed = gate_b * values
        beside = carry[...]
        convolved = (
            gains[4:5, :] * mixed
            + gains[3:4, :] * masks[:, 0:1] * shifted(mixed, beside, -1)
            + gains[2:3, :] * masks[:, 1:2] * shifted(mixed, beside, -2)
        )
        carry[...] = mixed[mixed.shape[0] - 8 :, :]
        conv[...] = convolved
        mixer_out = (gate_c * convolved).astype(low)
        zt[...] = mixer_out.T
        hidden = x + kernel_dot(mixer_out, w_out[...])
        hid[...] = hidden
        second = (hidden * scale_of(hidden) * gains[1:2, :]).astype(low)
        n2[...] = second
        n2t[...] = second.T

    @pl.when(step == STEPS)
    def _():
        for copy in keeps:
            copy.wait()
        for i in range(STEPS):
            for m in range(3):
                if i >= STEPS - 2:
                    part_out(m, i).wait_send()
                    part_own(m, i).wait()
                part_out(m, i).wait_recv()


def resident(shape):
    return pl.BlockSpec(shape, lambda i: (0,) * len(shape), pipeline_mode=pl.Buffered(1))


def mixer(x, masks, pack, masters):
    rows, width = x.shape
    step = rows // STEPS
    at = lambda i: jnp.maximum(i - 1, 0)
    tile = lambda cols: pl.BlockSpec((step, cols), lambda i: (at(i), 0))
    turned = pl.BlockSpec((width, step), lambda i: (0, at(i)))
    low, full = jnp.bfloat16, jnp.float32
    shape = jax.ShapeDtypeStruct
    in_master, out_master = masters[:2]
    large = masters[2:]
    whole = [shape((2 * m.shape[0], m.shape[1]), low) for m in masters]
    parts = [(m.shape[0] // STEPS, m.shape[1]) for m in large]
    semaphore = pltpu.SemaphoreType.DMA
    return pl.pallas_call(
        mixer_kernel,
        grid=(STEPS + 1,),
        in_specs=[tile(width), ANY, tile(masks.shape[1]), resident(pack.shape)] + [ANY] * 5,
        out_specs=[tile(3 * width), tile(width), tile(width), turned, turned, tile(width), turned]
        + [resident((8, width))]
        + [ANY] * 5,
        out_shape=[
            shape((rows, 3 * width), full),
            shape((rows, width), full),
            shape((rows, width), full),
            shape((width, rows), low),
            shape((width, rows), low),
            shape((rows, width), low),
            shape((width, rows), low),
            shape((8, width), full),
        ]
        + whole,
        scratch_shapes=[
            pltpu.VMEM((8, width), full),
            pltpu.VMEM((16, width), low),
            pltpu.VMEM(pack.shape, full),
            pltpu.VMEM(whole[0].shape, low),
            pltpu.VMEM(whole[1].shape, low),
            pltpu.VMEM(in_master.shape, full),
            pltpu.VMEM(out_master.shape, full),
        ]
        + [pltpu.VMEM(part, full) for part in parts]
        + [pltpu.VMEM((2, *part), low) for part in parts]
        + [
            semaphore((3,)),
            semaphore((5,)),
            semaphore((5,)),
            semaphore((2,)),
            semaphore((3,)),
            semaphore((STEPS, 3)),
            semaphore((STEPS, 3)),
            semaphore((STEPS, 3)),
        ],
        compiler_params=pltpu.CompilerParams(
            collective_id=1, has_side_effects=True, vmem_limit_bytes=60 * 1024 * 1024
        ),
    )(x, x, masks, pack, *masters)


def update_kernel(bits, scalars, *refs):
    core = bits[2]
    clip, scale = scalars[0:1, 0:1], scalars[1:2, 0:1]
    count = len(refs) // 7
    for n in range(count):
        own, other, base_own, base_other, moment = refs[5 * n : 5 * n + 5]
        weight, new_moment = refs[5 * count + 2 * n : 5 * count + 2 * n + 2]
        rows = own.shape[0]
        gradient = own[...].astype(jnp.float32)
        new_moment[...] = MOMENTUM_BETA * moment[...] + clip * gradient
        mine = pl.ds(pl.multiple_of(core * rows, rows), rows)
        theirs = pl.ds(pl.multiple_of((1 - core) * rows, rows), rows)
        weight[mine, :] = (base_own[...].astype(jnp.float32) - scale * gradient).astype(jnp.bfloat16)
        weight[theirs, :] = (
            base_other[...].astype(jnp.float32) - scale * other[...].astype(jnp.float32)
        ).astype(jnp.bfloat16)


def update_rows(bits, scalars, grid, block, matrices):
    width = block[1]
    in_specs, out_specs, out_shape, operands = [], [], [], []
    total = 0
    for gradient, source, column, base, base_other, moment in matrices:
        in_specs += [
            pl.BlockSpec(block, lambda *a, source=source: source(a[-1][2], *a[:-1])),
            pl.BlockSpec(block, lambda *a, source=source: source(1 - a[-1][2], *a[:-1])),
        ]
        in_specs += [pl.BlockSpec(block, lambda *a, column=column: (0, column(*a[:-1])))] * 3
        out_specs += [
            pl.BlockSpec((2 * block[0], width), lambda *a, column=column: (0, column(*a[:-1]))),
            pl.BlockSpec(block, lambda *a, column=column: (0, column(*a[:-1]))),
        ]
        rows, cols = moment.shape
        total += rows * cols
        out_shape += [
            jax.ShapeDtypeStruct((2 * rows, cols), jnp.bfloat16),
            jax.ShapeDtypeStruct((rows, cols), jnp.float32),
        ]
        operands += [gradient, gradient, base, base_other, moment]
    in_specs = [INTO_VMEM] + in_specs
    return pl.pallas_call(
        update_kernel,
        grid_spec=pltpu.PrefetchScalarGridSpec(
            num_scalar_prefetch=1, grid=grid, in_specs=in_specs, out_specs=out_specs
        ),
        out_shape=out_shape,
        compiler_params=pltpu.CompilerParams(vmem_limit_bytes=48 * 1024 * 1024),
        cost_estimate=pl.CostEstimate(flops=8 * total, bytes_accessed=20 * total, transcendentals=0),
    )(bits, scalars, *operands)


def update_down_kernel(bits, scalars, own, other, base_own, base_other, moment, weight, new_moment):
    core = bits[2]
    clip, scale = scalars[0:1, 0:1], scalars[1:2, 0:1]
    gradient = own[...].astype(jnp.float32).T
    new_moment[...] = MOMENTUM_BETA * moment[...] + clip * gradient
    weight[core] = (base_own[...].astype(jnp.float32) - scale * gradient).astype(jnp.bfloat16)
    gradient = other[...].astype(jnp.float32).T
    weight[1 - core] = (base_other[...].astype(jnp.float32) - scale * gradient).astype(jnp.bfloat16)


def update_down(bits, scalars, gradient, parts, base, base_other, moment):
    rows, width = moment.shape
    cols = gradient.shape[1]
    subs = 2
    step = cols // subs
    row = pl.BlockSpec((step, width), lambda k, t, b: (k * subs + t, 0))
    weight, new_moment = pl.pallas_call(
        update_down_kernel,
        grid_spec=pltpu.PrefetchScalarGridSpec(
            num_scalar_prefetch=1,
            grid=(parts, subs),
            in_specs=[
                INTO_VMEM,
                pl.BlockSpec((width, step), lambda k, t, b: ((k * 3 + 2) * 2 + b[2], t)),
                pl.BlockSpec((width, step), lambda k, t, b: ((k * 3 + 2) * 2 + 1 - b[2], t)),
                row,
                row,
                row,
            ],
            out_specs=[pl.BlockSpec((2, step, width), lambda k, t, b: (0, k * subs + t, 0)), row],
        ),
        out_shape=[
            jax.ShapeDtypeStruct((2, rows, width), jnp.bfloat16),
            jax.ShapeDtypeStruct((rows, width), jnp.float32),
        ],
        compiler_params=pltpu.CompilerParams(vmem_limit_bytes=48 * 1024 * 1024),
        cost_estimate=pl.CostEstimate(
            flops=8 * rows * width, bytes_accessed=20 * rows * width, transcendentals=0
        ),
    )(bits, scalars, gradient, gradient, base, base_other, moment)
    return weight.reshape(2 * rows, width), new_moment


def local_fast(
    tokens,
    segments,
    cotangent,
    norm_one,
    in_weight,
    conv_weight,
    out_weight,
    norm_two,
    gate_weight,
    up_weight,
    down_weight,
    moment_norm_one,
    moment_in,
    moment_conv,
    moment_out,
    moment_norm_two,
    moment_gate,
    moment_up,
    moment_down,
    learn_rate,
    step_number,
):
    masters = (
        norm_one,
        in_weight,
        conv_weight,
        out_weight,
        norm_two,
        gate_weight,
        up_weight,
        down_weight,
    )
    moments = (
        moment_norm_one,
        moment_in,
        moment_conv,
        moment_out,
        moment_norm_two,
        moment_gate,
        moment_up,
        moment_down,
    )
    seq_count, span, model_width = tokens.shape
    row_count = seq_count * span
    x = tokens.reshape(row_count, model_width)
    e = cotangent.reshape(row_count, model_width)
    core = lax.axis_index("shard")
    group = lax.axis_index("dp")
    bits = jnp.stack([lax.rem(group, 2), lax.div(group, 2), core]).astype(jnp.int32)
    start = lax.axis_index("seq") * span
    padding = jnp.full((seq_count, 2), -1, jnp.int32)
    extended = jnp.concatenate([padding, segments, padding], 1)
    current = segment_window(extended, start, 0, span)
    masks = jnp.stack(
        [
            (segment_window(extended, start, offset, span) == current).reshape(row_count)
            for offset in (-1, -2, 1, 2)
        ],
        1,
    ).astype(jnp.float32)
    pack = jnp.concatenate(
        [norm_one[None], norm_two[None], conv_weight, jnp.zeros((3, norm_one.size))], 0
    )
    pack = pack.astype(jnp.bfloat16).astype(jnp.float32)
    (
        proj,
        convolved,
        hidden,
        n1t,
        zt,
        n2,
        n2t,
        gains,
        in_matrix,
        out_matrix,
        gate_matrix,
        up_matrix,
        down_matrix,
    ) = mixer(x, masks, pack, (in_weight, out_weight, gate_weight, up_weight, down_weight))
    block_out, back, act, gate_back, up_back, et = feed(
        n2, e, hidden, gate_matrix, up_matrix, down_matrix, 2 * FEED_PARTS
    )
    rate_now = learn_rate * jnp.minimum(1.0, (step_number + 1).astype(jnp.float32) / WARMUP)
    large = (1, 3, 5, 6, 7)
    param_count = 2 * sum((member.size for member in masters))
    clip_level = CLIP_RATIO * math.sqrt(param_count)
    wholes, small_sum, input_grad, bases, bases_other, scalars = finish(
        (n2t, et, gate_back, up_back, act, back),
        (
            n1t,
            zt,
            hidden,
            convolved,
            proj,
            masks,
            gains,
            e,
            x,
            in_matrix,
            out_matrix,
            rate_now.reshape(1),
        ),
        [masters[place] for place in large],
        [moments[place] for place in large],
        clip_level,
        FEED_PARTS,
    )
    base = dict(zip(large, bases))
    base_other = dict(zip(large, bases_other))
    cols = gate_matrix.shape[1] // (2 * FEED_PARTS)
    input_grad = input_grad.reshape(tokens.shape)
    block_out = block_out.reshape(tokens.shape)
    clip_factor, grad_norm = scalars[0, 0], scalars[2, 0]
    half = model_width // 2
    narrow = cols // 2

    def feed_matrix(place, kind):
        return (
            wholes[2],
            lambda side, k, i, t: ((k * 3 + kind) * 4 + side * 2 + i, t),
            lambda k, i, t: (i * FEED_PARTS + k) * 2 + t,
            base[place],
            base_other[place],
            moments[place],
        )

    def plain_matrix(place, gradient):
        return (
            gradient,
            lambda side, t: (side, t),
            lambda t: t,
            base[place],
            base_other[place],
            moments[place],
        )

    new_weight, new_moment = {}, {}
    new_weight[3], new_moment[3] = update_rows(
        bits, scalars, (2,), (half, half), [plain_matrix(3, wholes[0])]
    )
    new_weight[5], new_moment[5], new_weight[6], new_moment[6] = update_rows(
        bits,
        scalars,
        (FEED_PARTS, 2, 2),
        (half, narrow),
        [feed_matrix(5, 0), feed_matrix(6, 1)],
    )
    new_weight[7], new_moment[7] = update_down(
        bits, scalars, wholes[2], FEED_PARTS, base[7], base_other[7], moments[7]
    )
    new_weight[1], new_moment[1] = update_rows(
        bits,
        scalars,
        (in_matrix.shape[1] // narrow // 4, 2, 2),
        (half, narrow),
        [
            (
                wholes[1],
                lambda side, k, i, t: (k * 4 + side * 2 + i, t),
                lambda k, i, t: (k * 2 + i) * 2 + t,
                base[1],
                base_other[1],
                moments[1],
            )
        ],
    )
    small_own = lax.dynamic_slice_in_dim(small_sum, core * half, half, 1)
    for place, gradient in ((0, small_own[0]), (2, small_own[1:4]), (4, small_own[4])):
        new_moment[place] = MOMENTUM_BETA * moments[place] + clip_factor * gradient
    return (
        (block_out, input_grad, grad_norm)
        + tuple(new_moment[place] for place in range(8))
        + tuple(new_weight[place] for place in (1, 3, 5, 6, 7))
    )


def local(
    tokens,
    segments,
    cotangent,
    norm_one,
    in_weight,
    conv_weight,
    out_weight,
    norm_two,
    gate_weight,
    up_weight,
    down_weight,
    moment_norm_one,
    moment_in,
    moment_conv,
    moment_out,
    moment_norm_two,
    moment_gate,
    moment_up,
    moment_down,
    learn_rate,
    step_number,
):
    masters = (
        norm_one,
        in_weight,
        conv_weight,
        out_weight,
        norm_two,
        gate_weight,
        up_weight,
        down_weight,
    )
    moments = (
        moment_norm_one,
        moment_in,
        moment_conv,
        moment_out,
        moment_norm_two,
        moment_gate,
        moment_up,
        moment_down,
    )
    whole = (
        lax.all_gather(norm_one.astype(jnp.bfloat16), "shard", axis=0, tiled=True),
        lax.all_gather(in_weight.astype(jnp.bfloat16), "shard", axis=0, tiled=True),
        lax.all_gather(conv_weight.astype(jnp.bfloat16), "shard", axis=1, tiled=True),
        lax.all_gather(out_weight.astype(jnp.bfloat16), "shard", axis=0, tiled=True),
        lax.all_gather(norm_two.astype(jnp.bfloat16), "shard", axis=0, tiled=True),
        lax.all_gather(gate_weight.astype(jnp.bfloat16), "shard", axis=0, tiled=True),
        lax.all_gather(up_weight.astype(jnp.bfloat16), "shard", axis=0, tiled=True),
        lax.all_gather(down_weight.astype(jnp.bfloat16), "shard", axis=0, tiled=True),
    )
    gain_one = whole[0].astype(jnp.float32)
    in_matrix = whole[1]
    conv_taps = whole[2].astype(jnp.float32)
    out_matrix = whole[3]
    gain_two = whole[4].astype(jnp.float32)
    gate_matrix = whole[5]
    up_matrix = whole[6]
    down_matrix = whole[7]
    seq_count, span, model_width = tokens.shape
    row_count = seq_count * span
    hidden_in = tokens.reshape(row_count, model_width).astype(jnp.float32)
    start = lax.axis_index("seq") * span
    padding = jnp.full((seq_count, 2), -1, jnp.int32)
    extended = jnp.concatenate([padding, segments, padding], 1)
    current = segment_window(extended, start, 0, span)
    keep_one = (
        (segment_window(extended, start, -1, span) == current)
        .astype(jnp.float32)
        .reshape(row_count, 1)
    )
    keep_two = (
        (segment_window(extended, start, -2, span) == current)
        .astype(jnp.float32)
        .reshape(row_count, 1)
    )
    next_one = (
        (segment_window(extended, start, 1, span) == current)
        .astype(jnp.float32)
        .reshape(row_count, 1)
    )
    next_two = (
        (segment_window(extended, start, 2, span) == current)
        .astype(jnp.float32)
        .reshape(row_count, 1)
    )
    normed_f, scale_one = norm_forward(hidden_in, gain_one)
    normed_one = normed_f.astype(jnp.bfloat16)
    projected = rows_dot(normed_one, in_matrix)
    gate_b = projected[:, :model_width]
    gate_c = projected[:, model_width : 2 * model_width]
    values = projected[:, 2 * model_width :]
    mixed_in = gate_b * values
    mixed_grid = mixed_in.reshape(seq_count, span, model_width)
    before_edge = from_behind(mixed_grid[:, span - 2 :, :], "seq", 1)
    before = jnp.concatenate([before_edge, mixed_grid], 1)
    before_one = before[:, 1:-1, :].reshape(row_count, model_width)
    before_two = before[:, :-2, :].reshape(row_count, model_width)
    convolved = (
        conv_taps[2] * mixed_in
        + conv_taps[1] * keep_one * before_one
        + conv_taps[0] * keep_two * before_two
    )
    mixer_out = (gate_c * convolved).astype(jnp.bfloat16)
    hidden = hidden_in + rows_dot(mixer_out, out_matrix)
    normed_g, scale_two = norm_forward(hidden, gain_two)
    normed_two = normed_g.astype(jnp.bfloat16)
    gate_pre = rows_dot(normed_two, gate_matrix)
    upward = rows_dot(normed_two, up_matrix)
    sigmoid_gate = jax.nn.sigmoid(gate_pre)
    activated = (gate_pre * sigmoid_gate * upward).astype(jnp.bfloat16)
    block_out = (
        (hidden + rows_dot(activated, down_matrix)).astype(jnp.bfloat16).reshape(tokens.shape)
    )
    cotangent_rows = cotangent.reshape(row_count, model_width)
    down_grad = outer_dot(activated, cotangent_rows)
    act_grad = back_dot(cotangent_rows, down_matrix)
    gate_back = (act_grad * upward * sigmoid_gate * (1.0 + gate_pre * (1.0 - sigmoid_gate))).astype(
        jnp.bfloat16
    )
    up_back = (act_grad * gate_pre * sigmoid_gate).astype(jnp.bfloat16)
    gate_grad = outer_dot(normed_two, gate_back)
    up_grad = outer_dot(normed_two, up_back)
    normed_two_grad = back_dot(gate_back, gate_matrix) + back_dot(up_back, up_matrix)
    hidden_part, gain_two_grad = norm_backward(hidden, scale_two, gain_two, normed_two_grad)
    hidden_grad = cotangent_rows.astype(jnp.float32) + hidden_part
    hidden_low = hidden_grad.astype(jnp.bfloat16)
    out_grad = outer_dot(mixer_out, hidden_low)
    mixer_grad = back_dot(hidden_low, out_matrix)
    gate_c_grad = mixer_grad * convolved
    conv_out_grad = mixer_grad * gate_c
    conv_grid = conv_out_grad.reshape(seq_count, span, model_width)
    after_edge = from_behind(conv_grid[:, :2, :], "seq", -1)
    after = jnp.concatenate([conv_grid, after_edge], 1)
    follow_one = after[:, 1:-1, :].reshape(row_count, model_width)
    follow_two = after[:, 2:, :].reshape(row_count, model_width)
    mixed_grad = (
        conv_taps[2] * conv_out_grad
        + conv_taps[1] * next_one * follow_one
        + conv_taps[0] * next_two * follow_two
    )
    conv_grad = jnp.stack(
        [
            jnp.sum(conv_out_grad * keep_two * before_two, axis=0),
            jnp.sum(conv_out_grad * keep_one * before_one, axis=0),
            jnp.sum(conv_out_grad * mixed_in, axis=0),
        ],
        0,
    )
    proj_back = jnp.concatenate([mixed_grad * values, gate_c_grad, mixed_grad * gate_b], 1).astype(
        jnp.bfloat16
    )
    in_grad = outer_dot(normed_one, proj_back)
    normed_one_grad = back_dot(proj_back, in_matrix)
    input_part, gain_one_grad = norm_backward(hidden_in, scale_one, gain_one, normed_one_grad)
    input_grad = (hidden_grad + input_part).astype(jnp.bfloat16).reshape(tokens.shape)
    shares = (
        lax.psum_scatter(gain_one_grad, "shard", scatter_dimension=0, tiled=True),
        lax.psum_scatter(in_grad, "shard", scatter_dimension=0, tiled=True),
        lax.psum_scatter(conv_grad, "shard", scatter_dimension=1, tiled=True),
        lax.psum_scatter(out_grad, "shard", scatter_dimension=0, tiled=True),
        lax.psum_scatter(gain_two_grad, "shard", scatter_dimension=0, tiled=True),
        lax.psum_scatter(gate_grad, "shard", scatter_dimension=0, tiled=True),
        lax.psum_scatter(up_grad, "shard", scatter_dimension=0, tiled=True),
        lax.psum_scatter(down_grad, "shard", scatter_dimension=0, tiled=True),
    )
    param_count = sum((member.size for member in whole))
    clip_level = CLIP_RATIO * math.sqrt(param_count)
    rate_now = learn_rate * jnp.minimum(1.0, (step_number + 1).astype(jnp.float32) / WARMUP)
    large_places = (1, 3, 5, 6, 7)
    summed = lax.psum(
        (shares[0], shares[1], shares[2], shares[3], shares[4], shares[5], shares[6], shares[7]),
        ("dp", "seq"),
    )
    squares_local = sum((jnp.sum(member * member) for member in summed))
    squares_sum = lax.psum(squares_local, "shard")
    grad_norm = jnp.sqrt(squares_sum)
    clip_factor = clip_level / jnp.maximum(grad_norm, clip_level)
    next_moments = new_moments(summed, moments, clip_factor)
    large_low = new_weights(
        tuple((masters[place] for place in large_places)),
        tuple((next_moments[place] for place in large_places)),
        rate_now,
    )
    weights = (
        lax.all_gather(large_low[0], "shard", axis=0, tiled=True),
        lax.all_gather(large_low[1], "shard", axis=0, tiled=True),
        lax.all_gather(large_low[2], "shard", axis=0, tiled=True),
        lax.all_gather(large_low[3], "shard", axis=0, tiled=True),
        lax.all_gather(large_low[4], "shard", axis=0, tiled=True),
    )
    return (
        block_out,
        input_grad,
        grad_norm,
        next_moments[0],
        next_moments[1],
        next_moments[2],
        next_moments[3],
        next_moments[4],
        next_moments[5],
        next_moments[6],
        next_moments[7],
        weights[0],
        weights[1],
        weights[2],
        weights[3],
        weights[4],
    )


def solution(mesh):
    placed = (
        P(("dp", "shard"), "seq", None),
        P(("dp", "shard"), None),
        P(("dp", "shard"), "seq", None),
        P("shard"),
        P("shard", None),
        P(None, "shard"),
        P("shard", None),
        P("shard"),
        P("shard", None),
        P("shard", None),
        P("shard", None),
        P("shard"),
        P("shard", None),
        P(None, "shard"),
        P("shard", None),
        P("shard"),
        P("shard", None),
        P("shard", None),
        P("shard", None),
        P(),
        P(),
    )
    sizes = (mesh.shape["dp"], mesh.shape["seq"], mesh.shape["shard"])
    return jax.shard_map(
        local_fast if sizes == (4, 4, 2) else local,
        mesh=mesh,
        in_specs=placed,
        out_specs=(
            P(("dp", "shard"), "seq", None),
            P(("dp", "shard"), "seq", None),
            P(),
            P("shard"),
            P("shard", None),
            P(None, "shard"),
            P("shard", None),
            P("shard"),
            P("shard", None),
            P("shard", None),
            P("shard", None),
            P(),
            P(),
            P(),
            P(),
            P(),
        ),
        check_vma=False,
    )
```
